32 devices in a mesh: ctx: 16 (over z, y, x), fsdp: 2 (over core).
Axes of the slice: x: 2, y: 2, z: 4, core: 2. Of those that a mesh axis runs over, the one named last changes fastest.
Arguments:
- tokens: bfloat16 [2, 2048, 1024], P('fsdp', 'ctx'), may hold values from -6 to 6
- in_weight: bfloat16 [1024, 3072], P('fsdp'), may hold values from -0.1875 to 0.1875
- query_bias: bfloat16 [1024], P('fsdp'), may hold values from -3 to 3
- value_bias: bfloat16 [1024], P('fsdp'), may hold values from -0.23925781 to 0.23925781
- out_weight: bfloat16 [1024, 1024], P('fsdp'), may hold values from -2 to 2
- out_bias: bfloat16 [1024], P('fsdp'), may hold values from -1.1953125 to 1.1953125
- up_weight: bfloat16 [1024, 4096], P('fsdp'), may hold values from -0.1875 to 0.1875
- up_bias: bfloat16 [4096], P('fsdp'), may hold values from -1.796875 to 1.796875
- down_weight: bfloat16 [4096, 1024], P('fsdp'), may hold values from -0.125 to 0.125
- down_bias: bfloat16 [1024], P('fsdp'), may hold values from -2.390625 to 2.390625
- first_gain: bfloat16 [1024], P('fsdp'), may hold values from 0.5 to 1.5
- first_shift: bfloat16 [1024], P('fsdp'), may hold values from -1.1953125 to 1.1953125
- second_gain: bfloat16 [1024], P('fsdp'), may hold values from 0.5 to 1.5
- second_shift: bfloat16 [1024], P('fsdp'), may hold values from -1.1953125 to 1.1953125
- lengths: int32 [2, 2], P('fsdp'), may hold values from 1 to 1536, 2048 in all within a row
- slot_places: int32 [2, 2048], P('fsdp'), may hold values from 0 to 2047, each once within a row
- cotangent: bfloat16 [2, 2048, 1024], P('fsdp', 'ctx'), may hold values from -6 to 6
Outputs:
- layer_out: bfloat16 [2, 2048, 1024], P('fsdp', 'ctx')
- input_grad: bfloat16 [2, 2048, 1024], P('fsdp', 'ctx')
- in_weight_grad: float32 [1024, 3072], P(('ctx', 'fsdp'))
- query_bias_grad: float32 [1024], P(('ctx', 'fsdp'))
- value_bias_grad: float32 [1024], P(('ctx', 'fsdp'))
- out_weight_grad: float32 [1024, 1024], P(('ctx', 'fsdp'))
- out_bias_grad: float32 [1024], P(('ctx', 'fsdp'))
- up_weight_grad: float32 [1024, 4096], P(('ctx', 'fsdp'))
- up_bias_grad: float32 [4096], P(('ctx', 'fsdp'))
- down_weight_grad: float32 [4096, 1024], P(('ctx', 'fsdp'))
- down_bias_grad: float32 [1024], P(('ctx', 'fsdp'))
- first_gain_grad: float32 [1024], P(('ctx', 'fsdp'))
- first_shift_grad: float32 [1024], P(('ctx', 'fsdp'))
- second_gain_grad: float32 [1024], P(('ctx', 'fsdp'))
- second_shift_grad: float32 [1024], P(('ctx', 'fsdp'))
The draws below stay inside these ranges and needn't reach their ends.
Inputs may be any that keep to these rules, and one draw needn't show every extreme that they name: In each batch 2 sequence lengths that sum to 2048; none is longer than 1536. `slot_places`: in each batch a permutation of the 2048 places: the place, in the batch's packed order, of the token held in each slot.
All inputs are finite; a program needn't handle non-finite values.
Results may differ from the reference program's by a relative error of at most 0.014.
Values may be sent and summed in bfloat16 or wider, within the bound.
A program may use at most 448 MiB of HBM per device.

```python
import math
from functools import partial
import jax
import jax.numpy as jnp
import numpy as np
from jax import lax

D = 1024
H = 16
HD = 64
FF = 4096
TOK_DEV = 128
BATCHES = 2
TOKENS = 2048
NSEQ = 2
LMAX = 1536
N_FSDP = 2


def block_scale(rng, shape, pieces, smallest, largest):
    def one(axis_at, blocks):
        steps = jax.random.uniform(jax.random.fold_in(jax.random.fold_in(rng, 6), axis_at), (blocks,), jnp.float32, smallest / len(pieces), largest / len(pieces))
        return jnp.repeat(jnp.exp(steps), shape[axis_at] // blocks).reshape((-1,) + (1,) * (len(shape) - axis_at - 1))

    factor_of = one(*pieces[0])
    for cut in pieces[1:]:
        factor_of = factor_of * one(*cut)
    return factor_of


def split_up(count, total, most, skew):
    weights = [(1 << 20) // math.isqrt(standing ** skew) + 1 for standing in range(2, count + 1)]
    surplus, given = total - most - (count - 1), [1] * (count - 1)
    while surplus > 0:
        free = [i for i in range(count - 1) if given[i] < most]
        mass, left = sum([weights[i] for i in free]), surplus
        for i in free:
            extra = min(most - given[i], max(1, left * weights[i] // mass), surplus)
            given[i] = given[i] + extra
            surplus = surplus - extra
    return np.array([most] + given)


def uneven(own_key, count, total, reach, skew):
    if count == 2:
        one = jax.random.randint(own_key, (), max(1, total - reach), min(reach, total - 1) + 1)
        return jnp.stack([one, total - one])
    sizes = jnp.asarray(split_up(count, total, reach, skew), jnp.int32)
    twos = (count - 1) // 2
    giver, receiver = sizes[1:1 + 2 * twos:2], sizes[2:2 + 2 * twos:2]
    margin = jnp.minimum(giver - 1, reach - receiver)
    moved = jax.random.randint(jax.random.fold_in(own_key, 1), (twos,), 0, 1 << 20) % (margin + 1)
    sizes = sizes.at[1:1 + 2 * twos:2].set(giver - moved).at[2:2 + 2 * twos:2].set(receiver + moved)
    return sizes[jax.random.permutation(jax.random.fold_in(own_key, 2), count)]


def scatter_about(key, shape, scale, reach, shards=(), kind=jnp.bfloat16):
    level = block_scale(key, shape, shards, -0.22, 0.18) if shards else 1.0
    drawn = jax.random.normal(key, shape, jnp.float32) * scale * level
    return jnp.minimum(jnp.maximum(drawn, -reach), reach).astype(kind)


def setup_inputs(seed: int = 0) -> dict:
    key_of = jax.random.split(jax.random.key(seed), 18)
    return {
        "tokens": scatter_about(key_of[0], (BATCHES, TOKENS, D), 1.0, 6.0, ((0, 2), (1, 16))),
        "in_weight": scatter_about(key_of[1], (D, 3 * D), D ** -0.5, 0.1875, ((0, 2),)),
        "query_bias": scatter_about(key_of[2], (D,), 0.5, 3.0, ((0, 2),)),
        "value_bias": scatter_about(key_of[3], (D,), 0.04, 0.23925781, ((0, 2),)),
        "out_weight": scatter_about(key_of[4], (D, D), (max(1, D // 128)) ** -0.5, 2.0, ((0, 2),)),
        "out_bias": scatter_about(key_of[5], (D,), 0.2, 1.1953125, ((0, 2),)),
        "up_weight": scatter_about(key_of[6], (D, FF), D ** -0.5, 0.1875, ((0, 2),)),
        "up_bias": scatter_about(key_of[7], (FF,), 0.3, 1.796875, ((0, 2),)),
        "down_weight": scatter_about(key_of[8], (FF, D), (FF // 2) ** -0.5, 0.125, ((0, 2),)),
        "down_bias": scatter_about(key_of[9], (D,), 0.4, 2.390625, ((0, 2),)),
        "first_gain": jnp.clip(1.0 + 0.1 * jax.random.normal(key_of[10], (D,), jnp.float32), 0.5, 1.5).astype(jnp.bfloat16),
        "first_shift": scatter_about(key_of[11], (D,), 0.2, 1.1953125, ((0, 2),)),
        "second_gain": jnp.clip(1.0 + 0.1 * jax.random.normal(key_of[12], (D,), jnp.float32), 0.5, 1.5).astype(jnp.bfloat16),
        "second_shift": scatter_about(key_of[13], (D,), 0.2, 1.1953125, ((0, 2),)),
        "lengths": jax.vmap(lambda own: uneven(own, NSEQ, TOKENS, LMAX, 2))(jax.random.split(key_of[14], BATCHES)).reshape((BATCHES, NSEQ)).astype(jnp.int32),
        "slot_places": jax.vmap(lambda own: jax.random.permutation(own, TOKENS))(jax.random.split(key_of[15], BATCHES)).reshape((BATCHES, TOKENS)).astype(jnp.int32),
        "cotangent": scatter_about(key_of[16], (BATCHES, TOKENS, D), 1.0, 6.0, ((0, 2), (1, 16))),
    }


@jax.custom_vjp
def low(v):
    return lax.optimization_barrier(v.astype(jnp.bfloat16)).astype(jnp.float32)

@jax.custom_vjp
def low_back(v):
    return v

def low_keep(v):
    return (low(v), None)

def low_pass(kept, grad):
    return (grad,)

def back_keep(v):
    return (v, None)

def back_low(kept, grad):
    return (low(grad),)
low.defvjp(low_keep, low_pass)
low_back.defvjp(back_keep, back_low)
epsilon = 1e-05
far_below = -1e+30
highest = lax.Precision.HIGHEST

def normalize(values, gain, shift):
    center = values - lax.optimization_barrier(jnp.mean(values, axis=-1, keepdims=True))
    spread = lax.optimization_barrier(jnp.mean(center * center, axis=-1, keepdims=True))
    return center * lax.rsqrt(spread + epsilon) * gain + shift

def gelu_exact(values):
    return jax.nn.gelu(values, approximate=False)

def matmul(left, right):
    return jnp.dot(left, right, precision=highest)

def attend_block(queries, key_rows, value_rows, segments, window, index):
    first = (index * TOK_DEV).astype(jnp.int32)
    stop = first + TOK_DEV
    key_first = jnp.maximum(stop - window, 0).astype(jnp.int32)
    query_block = lax.dynamic_slice_in_dim(queries, first, TOK_DEV, 0)
    key_block = lax.dynamic_slice_in_dim(key_rows, key_first, window, 0)
    value_block = lax.dynamic_slice_in_dim(value_rows, key_first, window, 0)
    query_place = first + jnp.arange(TOK_DEV, dtype=jnp.int32)
    key_place = key_first + jnp.arange(window, dtype=jnp.int32)
    query_segment = lax.dynamic_slice_in_dim(segments, first, TOK_DEV, 0)
    key_segment = lax.dynamic_slice_in_dim(segments, key_first, window, 0)
    allowed = (key_segment[None, :] == query_segment[:, None]) & (key_place[None, :] <= query_place[:, None])
    scores = low_back(jnp.einsum('qhd,khd->hqk', query_block, key_block, precision=highest))
    scores = jnp.where(allowed[None], scores, far_below)
    log_total = jax.nn.logsumexp(scores, axis=2, keepdims=True)
    probs = low(jnp.exp(scores - log_total))
    return jnp.einsum('hqk,khd->qhd', probs, value_block, precision=highest)

def layer(params, inputs, places, lengths):
    in_weight, query_bias, value_bias, out_weight, out_bias, up_weight, up_bias, down_weight, down_bias, first_gain, first_shift, second_gain, second_shift = params
    normed_one = low(normalize(inputs, first_gain, first_shift))
    projected = matmul(normed_one, in_weight)
    queries = low_back(low((projected[:, :D] + query_bias) * HD ** (-0.5)))
    key_rows = low_back(low(projected[:, D:2 * D]))
    value_rows = low_back(low(projected[:, 2 * D:] + value_bias))
    ordered = [jnp.zeros_like(member).at[places].set(member).reshape(TOKENS, H, HD) for member in (queries, key_rows, value_rows)]
    starts = (jnp.cumsum(lengths) - lengths).astype(jnp.int32)
    positions = jnp.arange(TOKENS, dtype=jnp.int32)
    segments = (lax.optimization_barrier(jnp.sum((starts[None, :] <= positions[:, None]).astype(jnp.int32), axis=1)) - 1).astype(jnp.int32)
    window = min(TOKENS, LMAX + TOK_DEV)
    stepper = jax.checkpoint(partial(attend_block, ordered[0], ordered[1], ordered[2], segments, window))
    blocks = lax.map(stepper, jnp.arange(TOKENS // TOK_DEV, dtype=jnp.int32))
    attended = low_back(low(blocks.reshape(TOKENS, D)[places]))
    branch = low_back(matmul(attended, out_weight) + out_bias)
    middle = inputs + branch
    normed_two = low(normalize(middle, second_gain, second_shift))
    hidden = low_back(matmul(normed_two, up_weight) + up_bias)
    active = low(gelu_exact(hidden))
    return middle + matmul(active, down_weight) + down_bias

def forward(params, inputs_all, places_all, lengths_all):
    results = []
    for batch in range(N_FSDP):
        results.append(layer(params, inputs_all[batch], places_all[batch], lengths_all[batch]))
    return jnp.stack(results)

def reference(tokens, in_weight, query_bias, value_bias, out_weight, out_bias, up_weight, up_bias, down_weight, down_bias, first_gain, first_shift, second_gain, second_shift, lengths, slot_places, cotangent):
    params = tuple((member.astype(jnp.float32) for member in (in_weight, query_bias, value_bias, out_weight, out_bias, up_weight, up_bias, down_weight, down_bias, first_gain, first_shift, second_gain, second_shift)))
    inputs = tokens.astype(jnp.float32)

    def apply(weights, values):
        return forward(weights, values, slot_places, lengths)
    result, pullback = jax.vjp(apply, params, inputs)
    grad_params, grad_inputs = pullback(cotangent.astype(jnp.float32))
    in_weight_grad, query_bias_grad, value_bias_grad, out_weight_grad, out_bias_grad, up_weight_grad, up_bias_grad, down_weight_grad, down_bias_grad, first_gain_grad, first_shift_grad, second_gain_grad, second_shift_grad = grad_params
    return (result.astype(jnp.bfloat16), grad_inputs.astype(jnp.bfloat16), in_weight_grad, query_bias_grad, value_bias_grad, out_weight_grad, out_bias_grad, up_weight_grad, up_bias_grad, down_weight_grad, down_bias_grad, first_gain_grad, first_shift_grad, second_gain_grad, second_shift_grad)
```

```python
import jax
import jax.numpy as jnp
from jax import lax
from jax.sharding import PartitionSpec as P

H = 16
HD = 64


epsilon = 1e-05
far_below = -1e30


def normalize(values, gain, shift):
    center = values - jnp.mean(values, axis=-1, keepdims=True)
    spread = jnp.mean(center * center, axis=-1, keepdims=True)
    return center * lax.rsqrt(spread + epsilon) * gain + shift


def gelu_exact(values):
    return jax.nn.gelu(values, approximate=False)


def block_size(total):
    for size in range(min(2048, total), 0, -1):
        if total % size == 0:
            return size
    return total


def segment_of(places, starts):
    return jnp.sum((starts[None, :] <= places[:, None]).astype(jnp.int32), axis=1) - 1


def visible(query_place, query_segment, key_place, key_segment):
    return (key_segment[None, :] == query_segment[:, None]) & (
        key_place[None, :] <= query_place[:, None]
    )


def scores_of(queries, key_rows, allowed):
    scores = jnp.einsum("qhd,khd->hqk", queries, key_rows, preferred_element_type=jnp.float32)
    return jnp.where(allowed[None], scores, far_below)


def inner_rows(left, right):
    return jnp.einsum("tf,tg->fg", left, right, preferred_element_type=jnp.float32)


def times_transposed(left, right):
    return jnp.einsum("tg,fg->tf", left, right, preferred_element_type=jnp.float32)


def key_terms(probs_low, grad_scores, query_rows, grad_rows, size, width):
    grad_keys = jnp.einsum(
        "hqk,qhd->khd", grad_scores, query_rows, preferred_element_type=jnp.float32
    )
    grad_values = jnp.einsum(
        "hqk,qhd->khd", probs_low, grad_rows, preferred_element_type=jnp.float32
    )
    return jnp.concatenate(
        [grad_keys.reshape(size, width), grad_values.reshape(size, width)], axis=1
    )


def body_general(
    tokens,
    in_weight,
    query_bias,
    value_bias,
    out_weight,
    out_bias,
    up_weight,
    up_bias,
    down_weight,
    down_bias,
    first_gain,
    first_shift,
    second_gain,
    second_shift,
    lengths,
    slot_places,
    cotangent,
):
    gathered_params = (
        lax.all_gather(in_weight, "fsdp", axis=0, tiled=True),
        lax.all_gather(query_bias, "fsdp", axis=0, tiled=True),
        lax.all_gather(value_bias, "fsdp", axis=0, tiled=True),
        lax.all_gather(out_weight, "fsdp", axis=0, tiled=True),
        lax.all_gather(out_bias, "fsdp", axis=0, tiled=True),
        lax.all_gather(up_weight, "fsdp", axis=0, tiled=True),
        lax.all_gather(up_bias, "fsdp", axis=0, tiled=True),
        lax.all_gather(down_weight, "fsdp", axis=0, tiled=True),
        lax.all_gather(down_bias, "fsdp", axis=0, tiled=True),
        lax.all_gather(first_gain, "fsdp", axis=0, tiled=True),
        lax.all_gather(first_shift, "fsdp", axis=0, tiled=True),
        lax.all_gather(second_gain, "fsdp", axis=0, tiled=True),
        lax.all_gather(second_shift, "fsdp", axis=0, tiled=True),
    )
    (
        in_full,
        query_shift,
        value_shift,
        out_full,
        out_shift,
        up_full,
        up_shift,
        down_full,
        down_shift,
        gain_first,
        shift_first,
        gain_second,
        shift_second,
    ) = gathered_params
    query_shift = query_shift.astype(jnp.float32)
    value_shift = value_shift.astype(jnp.float32)
    out_shift = out_shift.astype(jnp.float32)
    up_shift = up_shift.astype(jnp.float32)
    down_shift = down_shift.astype(jnp.float32)
    gain_first = gain_first.astype(jnp.float32)
    shift_first = shift_first.astype(jnp.float32)
    gain_second = gain_second.astype(jnp.float32)
    shift_second = shift_second.astype(jnp.float32)
    inputs = tokens[0].astype(jnp.float32)
    rows = inputs.shape[0]
    width = inputs.shape[1]
    scale = HD ** (-0.5)
    places = slot_places[0]
    seq_lengths = lengths[0]
    starts = jnp.cumsum(seq_lengths) - seq_lengths
    key_segments = segment_of(places, starts)
    first_slot = lax.axis_index("ctx") * rows
    query_places = lax.dynamic_slice_in_dim(places, first_slot, rows)
    query_segments = lax.dynamic_slice_in_dim(key_segments, first_slot, rows)
    total_keys = places.shape[0]
    key_step = block_size(total_keys)
    block_count = total_keys // key_step
    place_blocks = places.reshape(block_count, key_step)
    segment_blocks = key_segments.reshape(block_count, key_step)
    normed_one = normalize(inputs, gain_first, shift_first).astype(jnp.bfloat16)
    projected = jnp.dot(normed_one, in_full, preferred_element_type=jnp.float32)
    queries = (
        ((projected[:, :width] + query_shift) * scale).astype(jnp.bfloat16).reshape(rows, H, HD)
    )
    key_value = jnp.concatenate(
        [projected[:, width : 2 * width], projected[:, 2 * width :] + value_shift], axis=1
    ).astype(jnp.bfloat16)
    gathered = lax.all_gather(key_value, "ctx", axis=0, tiled=True)
    pair_blocks = gathered.reshape(block_count, key_step, 2 * width)

    def split_pair(pair, size):
        return (pair[:, :width].reshape(size, H, HD), pair[:, width:].reshape(size, H, HD))

    def max_step(carry, block):
        top, total = carry
        pair, key_place, key_segment = block
        key_rows, value_rows = split_pair(pair, key_step)
        allowed = visible(query_places, query_segments, key_place, key_segment)
        scores = scores_of(queries, key_rows, allowed)
        new_top = jnp.maximum(top, jnp.max(scores, axis=2))
        expand = jnp.where(allowed[None], jnp.exp(scores - new_top[:, :, None]), 0.0)
        total = total * jnp.exp(top - new_top) + jnp.sum(expand, axis=2)
        return ((new_top, total), None)

    start_top = jnp.full((H, rows), far_below, jnp.float32)
    (top, total), unused = lax.scan(
        max_step,
        (start_top, jnp.zeros((H, rows), jnp.float32)),
        (pair_blocks, place_blocks, segment_blocks),
    )
    log_total = top + jnp.log(total)

    def value_step(summed, block):
        pair, key_place, key_segment = block
        key_rows, value_rows = split_pair(pair, key_step)
        allowed = visible(query_places, query_segments, key_place, key_segment)
        scores = scores_of(queries, key_rows, allowed)
        weights = jnp.where(allowed[None], jnp.exp(scores - log_total[:, :, None]), 0.0).astype(
            jnp.bfloat16
        )
        summed = summed + jnp.einsum(
            "hqk,khd->qhd", weights, value_rows, preferred_element_type=jnp.float32
        )
        return (summed, None)

    heads_out, unused = lax.scan(
        value_step,
        jnp.zeros((rows, H, HD), jnp.float32),
        (pair_blocks, place_blocks, segment_blocks),
    )
    attended = heads_out.reshape(rows, width).astype(jnp.bfloat16)
    middle = inputs + jnp.dot(attended, out_full, preferred_element_type=jnp.float32) + out_shift
    normed_two = normalize(middle, gain_second, shift_second).astype(jnp.bfloat16)
    hidden = jnp.dot(normed_two, up_full, preferred_element_type=jnp.float32) + up_shift
    active_full, gelu_back = jax.vjp(gelu_exact, hidden)
    active = active_full.astype(jnp.bfloat16)
    result = middle + jnp.dot(active, down_full, preferred_element_type=jnp.float32) + down_shift
    layer_out = result.astype(jnp.bfloat16)[None]
    grad_low = cotangent[0]
    grad_result = grad_low.astype(jnp.float32)
    down_grad = inner_rows(active, grad_low)
    down_bias_grad = jnp.sum(grad_result, axis=0)
    grad_active = times_transposed(grad_low, down_full)
    grad_hidden = gelu_back(grad_active)[0].astype(jnp.bfloat16)
    up_grad = inner_rows(normed_two, grad_hidden)
    up_bias_grad = jnp.sum(grad_hidden.astype(jnp.float32), axis=0)
    grad_normed_two = times_transposed(grad_hidden, up_full)
    unused, second_back = jax.vjp(normalize, middle, gain_second, shift_second)
    grad_middle_norm, gain_two_grad, shift_two_grad = second_back(grad_normed_two)
    grad_middle = grad_result + grad_middle_norm
    grad_branch = grad_middle.astype(jnp.bfloat16)
    out_grad = inner_rows(attended, grad_branch)
    out_bias_grad = jnp.sum(grad_branch.astype(jnp.float32), axis=0)
    grad_attended = (
        times_transposed(grad_branch, out_full).astype(jnp.bfloat16).reshape(rows, H, HD)
    )
    deltas = jnp.sum(grad_attended.astype(jnp.float32) * heads_out, axis=2).T

    def block_back(key_rows, value_rows, allowed):
        scores = scores_of(queries, key_rows, allowed)
        probs = jnp.where(allowed[None], jnp.exp(scores - log_total[:, :, None]), 0.0)
        grad_probs = jnp.einsum(
            "qhd,khd->hqk", grad_attended, value_rows, preferred_element_type=jnp.float32
        )
        grad_scores = (probs * (grad_probs - deltas[:, :, None])).astype(jnp.bfloat16)
        return (probs.astype(jnp.bfloat16), grad_scores)

    def query_term(grad_scores, key_rows):
        return jnp.einsum("hqk,khd->qhd", grad_scores, key_rows, preferred_element_type=jnp.float32)

    def whole_step(grad_queries, block):
        pair, key_place, key_segment = block
        key_rows, value_rows = split_pair(pair, key_step)
        allowed = visible(query_places, query_segments, key_place, key_segment)
        probs_low, grad_scores = block_back(key_rows, value_rows, allowed)
        grad_queries = grad_queries + query_term(grad_scores, key_rows)
        return (
            grad_queries,
            key_terms(probs_low, grad_scores, queries, grad_attended, key_step, width),
        )

    grad_queries, terms = lax.scan(
        whole_step,
        jnp.zeros((rows, H, HD), jnp.float32),
        (pair_blocks, place_blocks, segment_blocks),
    )
    key_grads = lax.psum_scatter(
        terms.reshape(total_keys, 2 * width), "ctx", scatter_dimension=0, tiled=True
    )
    key_grads_low = key_grads.astype(jnp.bfloat16)
    grad_queries_low = grad_queries.reshape(rows, width).astype(jnp.bfloat16)
    grad_projected = jnp.concatenate([grad_queries_low, key_grads_low], axis=1)
    in_grad_raw = inner_rows(normed_one, grad_projected)
    in_grad = jnp.concatenate([in_grad_raw[:, :width] * scale, in_grad_raw[:, width:]], axis=1)
    query_bias_grad = jnp.sum(grad_queries_low.astype(jnp.float32), axis=0) * scale
    value_bias_grad = jnp.sum(key_grads_low[:, width:].astype(jnp.float32), axis=0)
    grad_normed_one = times_transposed(
        grad_queries_low, in_full[:, :width]
    ) * scale + times_transposed(key_grads_low, in_full[:, width:])
    unused, first_back = jax.vjp(normalize, inputs, gain_first, shift_first)
    grad_inputs_norm, gain_one_grad, shift_one_grad = first_back(grad_normed_one)
    input_grad = (grad_middle + grad_inputs_norm).astype(jnp.bfloat16)[None]
    grads = (
        in_grad,
        query_bias_grad,
        value_bias_grad,
        out_grad,
        out_bias_grad,
        up_grad,
        up_bias_grad,
        down_grad,
        down_bias_grad,
        gain_one_grad,
        shift_one_grad,
        gain_two_grad,
        shift_two_grad,
    )
    summed = (
        lax.psum_scatter(grads[0], ("ctx", "fsdp"), scatter_dimension=0, tiled=True),
        lax.psum_scatter(grads[1], ("ctx", "fsdp"), scatter_dimension=0, tiled=True),
        lax.psum_scatter(grads[2], ("ctx", "fsdp"), scatter_dimension=0, tiled=True),
        lax.psum_scatter(grads[3], ("ctx", "fsdp"), scatter_dimension=0, tiled=True),
        lax.psum_scatter(grads[4], ("ctx", "fsdp"), scatter_dimension=0, tiled=True),
        lax.psum_scatter(grads[5], ("ctx", "fsdp"), scatter_dimension=0, tiled=True),
        lax.psum_scatter(grads[6], ("ctx", "fsdp"), scatter_dimension=0, tiled=True),
        lax.psum_scatter(grads[7], ("ctx", "fsdp"), scatter_dimension=0, tiled=True),
        lax.psum_scatter(grads[8], ("ctx", "fsdp"), scatter_dimension=0, tiled=True),
        lax.psum_scatter(grads[9], ("ctx", "fsdp"), scatter_dimension=0, tiled=True),
        lax.psum_scatter(grads[10], ("ctx", "fsdp"), scatter_dimension=0, tiled=True),
        lax.psum_scatter(grads[11], ("ctx", "fsdp"), scatter_dimension=0, tiled=True),
        lax.psum_scatter(grads[12], ("ctx", "fsdp"), scatter_dimension=0, tiled=True),
    )
    (
        in_weight_grad,
        query_bias_grad_out,
        value_bias_grad_out,
        out_weight_grad,
        out_bias_grad_out,
        up_weight_grad,
        up_bias_grad_out,
        down_weight_grad,
        down_bias_grad_out,
        first_gain_grad,
        first_shift_grad,
        second_gain_grad,
        second_shift_grad,
    ) = summed
    return (
        layer_out,
        input_grad,
        in_weight_grad,
        query_bias_grad_out,
        value_bias_grad_out,
        out_weight_grad,
        out_bias_grad_out,
        up_weight_grad,
        up_bias_grad_out,
        down_weight_grad,
        down_bias_grad_out,
        first_gain_grad,
        first_shift_grad,
        second_gain_grad,
        second_shift_grad,
    )


def body_heads(
    tokens,
    in_weight,
    query_bias,
    value_bias,
    out_weight,
    out_bias,
    up_weight,
    up_bias,
    down_weight,
    down_bias,
    first_gain,
    first_shift,
    second_gain,
    second_shift,
    lengths,
    slot_places,
    cotangent,
):
    low = jnp.bfloat16
    vectors = [
        query_bias,
        value_bias,
        out_bias,
        down_bias,
        first_gain,
        first_shift,
        second_gain,
        second_shift,
    ]
    half = query_bias.shape[0]
    packed = jnp.concatenate(vectors + [up_bias]).reshape(-1, half)
    packed = lax.all_gather(packed, "fsdp", axis=0).astype(jnp.float32)
    pieces = jnp.concatenate([packed[0], packed[1]], axis=1)
    (query_shift, value_shift, out_shift, down_shift) = (pieces[i] for i in range(4))
    (gain_first, shift_first, gain_second, shift_second) = (pieces[i] for i in range(4, 8))
    up_shift = packed[:, 8:].reshape(-1)
    in_full = lax.all_gather(in_weight, "fsdp", axis=0, tiled=True)
    out_full = lax.all_gather(out_weight, "fsdp", axis=0, tiled=True)
    up_full = lax.all_gather(up_weight, "fsdp", axis=0, tiled=True)
    down_full = lax.all_gather(down_weight, "fsdp", axis=0, tiled=True)
    inputs = tokens[0].astype(jnp.float32)
    rows, width = inputs.shape
    scale = HD ** (-0.5)
    places = slot_places[0]
    starts = jnp.cumsum(lengths[0]) - lengths[0]
    segments = segment_of(places, starts)
    allowed = visible(places, segments, places, segments)
    normed_one = normalize(inputs, gain_first, shift_first).astype(low)
    projected = jnp.dot(normed_one, in_full, preferred_element_type=jnp.float32)
    triple = jnp.concatenate(
        [
            (projected[:, :width] + query_shift) * scale,
            projected[:, width : 2 * width],
            projected[:, 2 * width :] + value_shift,
        ],
        axis=1,
    ).astype(low)

    def to_heads(rows_in, count):
        parts = rows_in.reshape(rows, count, H, HD)
        out = lax.all_to_all(parts, "ctx", split_axis=2, concat_axis=0, tiled=True)
        return out.reshape(-1, count, HD)

    def to_tokens(heads_in, count):
        parts = heads_in.reshape(-1, count, 1, HD)
        out = lax.all_to_all(parts, "ctx", split_axis=0, concat_axis=2, tiled=True)
        return out.reshape(rows, count * width)

    head = to_heads(triple, 3)
    queries, key_rows, value_rows = head[:, 0], head[:, 1], head[:, 2]
    scores = jnp.where(allowed, times_transposed(queries, key_rows), far_below)
    top = jnp.max(scores, axis=1, keepdims=True)
    total = jnp.sum(jnp.where(allowed, jnp.exp(scores - top), 0.0), axis=1, keepdims=True)
    probs = jnp.where(allowed, jnp.exp(scores - (top + jnp.log(total))), 0.0)
    probs_low = probs.astype(low)
    head_out = jnp.dot(probs_low, value_rows, preferred_element_type=jnp.float32)
    attended = to_tokens(head_out.astype(low), 1)
    middle = inputs + jnp.dot(attended, out_full, preferred_element_type=jnp.float32) + out_shift
    normed_two = normalize(middle, gain_second, shift_second).astype(low)
    hidden = jnp.dot(normed_two, up_full, preferred_element_type=jnp.float32) + up_shift
    active_full, gelu_back = jax.vjp(gelu_exact, hidden)
    active = active_full.astype(low)
    result = middle + jnp.dot(active, down_full, preferred_element_type=jnp.float32) + down_shift
    layer_out = result.astype(low)[None]
    grad_low = cotangent[0]
    grad_result = grad_low.astype(jnp.float32)

    def scattered(grad):
        return lax.psum_scatter(
            grad.astype(low), ("ctx", "fsdp"), scatter_dimension=0, tiled=True
        ).astype(jnp.float32)

    down_grad = scattered(inner_rows(active, grad_low))
    down_bias_grad = jnp.sum(grad_result, axis=0)
    grad_active = times_transposed(grad_low, down_full)
    grad_hidden = gelu_back(grad_active)[0].astype(low)
    up_grad = scattered(inner_rows(normed_two, grad_hidden))
    up_bias_grad = jnp.sum(grad_hidden.astype(jnp.float32), axis=0)
    grad_normed_two = times_transposed(grad_hidden, up_full)
    unused, second_back = jax.vjp(normalize, middle, gain_second, shift_second)
    grad_middle_norm, gain_two_grad, shift_two_grad = second_back(grad_normed_two)
    grad_middle = grad_result + grad_middle_norm
    grad_branch = grad_middle.astype(low)
    out_grad = scattered(inner_rows(attended, grad_branch))
    out_bias_grad = jnp.sum(grad_branch.astype(jnp.float32), axis=0)
    grad_out = to_heads(times_transposed(grad_branch, out_full).astype(low), 1)[:, 0]
    deltas = jnp.sum(grad_out.astype(jnp.float32) * head_out, axis=1, keepdims=True)
    grad_probs = times_transposed(grad_out, value_rows)
    grad_scores = (probs * (grad_probs - deltas)).astype(low)
    grad_head = jnp.stack(
        [
            jnp.dot(grad_scores, key_rows, preferred_element_type=jnp.float32),
            inner_rows(grad_scores, queries),
            inner_rows(probs_low, grad_out),
        ],
        axis=1,
    ).astype(low)
    grad_projected = to_tokens(grad_head, 3)
    in_raw = inner_rows(normed_one, grad_projected)
    in_grad = scattered(jnp.concatenate([in_raw[:, :width] * scale, in_raw[:, width:]], axis=1))
    bias_sums = jnp.sum(grad_projected.astype(jnp.float32), axis=0)
    grad_normed_one = times_transposed(
        grad_projected[:, :width], in_full[:, :width]
    ) * scale + times_transposed(grad_projected[:, width:], in_full[:, width:])
    unused, first_back = jax.vjp(normalize, inputs, gain_first, shift_first)
    grad_inputs_norm, gain_one_grad, shift_one_grad = first_back(grad_normed_one)
    input_grad = (grad_middle + grad_inputs_norm).astype(low)[None]
    count = lax.axis_size("ctx") * lax.axis_size("fsdp")
    small = (
        bias_sums[:width] * scale,
        bias_sums[2 * width :],
        out_bias_grad,
        up_bias_grad,
        down_bias_grad,
        gain_one_grad,
        shift_one_grad,
        gain_two_grad,
        shift_two_grad,
    )
    split = jnp.concatenate([one.reshape(count, -1) for one in small], axis=1)
    summed = lax.psum_scatter(split, ("ctx", "fsdp"), scatter_dimension=0, tiled=True)[0]
    parts, at = [], 0
    for one in small:
        size = one.shape[0] // count
        parts.append(summed[at : at + size])
        at += size
    return (
        layer_out,
        input_grad,
        in_grad,
        parts[0],
        parts[1],
        out_grad,
        parts[2],
        up_grad,
        parts[3],
        down_grad,
        parts[4],
        parts[5],
        parts[6],
        parts[7],
        parts[8],
    )


def solution(mesh):
    placed = (
        P("fsdp", "ctx", None),
        P("fsdp", None),
        P("fsdp"),
        P("fsdp"),
        P("fsdp", None),
        P("fsdp"),
        P("fsdp", None),
        P("fsdp"),
        P("fsdp", None),
        P("fsdp"),
        P("fsdp"),
        P("fsdp"),
        P("fsdp"),
        P("fsdp"),
        P("fsdp", None),
        P("fsdp", None),
        P("fsdp", "ctx", None),
    )
    return jax.shard_map(
        body_heads if mesh.shape["ctx"] == H else body_general,
        mesh=mesh,
        in_specs=placed,
        out_specs=(
            P("fsdp", "ctx", None),
            P("fsdp", "ctx", None),
            P(("ctx", "fsdp"), None),
            P(("ctx", "fsdp")),
            P(("ctx", "fsdp")),
            P(("ctx", "fsdp"), None),
            P(("ctx", "fsdp")),
            P(("ctx", "fsdp"), None),
            P(("ctx", "fsdp")),
            P(("ctx", "fsdp"), None),
            P(("ctx", "fsdp")),
            P(("ctx", "fsdp")),
            P(("ctx", "fsdp")),
            P(("ctx", "fsdp")),
            P(("ctx", "fsdp")),
        ),
        check_vma=False,
    )
```

```python
import jax
import jax.numpy as jnp
from jax import lax
from typing import Any, NamedTuple
from jax.experimental import pallas as pl
from jax.experimental.pallas import tpu as pltpu
from jax.sharding import PartitionSpec as P

H = 16
HD = 64


epsilon = 1e-05
far_below = -1e30


def normalize(values, gain, shift):
    center = values - jnp.mean(values, axis=-1, keepdims=True)
    spread = jnp.mean(center * center, axis=-1, keepdims=True)
    return center * lax.rsqrt(spread + epsilon) * gain + shift


def gelu_exact(values):
    return jax.nn.gelu(values, approximate=False)


def block_size(total):
    for size in range(min(2048, total), 0, -1):
        if total % size == 0:
            return size
    return total


def segment_of(places, starts):
    return jnp.sum((starts[None, :] <= places[:, None]).astype(jnp.int32), axis=1) - 1


def visible(query_place, query_segment, key_place, key_segment):
    return (key_segment[None, :] == query_segment[:, None]) & (
        key_place[None, :] <= query_place[:, None]
    )


def scores_of(queries, key_rows, allowed):
    scores = jnp.einsum("qhd,khd->hqk", queries, key_rows, preferred_element_type=jnp.float32)
    return jnp.where(allowed[None], scores, far_below)


def inner_rows(left, right):
    return jnp.einsum("tf,tg->fg", left, right, preferred_element_type=jnp.float32)


def times_transposed(left, right):
    return jnp.einsum("tg,fg->tf", left, right, preferred_element_type=jnp.float32)


def key_terms(probs_low, grad_scores, query_rows, grad_rows, size, width):
    grad_keys = jnp.einsum(
        "hqk,qhd->khd", grad_scores, query_rows, preferred_element_type=jnp.float32
    )
    grad_values = jnp.einsum(
        "hqk,qhd->khd", probs_low, grad_rows, preferred_element_type=jnp.float32
    )
    return jnp.concatenate(
        [grad_keys.reshape(size, width), grad_values.reshape(size, width)], axis=1
    )


def body_general(
    tokens,
    in_weight,
    query_bias,
    value_bias,
    out_weight,
    out_bias,
    up_weight,
    up_bias,
    down_weight,
    down_bias,
    first_gain,
    first_shift,
    second_gain,
    second_shift,
    lengths,
    slot_places,
    cotangent,
):
    gathered_params = (
        lax.all_gather(in_weight, "fsdp", axis=0, tiled=True),
        lax.all_gather(query_bias, "fsdp", axis=0, tiled=True),
        lax.all_gather(value_bias, "fsdp", axis=0, tiled=True),
        lax.all_gather(out_weight, "fsdp", axis=0, tiled=True),
        lax.all_gather(out_bias, "fsdp", axis=0, tiled=True),
        lax.all_gather(up_weight, "fsdp", axis=0, tiled=True),
        lax.all_gather(up_bias, "fsdp", axis=0, tiled=True),
        lax.all_gather(down_weight, "fsdp", axis=0, tiled=True),
        lax.all_gather(down_bias, "fsdp", axis=0, tiled=True),
        lax.all_gather(first_gain, "fsdp", axis=0, tiled=True),
        lax.all_gather(first_shift, "fsdp", axis=0, tiled=True),
        lax.all_gather(second_gain, "fsdp", axis=0, tiled=True),
        lax.all_gather(second_shift, "fsdp", axis=0, tiled=True),
    )
    (
        in_full,
        query_shift,
        value_shift,
        out_full,
        out_shift,
        up_full,
        up_shift,
        down_full,
        down_shift,
        gain_first,
        shift_first,
        gain_second,
        shift_second,
    ) = gathered_params
    query_shift = query_shift.astype(jnp.float32)
    value_shift = value_shift.astype(jnp.float32)
    out_shift = out_shift.astype(jnp.float32)
    up_shift = up_shift.astype(jnp.float32)
    down_shift = down_shift.astype(jnp.float32)
    gain_first = gain_first.astype(jnp.float32)
    shift_first = shift_first.astype(jnp.float32)
    gain_second = gain_second.astype(jnp.float32)
    shift_second = shift_second.astype(jnp.float32)
    inputs = tokens[0].astype(jnp.float32)
    rows = inputs.shape[0]
    width = inputs.shape[1]
    scale = HD ** (-0.5)
    places = slot_places[0]
    seq_lengths = lengths[0]
    starts = jnp.cumsum(seq_lengths) - seq_lengths
    key_segments = segment_of(places, starts)
    first_slot = lax.axis_index("ctx") * rows
    query_places = lax.dynamic_slice_in_dim(places, first_slot, rows)
    query_segments = lax.dynamic_slice_in_dim(key_segments, first_slot, rows)
    total_keys = places.shape[0]
    key_step = block_size(total_keys)
    block_count = total_keys // key_step
    place_blocks = places.reshape(block_count, key_step)
    segment_blocks = key_segments.reshape(block_count, key_step)
    normed_one = normalize(inputs, gain_first, shift_first).astype(jnp.bfloat16)
    projected = jnp.dot(normed_one, in_full, preferred_element_type=jnp.float32)
    queries = (
        ((projected[:, :width] + query_shift) * scale).astype(jnp.bfloat16).reshape(rows, H, HD)
    )
    key_value = jnp.concatenate(
        [projected[:, width : 2 * width], projected[:, 2 * width :] + value_shift], axis=1
    ).astype(jnp.bfloat16)
    gathered = lax.all_gather(key_value, "ctx", axis=0, tiled=True)
    pair_blocks = gathered.reshape(block_count, key_step, 2 * width)

    def split_pair(pair, size):
        return (pair[:, :width].reshape(size, H, HD), pair[:, width:].reshape(size, H, HD))

    def max_step(carry, block):
        top, total = carry
        pair, key_place, key_segment = block
        key_rows, value_rows = split_pair(pair, key_step)
        allowed = visible(query_places, query_segments, key_place, key_segment)
        scores = scores_of(queries, key_rows, allowed)
        new_top = jnp.maximum(top, jnp.max(scores, axis=2))
        expand = jnp.where(allowed[None], jnp.exp(scores - new_top[:, :, None]), 0.0)
        total = total * jnp.exp(top - new_top) + jnp.sum(expand, axis=2)
        return ((new_top, total), None)

    start_top = jnp.full((H, rows), far_below, jnp.float32)
    (top, total), unused = lax.scan(
        max_step,
        (start_top, jnp.zeros((H, rows), jnp.float32)),
        (pair_blocks, place_blocks, segment_blocks),
    )
    log_total = top + jnp.log(total)

    def value_step(summed, block):
        pair, key_place, key_segment = block
        key_rows, value_rows = split_pair(pair, key_step)
        allowed = visible(query_places, query_segments, key_place, key_segment)
        scores = scores_of(queries, key_rows, allowed)
        weights = jnp.where(allowed[None], jnp.exp(scores - log_total[:, :, None]), 0.0).astype(
            jnp.bfloat16
        )
        summed = summed + jnp.einsum(
            "hqk,khd->qhd", weights, value_rows, preferred_element_type=jnp.float32
        )
        return (summed, None)

    heads_out, unused = lax.scan(
        value_step,
        jnp.zeros((rows, H, HD), jnp.float32),
        (pair_blocks, place_blocks, segment_blocks),
    )
    attended = heads_out.reshape(rows, width).astype(jnp.bfloat16)
    middle = inputs + jnp.dot(attended, out_full, preferred_element_type=jnp.float32) + out_shift
    normed_two = normalize(middle, gain_second, shift_second).astype(jnp.bfloat16)
    hidden = jnp.dot(normed_two, up_full, preferred_element_type=jnp.float32) + up_shift
    active_full, gelu_back = jax.vjp(gelu_exact, hidden)
    active = active_full.astype(jnp.bfloat16)
    result = middle + jnp.dot(active, down_full, preferred_element_type=jnp.float32) + down_shift
    layer_out = result.astype(jnp.bfloat16)[None]
    grad_low = cotangent[0]
    grad_result = grad_low.astype(jnp.float32)
    down_grad = inner_rows(active, grad_low)
    down_bias_grad = jnp.sum(grad_result, axis=0)
    grad_active = times_transposed(grad_low, down_full)
    grad_hidden = gelu_back(grad_active)[0].astype(jnp.bfloat16)
    up_grad = inner_rows(normed_two, grad_hidden)
    up_bias_grad = jnp.sum(grad_hidden.astype(jnp.float32), axis=0)
    grad_normed_two = times_transposed(grad_hidden, up_full)
    unused, second_back = jax.vjp(normalize, middle, gain_second, shift_second)
    grad_middle_norm, gain_two_grad, shift_two_grad = second_back(grad_normed_two)
    grad_middle = grad_result + grad_middle_norm
    grad_branch = grad_middle.astype(jnp.bfloat16)
    out_grad = inner_rows(attended, grad_branch)
    out_bias_grad = jnp.sum(grad_branch.astype(jnp.float32), axis=0)
    grad_attended = (
        times_transposed(grad_branch, out_full).astype(jnp.bfloat16).reshape(rows, H, HD)
    )
    deltas = jnp.sum(grad_attended.astype(jnp.float32) * heads_out, axis=2).T

    def block_back(key_rows, value_rows, allowed):
        scores = scores_of(queries, key_rows, allowed)
        probs = jnp.where(allowed[None], jnp.exp(scores - log_total[:, :, None]), 0.0)
        grad_probs = jnp.einsum(
            "qhd,khd->hqk", grad_attended, value_rows, preferred_element_type=jnp.float32
        )
        grad_scores = (probs * (grad_probs - deltas[:, :, None])).astype(jnp.bfloat16)
        return (probs.astype(jnp.bfloat16), grad_scores)

    def query_term(grad_scores, key_rows):
        return jnp.einsum("hqk,khd->qhd", grad_scores, key_rows, preferred_element_type=jnp.float32)

    def whole_step(grad_queries, block):
        pair, key_place, key_segment = block
        key_rows, value_rows = split_pair(pair, key_step)
        allowed = visible(query_places, query_segments, key_place, key_segment)
        probs_low, grad_scores = block_back(key_rows, value_rows, allowed)
        grad_queries = grad_queries + query_term(grad_scores, key_rows)
        return (
            grad_queries,
            key_terms(probs_low, grad_scores, queries, grad_attended, key_step, width),
        )

    grad_queries, terms = lax.scan(
        whole_step,
        jnp.zeros((rows, H, HD), jnp.float32),
        (pair_blocks, place_blocks, segment_blocks),
    )
    key_grads = lax.psum_scatter(
        terms.reshape(total_keys, 2 * width), "ctx", scatter_dimension=0, tiled=True
    )
    key_grads_low = key_grads.astype(jnp.bfloat16)
    grad_queries_low = grad_queries.reshape(rows, width).astype(jnp.bfloat16)
    grad_projected = jnp.concatenate([grad_queries_low, key_grads_low], axis=1)
    in_grad_raw = inner_rows(normed_one, grad_projected)
    in_grad = jnp.concatenate([in_grad_raw[:, :width] * scale, in_grad_raw[:, width:]], axis=1)
    query_bias_grad = jnp.sum(grad_queries_low.astype(jnp.float32), axis=0) * scale
    value_bias_grad = jnp.sum(key_grads_low[:, width:].astype(jnp.float32), axis=0)
    grad_normed_one = times_transposed(
        grad_queries_low, in_full[:, :width]
    ) * scale + times_transposed(key_grads_low, in_full[:, width:])
    unused, first_back = jax.vjp(normalize, inputs, gain_first, shift_first)
    grad_inputs_norm, gain_one_grad, shift_one_grad = first_back(grad_normed_one)
    input_grad = (grad_middle + grad_inputs_norm).astype(jnp.bfloat16)[None]
    grads = (
        in_grad,
        query_bias_grad,
        value_bias_grad,
        out_grad,
        out_bias_grad,
        up_grad,
        up_bias_grad,
        down_grad,
        down_bias_grad,
        gain_one_grad,
        shift_one_grad,
        gain_two_grad,
        shift_two_grad,
    )
    summed = (
        lax.psum_scatter(grads[0], ("ctx", "fsdp"), scatter_dimension=0, tiled=True),
        lax.psum_scatter(grads[1], ("ctx", "fsdp"), scatter_dimension=0, tiled=True),
        lax.psum_scatter(grads[2], ("ctx", "fsdp"), scatter_dimension=0, tiled=True),
        lax.psum_scatter(grads[3], ("ctx", "fsdp"), scatter_dimension=0, tiled=True),
        lax.psum_scatter(grads[4], ("ctx", "fsdp"), scatter_dimension=0, tiled=True),
        lax.psum_scatter(grads[5], ("ctx", "fsdp"), scatter_dimension=0, tiled=True),
        lax.psum_scatter(grads[6], ("ctx", "fsdp"), scatter_dimension=0, tiled=True),
        lax.psum_scatter(grads[7], ("ctx", "fsdp"), scatter_dimension=0, tiled=True),
        lax.psum_scatter(grads[8], ("ctx", "fsdp"), scatter_dimension=0, tiled=True),
        lax.psum_scatter(grads[9], ("ctx", "fsdp"), scatter_dimension=0, tiled=True),
        lax.psum_scatter(grads[10], ("ctx", "fsdp"), scatter_dimension=0, tiled=True),
        lax.psum_scatter(grads[11], ("ctx", "fsdp"), scatter_dimension=0, tiled=True),
        lax.psum_scatter(grads[12], ("ctx", "fsdp"), scatter_dimension=0, tiled=True),
    )
    (
        in_weight_grad,
        query_bias_grad_out,
        value_bias_grad_out,
        out_weight_grad,
        out_bias_grad_out,
        up_weight_grad,
        up_bias_grad_out,
        down_weight_grad,
        down_bias_grad_out,
        first_gain_grad,
        first_shift_grad,
        second_gain_grad,
        second_shift_grad,
    ) = summed
    return (
        layer_out,
        input_grad,
        in_weight_grad,
        query_bias_grad_out,
        value_bias_grad_out,
        out_weight_grad,
        out_bias_grad_out,
        up_weight_grad,
        up_bias_grad_out,
        down_weight_grad,
        down_bias_grad_out,
        first_gain_grad,
        first_shift_grad,
        second_gain_grad,
        second_shift_grad,
    )


MESH_ID = pl.DeviceIdType.MESH
LOW = jnp.bfloat16
F32 = jnp.float32
T = 128


def dot(left, right):
    return jnp.dot(left, right, preferred_element_type=jnp.float32)


def dot_nt(left, right):
    return lax.dot_general(left, right, (((1,), (1,)), ((), ())), preferred_element_type=F32)


def dot_tn(left, right):
    return lax.dot_general(left, right, (((0,), (0,)), ((), ())), preferred_element_type=F32)


def turned(block):
    return block.astype(F32).T


def standard(values):
    center = values - jnp.mean(values, axis=1, keepdims=True)
    spread = lax.rsqrt(jnp.mean(center * center, axis=1, keepdims=True) + epsilon)
    return center * spread, spread


def standard_back(grad, gain, unit, spread):
    e = grad * gain
    return spread * (
        e - jnp.mean(e, axis=1, keepdims=True) - unit * jnp.mean(e * unit, axis=1, keepdims=True)
    )


def gelu_pair(hidden):
    phi = 0.5 * (1.0 + lax.erf(hidden * 0.7071067811865476))
    density = jnp.exp(hidden * hidden * -0.5) * 0.3989422804014327
    return hidden * phi, phi + hidden * density


def lanes(index, size):
    return pl.ds(pl.multiple_of(index * size, size), size)


def column_sum(values):
    return jnp.sum(values, axis=0, keepdims=True)


class Sems(NamedTuple):
    send: Any
    recv: Any


class Scratch(NamedTuple):
    vec: Any
    bias: Any
    in_full: Any
    out_full: Any
    up_full: Any
    down_full: Any
    normed_one: Any
    send_qkv: Any
    qkv_t: Any
    kv: Any
    scores: Any
    lse: Any
    delta: Any
    head_out: Any
    send_head: Any
    att_t: Any
    att_all: Any
    att: Any
    middle: Any
    grad_middle: Any
    cot_all: Any
    two_all: Any
    branch_all: Any
    acc_out: Any
    acc_grad: Any
    grad_hidden: Any
    vec_grad: Any
    do_t: Any
    q_rows: Any
    do_rows: Any
    dkv: Any
    down_mine: Any
    down_theirs: Any
    down_pair: Any
    down_line: Any
    up_mine: Any
    up_theirs: Any
    up_pair: Any
    up_line: Any
    up_piece: Any
    out_mine: Any
    out_theirs: Any
    out_pair: Any
    out_line: Any
    dqkv: Any
    gp_t: Any
    in_mine: Any
    in_theirs: Any
    in_pair: Any
    in_send: Any
    in_recv: Any
    vec_send: Any
    vec_recv: Any
    vec_mine: Any
    vec_pair: Any
    sem_load: Any
    sem_pair: Any
    sem_qkv: Any
    sem_one: Any
    sem_relay: Any
    sem_cot: Any
    sem_head: Any
    sem_att: Any
    sem_two: Any
    sem_back: Any
    sem_branch: Any
    sem_line: Any
    sem_grads: Any
    sem_up: Any
    sem_in: Any
    sem_vec: Any
    sem_one_load: Any


def scratch():
    def v(shape, kind):
        return pltpu.VMEM(shape, kind)

    def sems(count):
        return Sems(pltpu.SemaphoreType.DMA((count,)), pltpu.SemaphoreType.DMA((count,)))

    return Scratch(
        vec=v((2, 12, 1, 512), F32),
        bias=v((2, 1, 1024), F32),
        in_full=v((1024, 3072), LOW),
        out_full=v((1024, 1024), LOW),
        up_full=v((1024, 4096), LOW),
        down_full=v((4096, 1024), LOW),
        normed_one=v((128, 1024), LOW),
        send_qkv=v((16, 192, 128), LOW),
        qkv_t=v((192, 2048), LOW),
        kv=v((2048, 128), LOW),
        scores=v((2048, 256), F32),
        lse=v((1, 2048), F32),
        delta=v((1, 2048), F32),
        head_out=v((64, 2048), F32),
        send_head=v((16, 64, 128), LOW),
        att_t=v((16, 64, 128), LOW),
        att_all=v((4, 4, 64, 128), LOW),
        att=v((128, 1024), LOW),
        middle=v((128, 1024), F32),
        grad_middle=v((128, 1024), F32),
        cot_all=v((4, 128, 1024), LOW),
        two_all=v((4, 128, 1024), LOW),
        branch_all=v((4, 128, 1024), LOW),
        acc_out=v((128, 1024), F32),
        acc_grad=v((128, 1024), F32),
        grad_hidden=v((512, 1024), LOW),
        vec_grad=v((16, 1024), F32),
        do_t=v((64, 2048), LOW),
        q_rows=v((2048, 128), LOW),
        do_rows=v((2048, 128), LOW),
        dkv=v((2048, 128), F32),
        down_mine=v((4, 128, 1024), F32),
        down_theirs=v((4, 128, 1024), LOW),
        down_pair=v((4, 128, 1024), LOW),
        down_line=v((3, 128, 1024), LOW),
        up_mine=v((4, 128, 1024), F32),
        up_theirs=v((4, 128, 1024), LOW),
        up_pair=v((4, 128, 1024), LOW),
        up_line=v((3, 128, 1024), LOW),
        up_piece=v((4, 32, 1024), F32),
        out_mine=v((4, 32, 1024), F32),
        out_theirs=v((4, 32, 1024), LOW),
        out_pair=v((4, 32, 1024), LOW),
        out_line=v((3, 32, 1024), LOW),
        dqkv=v((16, 192, 128), LOW),
        gp_t=v((3072, 128), LOW),
        in_mine=v((16, 32, 256), F32),
        in_theirs=v((16, 32, 256), LOW),
        in_pair=v((16, 32, 256), LOW),
        in_send=v((16, 32, 256), LOW),
        in_recv=v((16, 32, 256), LOW),
        vec_send=v((8, 16, 128), F32),
        vec_recv=v((16, 16, 128), F32),
        vec_mine=v((16, 128), F32),
        vec_pair=v((16, 128), F32),
        sem_load=sems(6),
        sem_pair=sems(10),
        sem_qkv=sems(16),
        sem_one=sems(16),
        sem_relay=sems(12),
        sem_cot=sems(3),
        sem_head=sems(16),
        sem_att=sems(3),
        sem_two=sems(3),
        sem_back=sems(16),
        sem_branch=sems(3),
        sem_line=sems(9),
        sem_grads=sems(16),
        sem_up=sems(12),
        sem_in=sems(16),
        sem_vec=sems(16),
        sem_one_load=pltpu.SemaphoreType.DMA((16,)),
    )


def layer_kernel(
    tok_ref,
    cot_ref,
    vec_ref,
    key_ref,
    query_ref,
    in_hbm,
    out_hbm,
    up_hbm,
    down_hbm,
    layer_out,
    input_grad,
    in_out,
    out_out,
    up_out,
    down_out,
    vec_out,
    one_hbm,
    s,
):
    n = 16
    scale = HD ** (-0.5)
    c, f = lax.axis_index("ctx"), lax.axis_index("fsdp")
    z, p = c // 4, c % 4
    y, x = p // 2, p % 2
    home = c - p
    sibling = (c, 1 - f)
    plane_places = [2 * y + 1 - x, 2 * (1 - y) + x, 2 * (1 - y) + 1 - x]
    planes = [(home + place, f) for place in plane_places]
    z_peers = [((z + k) % 4) for k in range(1, 4)]
    first_core = f == 0

    def remote(src, dst, sems, i, j, device):
        return pltpu.make_async_remote_copy(
            src_ref=src,
            dst_ref=dst,
            send_sem=sems.send.at[i],
            recv_sem=sems.recv.at[j],
            device_id=device,
            device_id_type=MESH_ID,
        )

    def each_peer(step):
        def one(k, carry):
            step((c + k) % n)
            return carry

        lax.fori_loop(1, n, one, 0)

    def to_planes(src_of, dst, sems):
        copies = []
        for i in range(3):
            copy = remote(src_of(i), dst.at[1 + i], sems, i, i, planes[i])
            copy.start()
            copies.append(copy)
        return copies

    barrier = pltpu.get_barrier_semaphore()

    def greet(peer):
        pl.semaphore_signal(barrier, inc=1, device_id=(peer, f), device_id_type=MESH_ID)

    each_peer(greet)
    pl.semaphore_signal(barrier, inc=1, device_id=sibling, device_id_type=MESH_ID)
    weights = [
        (in_hbm, s.in_full, 512),
        (out_hbm, s.out_full, 512),
        (up_hbm, s.up_full, 512),
        (down_hbm, s.down_full, 2048),
    ]
    loads, pairs = [], []
    for i, (src, dst, size) in enumerate(weights):
        load = pltpu.make_async_copy(src, dst.at[pl.ds(f * size, size)], s.sem_load.send.at[i])
        load.start()
        loads.append(load)
    s.vec[f] = vec_ref[...]
    pl.semaphore_wait(barrier, n)
    vec_copy = remote(vec_ref, s.vec.at[f], s.sem_pair, 4, 4, sibling)
    vec_copy.start()
    for i, (src, dst, size) in enumerate(weights):
        pair = remote(src, dst.at[pl.ds(f * size, size)], s.sem_pair, i, i, sibling)
        pair.start()
        pairs.append(pair)
    sent = [vec_copy] + pairs

    def row(i):
        return jnp.concatenate([s.vec[0, i], s.vec[1, i]], axis=1)

    unit_one, unused = standard(tok_ref[...].astype(F32))
    vec_copy.wait_recv()
    s.normed_one[...] = (unit_one * row(4) + row(5)).astype(LOW)
    s.bias[0] = row(0)
    s.bias[1] = row(1)
    loads[0].wait()
    pairs[0].wait_recv()

    def qkv_copy(dst):
        return remote(
            s.send_qkv.at[dst], s.qkv_t.at[:, lanes(c, T)], s.sem_qkv, dst, c, (dst, f)
        )

    def project(g, carry):
        group = (z + g) % 4
        for part in range(3):
            at = pl.ds(pl.multiple_of(part * 1024 + group * 256, 256), 256)
            acc = dot(s.normed_one[...], s.in_full[:, at])
            if part == 0:
                acc = (acc + s.bias[0, :, lanes(group, 256)]) * scale
            if part == 2:
                acc = acc + s.bias[1, :, lanes(group, 256)]
            for u in range(2):
                block = acc[:, u * T : (u + 1) * T].T.astype(LOW)
                for w in range(2):
                    s.send_qkv[group * 4 + 2 * u + w, part * 64 : part * 64 + 64, :] = block[
                        w * 64 : w * 64 + 64
                    ]
        for u in range(4):
            dst = group * 4 + u

            @pl.when(dst != c)
            def _():
                qkv_copy(dst).start()

            @pl.when(dst == c)
            def _():
                s.qkv_t[:, lanes(c, T)] = s.send_qkv[dst]

        return carry

    lax.fori_loop(0, 4, project, 0)
    keep = pltpu.make_async_copy(s.normed_one, one_hbm.at[c], s.sem_load.send.at[4])
    keep.start()
    for k in range(3):
        copy = remote(s.normed_one, one_hbm.at[c], s.sem_one, k, c, (z_peers[k] * 4 + p, f))
        copy.start()
        sent.append(copy)
    s.cot_all[0] = cot_ref[...]
    cot_copies = to_planes(lambda i: cot_ref, s.cot_all, s.sem_cot)
    sent += cot_copies

    def qkv_arrived(src):
        remote(
            s.send_qkv.at[src], s.qkv_t.at[:, lanes(src, T)], s.sem_qkv, src, src, (src, f)
        ).wait_recv()

    each_peer(qkv_arrived)

    for i in range(n):
        at = slice(i * T, i * T + T)
        s.kv[at] = turned(s.qkv_t[64:192, at]).astype(LOW)
    nothing = jnp.zeros((64, 256), LOW)

    def seen(keys, at):
        place = jnp.concatenate([key_ref[keys], key_ref[keys]], axis=1)
        return (place >= query_ref[1:2, at]) & (place <= query_ref[0:1, at])

    def head_copy(dst):
        return remote(s.send_head.at[dst], s.att_t.at[p * 4 + z], s.sem_head, dst, c, (dst, f))

    def forward(i, carry):
        block = (c // 2 + i) % 8
        at = lanes(block, 256)
        query = jnp.concatenate([s.qkv_t[0:64, at], nothing], axis=0)
        top = jnp.full((8, 256), far_below, F32)
        for k in range(8):
            keys = slice(k * 256, k * 256 + 256)
            score = jnp.where(seen(keys, at), dot(s.kv[keys], query), far_below)
            s.scores[keys] = score
            top = jnp.maximum(top, jnp.max(score.reshape(32, 8, 256), axis=0))
        top = jnp.max(top, axis=0, keepdims=True)
        total = jnp.zeros((8, 256), F32)
        acc = jnp.zeros((64, 256), F32)
        for k in range(8):
            keys = slice(k * 256, k * 256 + 256)
            grown = jnp.exp(s.scores[keys] - top)
            total = total + jnp.sum(grown.reshape(32, 8, 256), axis=0)
            acc = acc + dot(s.qkv_t[128:192, keys], grown.astype(LOW))
        total = column_sum(total)
        s.lse[:, at] = top + jnp.log(total)
        result = acc / total
        s.head_out[:, at] = result
        for u in range(2):
            dst = block * 2 + u
            s.send_head[dst] = result[:, u * T : u * T + T].astype(LOW)

            @pl.when(dst != c)
            def _():
                head_copy(dst).start()

            @pl.when(dst == c)
            def _():
                s.att_t[p * 4 + z] = s.send_head[dst]

        return carry

    lax.fori_loop(0, 8, forward, 0)

    def head_arrived(src):
        slot = (src % 4) * 4 + src // 4
        remote(s.send_head.at[src], s.att_t.at[slot], s.sem_head, src, src, (src, f)).wait_recv()

    each_peer(head_arrived)
    s.att_all[0] = s.att_t[pl.ds(p * 4, 4)]
    att_copies = to_planes(
        lambda i: s.att_t.at[pl.ds(plane_places[i] * 4, 4)], s.att_all, s.sem_att
    )
    sent += att_copies
    for i in range(8):
        slots = [(h % 4) * 4 + h // 4 for h in (2 * i, 2 * i + 1)]
        block = jnp.concatenate([s.att_t[slots[0]], s.att_t[slots[1]]], axis=0)
        s.att[:, i * T : i * T + T] = turned(block).astype(LOW)

    loads[1].wait()
    pairs[1].wait_recv()
    middle = tok_ref[...].astype(F32) + dot(s.att[...], s.out_full[...]) + row(2)
    s.middle[...] = middle
    unit_two, unused = standard(middle)
    s.two_all[0] = (unit_two * row(6) + row(7)).astype(LOW)
    two_copies = to_planes(lambda i: s.two_all.at[0], s.two_all, s.sem_two)
    sent += two_copies
    for i in (2, 3):
        loads[i].wait()
        pairs[i].wait_recv()
    s.acc_out[...] = jnp.zeros((T, 1024), F32)
    s.acc_grad[...] = jnp.zeros((T, 1024), F32)
    s.vec_grad[...] = jnp.zeros((16, 1024), F32)

    def feed(j, carry):
        at = lanes(j, 512)
        hidden = dot(s.two_all[0], s.up_full[:, at]) + s.vec[j // 4, 8 + j % 4]
        active, slope = gelu_pair(hidden)
        grad_active = dot_nt(cot_ref[...], s.down_full[at, :])
        grad_hidden = (grad_active * slope).astype(LOW)
        s.acc_out[...] += dot(active.astype(LOW), s.down_full[at, :])
        s.acc_grad[...] += dot_nt(grad_hidden, s.up_full[:, at])
        summed = column_sum(grad_hidden.astype(F32))
        for q in range(4):
            s.vec_grad[8 + q : 9 + q, lanes(j, T)] = summed[:, q * T : q * T + T]
        return carry

    lax.fori_loop(0, 8, feed, 0)
    layer_out[...] = (s.middle[...] + s.acc_out[...] + row(3)).astype(LOW)
    grad_result = cot_ref[...].astype(F32)
    s.vec_grad[3:4] = column_sum(grad_result)
    unit_two, spread_two = standard(s.middle[...])
    grad_two = s.acc_grad[...]
    s.vec_grad[6:7] = column_sum(grad_two * unit_two)
    s.vec_grad[7:8] = column_sum(grad_two)
    grad_middle = grad_result + standard_back(grad_two, row(6), unit_two, spread_two)
    s.grad_middle[...] = grad_middle
    branch = grad_middle.astype(LOW)
    s.branch_all[0] = branch
    s.vec_grad[2:3] = column_sum(branch.astype(F32))

    def head_done(dst):
        head_copy(dst).wait_send()

    each_peer(head_done)
    for i in range(4):
        at = slice(i * 256, i * 256 + 256)
        part = dot_nt(s.out_full[at, :], branch).astype(LOW)
        s.send_head[4 * i : 4 * i + 4] = part.reshape(4, 64, T)

    def back_copy(dst):
        return remote(s.send_head.at[dst], s.do_t.at[:, lanes(c, T)], s.sem_back, dst, c, (dst, f))

    each_peer(lambda dst: back_copy(dst).start())
    s.do_t[:, lanes(c, T)] = s.send_head[c]
    branch_copies = to_planes(lambda i: s.branch_all.at[0], s.branch_all, s.sem_branch)
    sent += branch_copies

    def one_arrived(src):
        remote(s.normed_one, one_hbm.at[src], s.sem_one, 0, src, (src, f)).wait_recv()

    keep.wait()
    for k in range(3):
        one_arrived(z_peers[k] * 4 + p)
    for k in range(4):
        slot = (c if k == 0 else z_peers[k - 1] * 4 + p)
        for i in range(3):
            copy = pltpu.make_async_remote_copy(
                src_ref=one_hbm.at[slot],
                dst_ref=one_hbm.at[slot],
                send_sem=s.sem_relay.send.at[k * 3 + i],
                recv_sem=s.sem_one.recv.at[slot],
                device_id=planes[i],
                device_id_type=MESH_ID,
            )
            copy.start()
            sent.append(copy)

    for i in range(3):
        cot_copies[i].wait_recv()
        two_copies[i].wait_recv()

    def plane_rows(ref):
        return ref[...].reshape(512, 1024)

    def strip(q, carry):
        at = pl.ds(pl.multiple_of(q * 1024 + p * 256, 256), 256)
        shift = s.vec[q // 2, 8 + (q % 2) * 2 + p // 2, :, lanes(p % 2, 256)]
        hidden = dot(plane_rows(s.two_all), s.up_full[:, at]) + shift
        active, slope = gelu_pair(hidden)
        grad_active = dot_nt(plane_rows(s.cot_all), s.down_full[at, :])
        s.grad_hidden[:, lanes(q, 256)] = (grad_active * slope).astype(LOW)
        part = dot_tn(active.astype(LOW), plane_rows(s.cot_all))
        s.down_mine[q] = jnp.where(first_core, part[:T], part[T:])
        s.down_theirs[q] = jnp.where(first_core, part[T:], part[:T]).astype(LOW)
        return carry

    lax.fori_loop(0, 4, strip, 0)
    down_pair = remote(s.down_theirs, s.down_pair, s.sem_pair, 5, 5, sibling)
    down_pair.start()

    def split_rows(part):
        parts = part.reshape(4, 2, 32, 1024)
        mine = jnp.where(first_core, parts[:, 0], parts[:, 1])
        theirs = jnp.where(first_core, parts[:, 1], parts[:, 0])
        return mine, theirs.astype(LOW)

    def up_rows(q, carry):
        left = s.two_all[:, :, lanes(q, 256)].reshape(512, 256)
        mine, theirs = split_rows(dot_tn(left, s.grad_hidden[...]))
        s.up_mine[q] = mine.reshape(T, 1024)
        s.up_theirs[q] = theirs.reshape(T, 1024)
        return carry

    lax.fori_loop(0, 4, up_rows, 0)
    up_pair = remote(s.up_theirs, s.up_pair, s.sem_pair, 6, 6, sibling)
    up_pair.start()

    def to_line(mine, theirs, pair, line, base):
        copies = []
        for k in range(3):
            at = z_peers[k]
            theirs[at] = (
                mine[at] + pair[at].astype(F32)
            ).astype(LOW)
            copy = remote(
                theirs.at[at],
                line.at[k],
                s.sem_line,
                base + k,
                base + k,
                (at * 4 + p, f),
            )
            copy.start()
            copies.append(copy)
        mine[z] += pair[z].astype(F32)
        return copies

    down_pair.wait()
    down_line = to_line(s.down_mine, s.down_theirs, s.down_pair, s.down_line, 0)
    for i in range(3):
        att_copies[i].wait_recv()
        branch_copies[i].wait_recv()
    part = jnp.zeros((256, 1024), F32)
    for i in range(4):
        part = part + dot(s.att_all[i].reshape(256, T), s.branch_all[i])
    mine, theirs = split_rows(part)
    s.out_mine[...] = mine
    s.out_theirs[...] = theirs
    out_pair = remote(s.out_theirs, s.out_pair, s.sem_pair, 7, 7, sibling)
    out_pair.start()
    up_pair.wait()
    up_line = to_line(s.up_mine, s.up_theirs, s.up_pair, s.up_line, 3)
    out_pair.wait()
    out_line = to_line(s.out_mine, s.out_theirs, s.out_pair, s.out_line, 6)
    sent += down_line + up_line + out_line

    def qkv_done(dst):
        qkv_copy(dst).wait_send()

    each_peer(qkv_done)

    def back_arrived(src):
        remote(
            s.send_head.at[src], s.do_t.at[:, lanes(src, T)], s.sem_back, src, src, (src, f)
        ).wait_recv()

    each_peer(back_arrived)
    small_nothing = jnp.zeros((64, T), LOW)
    for i in range(n):
        at = slice(i * T, i * T + T)
        s.q_rows[at] = turned(
            jnp.concatenate([s.qkv_t[0:64, at], small_nothing], axis=0)
        ).astype(LOW)
        s.do_rows[at] = turned(
            jnp.concatenate([small_nothing, s.do_t[:, at]], axis=0)
        ).astype(LOW)
    s.delta[...] = column_sum(s.do_t[...].astype(F32) * s.head_out[...])
    s.dkv[...] = jnp.zeros((2048, 128), F32)

    def backward(block, carry):
        at = lanes(block, 256)
        query = jnp.concatenate([s.qkv_t[0:64, at], nothing], axis=0)
        grad = jnp.concatenate([nothing, s.do_t[:, at]], axis=0)
        lse, delta = s.lse[:, at], s.delta[:, at]
        dq = jnp.zeros((64, 256), F32)
        for k in range(8):
            keys = slice(k * 256, k * 256 + 256)
            score = dot(s.kv[keys], query)
            prob = jnp.where(seen(keys, at), jnp.exp(score - lse), 0.0)
            grad_prob = dot(s.kv[keys], grad)
            grad_score = (prob * (grad_prob - delta)).astype(LOW)
            s.dkv[keys] += dot(grad_score, s.q_rows[at]) + dot(
                prob.astype(LOW), s.do_rows[at]
            )
            dq = dq + dot(s.qkv_t[64:128, keys], grad_score)
        for u in range(2):
            s.send_qkv[block * 2 + u, 0:64] = dq[:, u * T : u * T + T].astype(LOW)
        return carry

    lax.fori_loop(0, 8, backward, 0)

    def grads_copy(dst):
        return remote(s.send_qkv.at[dst], s.dqkv.at[c], s.sem_grads, dst, c, (dst, f))

    for i in range(n):
        s.send_qkv[i, 64:192] = s.dkv[i * T : i * T + T].T.astype(LOW)
    each_peer(lambda dst: grads_copy(dst).start())
    s.dqkv[c] = s.send_qkv[c]

    for k in range(4):
        base = (z + k) % 4 * 4
        for i in range(3):
            one_arrived(base + plane_places[i])
    one_full = s.down_full.at[pl.ds(0, 2048)]
    one_loads = []
    for i in range(n):
        load = pltpu.make_async_copy(
            one_hbm.at[i], s.down_full.at[pl.ds(i * T, T)], s.sem_one_load.at[i]
        )
        load.start()
        one_loads.append(load)
    for load in one_loads:
        load.wait()
    head_grad = jnp.concatenate([s.send_qkv[i] for i in range(n)], axis=1)
    for i in range(4):
        part = dot(head_grad, s.down_full[0:2048, i * 256 : i * 256 + 256])
        part = jnp.concatenate(
            [part[0:64] * scale, part[64:192], jnp.zeros((64, 256), F32)], axis=0
        )
        for u in range(2):
            parts = part[:, u * T : u * T + T].T.reshape(2, 2, 32, 256)
            at = slice(4 * i + 2 * u, 4 * i + 2 * u + 2)
            s.in_mine[at] = jnp.where(first_core, parts[:, 0], parts[:, 1])
            s.in_theirs[at] = jnp.where(first_core, parts[:, 1], parts[:, 0]).astype(LOW)
    in_pair = remote(s.in_theirs, s.in_pair, s.sem_pair, 8, 8, sibling)
    in_pair.start()

    def grads_arrived(src):
        remote(s.send_qkv.at[src], s.dqkv.at[src], s.sem_grads, src, src, (src, f)).wait_recv()

    in_pair.wait()
    s.in_send[...] = (s.in_mine[...] + s.in_pair[...].astype(F32)).astype(LOW)

    def in_copy(dst):
        return remote(s.in_send.at[dst], s.in_recv.at[c], s.sem_in, dst, c, (dst, f))

    each_peer(lambda dst: in_copy(dst).start())
    s.in_recv[c] = s.in_send[c]
    each_peer(grads_arrived)
    for h in range(n):
        s.gp_t[h * 64 : h * 64 + 64] = s.dqkv[h, 0:64] * jnp.asarray(scale, LOW)
        s.gp_t[1024 + h * 64 : 1088 + h * 64] = s.dqkv[h, 64:128]
        s.gp_t[2048 + h * 64 : 2112 + h * 64] = s.dqkv[h, 128:192]
    ones = jnp.ones((8, T), LOW)
    s.vec_grad[0:1] = dot_nt(ones, s.gp_t[0:1024])[0:1]
    s.vec_grad[1:2] = dot_nt(ones, s.gp_t[2048:3072])[0:1]
    for i in range(4):
        at = slice(i * 256, i * 256 + 256)
        s.acc_grad[:, at] = dot(s.in_full[at, :], s.gp_t[...]).T
    unit_one, spread_one = standard(tok_ref[...].astype(F32))
    grad_one = s.acc_grad[...]
    s.vec_grad[4:5] = column_sum(grad_one * unit_one)
    s.vec_grad[5:6] = column_sum(grad_one)
    for i in range(8):
        s.vec_send[i] = s.vec_grad[:, i * T : i * T + T]

    def vec_to(dst):
        return remote(s.vec_send.at[dst // 2], s.vec_recv.at[c], s.sem_vec, dst, c, (dst, f))

    each_peer(lambda dst: vec_to(dst).start())
    s.vec_recv[c] = s.vec_send[c // 2]
    input_grad[...] = (
        s.grad_middle[...] + standard_back(grad_one, row(4), unit_one, spread_one)
    ).astype(LOW)

    for copy in up_line:
        copy.wait_recv()
    up_sum = s.up_mine[z]
    for k in range(3):
        up_sum = up_sum + s.up_line[k].astype(F32)
    s.up_piece[...] = up_sum.reshape(4, 32, 1024)
    up_copies = []
    for i in range(3):
        for q in range(4):
            copy = remote(
                s.up_piece.at[plane_places[i], :, pl.ds(q * 256, 256)],
                up_out.at[:, pl.ds(pl.multiple_of(q * 1024 + p * 256, 256), 256)],
                s.sem_up,
                i * 4 + q,
                i * 4 + q,
                planes[i],
            )
            copy.start()
            up_copies.append(copy)
    for q in range(4):
        up_out[:, pl.ds(pl.multiple_of(q * 1024 + p * 256, 256), 256)] = s.up_piece[
            p, :, q * 256 : q * 256 + 256
        ]
    for copy in down_line:
        copy.wait_recv()
    down_sum = s.down_mine[z]
    for k in range(3):
        down_sum = down_sum + s.down_line[k].astype(F32)
    down_out[...] = down_sum
    for copy in out_line:
        copy.wait_recv()
    out_sum = s.out_mine[z]
    for k in range(3):
        out_sum = out_sum + s.out_line[k].astype(F32)
    out_out[...] = out_sum

    def vec_arrived(src):
        remote(
            s.vec_send.at[src // 2], s.vec_recv.at[src], s.sem_vec, src, src, (src, f)
        ).wait_recv()

    each_peer(vec_arrived)
    s.vec_mine[...] = jnp.sum(s.vec_recv[...], axis=0)
    vec_pair = remote(s.vec_mine, s.vec_pair, s.sem_pair, 9, 9, sibling)
    vec_pair.start()

    def in_arrived(src):
        remote(s.in_send.at[src], s.in_recv.at[src], s.sem_in, src, src, (src, f)).wait_recv()

    each_peer(in_arrived)
    for part in range(3):
        for i in range(8):
            pieces = [
                s.in_recv[2 * i + w, :, part * 64 : part * 64 + 64].astype(F32)
                for w in range(2)
            ]
            at = part * 1024 + i * T
            in_out[:, at : at + T] = jnp.concatenate(pieces, axis=1)
    vec_pair.wait()
    vec_out[...] = s.vec_mine[...] + s.vec_pair[...]
    for copy in up_copies:
        copy.wait()
    for copy in sent:
        copy.wait_send()

    def all_sent(dst):
        back_copy(dst).wait_send()
        grads_copy(dst).wait_send()
        in_copy(dst).wait_send()
        vec_to(dst).wait_send()

    each_peer(all_sent)


def body_fused(
    tokens,
    in_weight,
    query_bias,
    value_bias,
    out_weight,
    out_bias,
    up_weight,
    up_bias,
    down_weight,
    down_bias,
    first_gain,
    first_shift,
    second_gain,
    second_shift,
    lengths,
    slot_places,
    cotangent,
):
    vectors = jnp.concatenate(
        [
            query_bias,
            value_bias,
            out_bias,
            down_bias,
            first_gain,
            first_shift,
            second_gain,
            second_shift,
            up_bias,
        ]
    )
    vectors = vectors.astype(F32).reshape(12, 1, 512)
    places = slot_places[0]
    starts = jnp.cumsum(lengths[0]) - lengths[0]
    first = jnp.max(jnp.where(starts[None, :] <= places[:, None], starts[None, :], 0), axis=1)
    query_info = jnp.zeros((8, places.shape[0]), jnp.int32).at[0].set(places).at[1].set(first)
    key_info = jnp.broadcast_to(places[:, None], (places.shape[0], T))
    hbm = pl.BlockSpec(memory_space=pl.ANY)
    vmem = pl.BlockSpec(memory_space=pltpu.VMEM)
    outs = pl.pallas_call(
        layer_kernel,
        out_shape=(
            jax.ShapeDtypeStruct((T, 1024), LOW),
            jax.ShapeDtypeStruct((T, 1024), LOW),
            jax.ShapeDtypeStruct((32, 3072), F32),
            jax.ShapeDtypeStruct((32, 1024), F32),
            jax.ShapeDtypeStruct((32, 4096), F32),
            jax.ShapeDtypeStruct((128, 1024), F32),
            jax.ShapeDtypeStruct((16, 128), F32),
            jax.ShapeDtypeStruct((16, T, 1024), LOW),
        ),
        in_specs=[vmem] * 5 + [hbm] * 4,
        out_specs=(vmem,) * 7 + (hbm,),
        scratch_shapes=[scratch()],
        compiler_params=pltpu.CompilerParams(
            collective_id=0, has_side_effects=True, vmem_limit_bytes=60 * 2**20
        ),
        cost_estimate=pl.CostEstimate(
            flops=16 * 10**9, bytes_accessed=40 * 2**20, transcendentals=10**7
        ),
    )(
        tokens[0],
        cotangent[0],
        vectors,
        key_info,
        query_info,
        in_weight,
        out_weight,
        up_weight,
        down_weight,
    )
    layer_out, input_grad, in_grad, out_grad, up_grad, down_grad, vec = outs[:7]
    index = lax.axis_index("ctx") * 2 + lax.axis_index("fsdp")
    at = index % 4
    small = lax.dynamic_slice(vec, (0, at * 32), (8, 32))
    up_small = lax.dynamic_slice(vec, (8 + at, 0), (1, 128))[0]
    return (
        layer_out[None],
        input_grad[None],
        in_grad,
        small[0],
        small[1],
        out_grad,
        small[2],
        up_grad,
        up_small,
        down_grad,
        small[3],
        small[4],
        small[5],
        small[6],
        small[7],
    )


def solution(mesh):
    placed = (
        P("fsdp", "ctx", None),
        P("fsdp", None),
        P("fsdp"),
        P("fsdp"),
        P("fsdp", None),
        P("fsdp"),
        P("fsdp", None),
        P("fsdp"),
        P("fsdp", None),
        P("fsdp"),
        P("fsdp"),
        P("fsdp"),
        P("fsdp"),
        P("fsdp"),
        P("fsdp", None),
        P("fsdp", None),
        P("fsdp", "ctx", None),
    )
    return jax.shard_map(
        body_fused if mesh.shape["ctx"] == H else body_general,
        mesh=mesh,
        in_specs=placed,
        out_specs=(
            P("fsdp", "ctx", None),
            P("fsdp", "ctx", None),
            P(("ctx", "fsdp"), None),
            P(("ctx", "fsdp")),
            P(("ctx", "fsdp")),
            P(("ctx", "fsdp"), None),
            P(("ctx", "fsdp")),
            P(("ctx", "fsdp"), None),
            P(("ctx", "fsdp")),
            P(("ctx", "fsdp"), None),
            P(("ctx", "fsdp")),
            P(("ctx", "fsdp")),
            P(("ctx", "fsdp")),
            P(("ctx", "fsdp")),
            P(("ctx", "fsdp")),
        ),
        check_vma=False,
    )
```

```python
import jax
import jax.numpy as jnp
from jax import lax
from typing import Any, NamedTuple
from jax.experimental import pallas as pl
from jax.experimental.pallas import tpu as pltpu
from jax.sharding import PartitionSpec as P

H = 16
HD = 64


epsilon = 1e-05
far_below = -1e30


def normalize(values, gain, shift):
    center = values - jnp.mean(values, axis=-1, keepdims=True)
    spread = jnp.mean(center * center, axis=-1, keepdims=True)
    return center * lax.rsqrt(spread + epsilon) * gain + shift


def gelu_exact(values):
    return jax.nn.gelu(values, approximate=False)


def block_size(total):
    for size in range(min(2048, total), 0, -1):
        if total % size == 0:
            return size
    return total


def segment_of(places, starts):
    return jnp.sum((starts[None, :] <= places[:, None]).astype(jnp.int32), axis=1) - 1


def visible(query_place, query_segment, key_place, key_segment):
    return (key_segment[None, :] == query_segment[:, None]) & (
        key_place[None, :] <= query_place[:, None]
    )


def scores_of(queries, key_rows, allowed):
    scores = jnp.einsum("qhd,khd->hqk", queries, key_rows, preferred_element_type=jnp.float32)
    return jnp.where(allowed[None], scores, far_below)


def inner_rows(left, right):
    return jnp.einsum("tf,tg->fg", left, right, preferred_element_type=jnp.float32)


def times_transposed(left, right):
    return jnp.einsum("tg,fg->tf", left, right, preferred_element_type=jnp.float32)


def key_terms(probs_low, grad_scores, query_rows, grad_rows, size, width):
    grad_keys = jnp.einsum(
        "hqk,qhd->khd", grad_scores, query_rows, preferred_element_type=jnp.float32
    )
    grad_values = jnp.einsum(
        "hqk,qhd->khd", probs_low, grad_rows, preferred_element_type=jnp.float32
    )
    return jnp.concatenate(
        [grad_keys.reshape(size, width), grad_values.reshape(size, width)], axis=1
    )


def body_general(
    tokens,
    in_weight,
    query_bias,
    value_bias,
    out_weight,
    out_bias,
    up_weight,
    up_bias,
    down_weight,
    down_bias,
    first_gain,
    first_shift,
    second_gain,
    second_shift,
    lengths,
    slot_places,
    cotangent,
):
    gathered_params = (
        lax.all_gather(in_weight, "fsdp", axis=0, tiled=True),
        lax.all_gather(query_bias, "fsdp", axis=0, tiled=True),
        lax.all_gather(value_bias, "fsdp", axis=0, tiled=True),
        lax.all_gather(out_weight, "fsdp", axis=0, tiled=True),
        lax.all_gather(out_bias, "fsdp", axis=0, tiled=True),
        lax.all_gather(up_weight, "fsdp", axis=0, tiled=True),
        lax.all_gather(up_bias, "fsdp", axis=0, tiled=True),
        lax.all_gather(down_weight, "fsdp", axis=0, tiled=True),
        lax.all_gather(down_bias, "fsdp", axis=0, tiled=True),
        lax.all_gather(first_gain, "fsdp", axis=0, tiled=True),
        lax.all_gather(first_shift, "fsdp", axis=0, tiled=True),
        lax.all_gather(second_gain, "fsdp", axis=0, tiled=True),
        lax.all_gather(second_shift, "fsdp", axis=0, tiled=True),
    )
    (
        in_full,
        query_shift,
        value_shift,
        out_full,
        out_shift,
        up_full,
        up_shift,
        down_full,
        down_shift,
        gain_first,
        shift_first,
        gain_second,
        shift_second,
    ) = gathered_params
    query_shift = query_shift.astype(jnp.float32)
    value_shift = value_shift.astype(jnp.float32)
    out_shift = out_shift.astype(jnp.float32)
    up_shift = up_shift.astype(jnp.float32)
    down_shift = down_shift.astype(jnp.float32)
    gain_first = gain_first.astype(jnp.float32)
    shift_first = shift_first.astype(jnp.float32)
    gain_second = gain_second.astype(jnp.float32)
    shift_second = shift_second.astype(jnp.float32)
    inputs = tokens[0].astype(jnp.float32)
    rows = inputs.shape[0]
    width = inputs.shape[1]
    scale = HD ** (-0.5)
    places = slot_places[0]
    seq_lengths = lengths[0]
    starts = jnp.cumsum(seq_lengths) - seq_lengths
    key_segments = segment_of(places, starts)
    first_slot = lax.axis_index("ctx") * rows
    query_places = lax.dynamic_slice_in_dim(places, first_slot, rows)
    query_segments = lax.dynamic_slice_in_dim(key_segments, first_slot, rows)
    total_keys = places.shape[0]
    key_step = block_size(total_keys)
    block_count = total_keys // key_step
    place_blocks = places.reshape(block_count, key_step)
    segment_blocks = key_segments.reshape(block_count, key_step)
    normed_one = normalize(inputs, gain_first, shift_first).astype(jnp.bfloat16)
    projected = jnp.dot(normed_one, in_full, preferred_element_type=jnp.float32)
    queries = (
        ((projected[:, :width] + query_shift) * scale).astype(jnp.bfloat16).reshape(rows, H, HD)
    )
    key_value = jnp.concatenate(
        [projected[:, width : 2 * width], projected[:, 2 * width :] + value_shift], axis=1
    ).astype(jnp.bfloat16)
    gathered = lax.all_gather(key_value, "ctx", axis=0, tiled=True)
    pair_blocks = gathered.reshape(block_count, key_step, 2 * width)

    def split_pair(pair, size):
        return (pair[:, :width].reshape(size, H, HD), pair[:, width:].reshape(size, H, HD))

    def max_step(carry, block):
        top, total = carry
        pair, key_place, key_segment = block
        key_rows, value_rows = split_pair(pair, key_step)
        allowed = visible(query_places, query_segments, key_place, key_segment)
        scores = scores_of(queries, key_rows, allowed)
        new_top = jnp.maximum(top, jnp.max(scores, axis=2))
        expand = jnp.where(allowed[None], jnp.exp(scores - new_top[:, :, None]), 0.0)
        total = total * jnp.exp(top - new_top) + jnp.sum(expand, axis=2)
        return ((new_top, total), None)

    start_top = jnp.full((H, rows), far_below, jnp.float32)
    (top, total), unused = lax.scan(
        max_step,
        (start_top, jnp.zeros((H, rows), jnp.float32)),
        (pair_blocks, place_blocks, segment_blocks),
    )
    log_total = top + jnp.log(total)

    def value_step(summed, block):
        pair, key_place, key_segment = block
        key_rows, value_rows = split_pair(pair, key_step)
        allowed = visible(query_places, query_segments, key_place, key_segment)
        scores = scores_of(queries, key_rows, allowed)
        weights = jnp.where(allowed[None], jnp.exp(scores - log_total[:, :, None]), 0.0).astype(
            jnp.bfloat16
        )
        summed = summed + jnp.einsum(
            "hqk,khd->qhd", weights, value_rows, preferred_element_type=jnp.float32
        )
        return (summed, None)

    heads_out, unused = lax.scan(
        value_step,
        jnp.zeros((rows, H, HD), jnp.float32),
        (pair_blocks, place_blocks, segment_blocks),
    )
    attended = heads_out.reshape(rows, width).astype(jnp.bfloat16)
    middle = inputs + jnp.dot(attended, out_full, preferred_element_type=jnp.float32) + out_shift
    normed_two = normalize(middle, gain_second, shift_second).astype(jnp.bfloat16)
    hidden = jnp.dot(normed_two, up_full, preferred_element_type=jnp.float32) + up_shift
    active_full, gelu_back = jax.vjp(gelu_exact, hidden)
    active = active_full.astype(jnp.bfloat16)
    result = middle + jnp.dot(active, down_full, preferred_element_type=jnp.float32) + down_shift
    layer_out = result.astype(jnp.bfloat16)[None]
    grad_low = cotangent[0]
    grad_result = grad_low.astype(jnp.float32)
    down_grad = inner_rows(active, grad_low)
    down_bias_grad = jnp.sum(grad_result, axis=0)
    grad_active = times_transposed(grad_low, down_full)
    grad_hidden = gelu_back(grad_active)[0].astype(jnp.bfloat16)
    up_grad = inner_rows(normed_two, grad_hidden)
    up_bias_grad = jnp.sum(grad_hidden.astype(jnp.float32), axis=0)
    grad_normed_two = times_transposed(grad_hidden, up_full)
    unused, second_back = jax.vjp(normalize, middle, gain_second, shift_second)
    grad_middle_norm, gain_two_grad, shift_two_grad = second_back(grad_normed_two)
    grad_middle = grad_result + grad_middle_norm
    grad_branch = grad_middle.astype(jnp.bfloat16)
    out_grad = inner_rows(attended, grad_branch)
    out_bias_grad = jnp.sum(grad_branch.astype(jnp.float32), axis=0)
    grad_attended = (
        times_transposed(grad_branch, out_full).astype(jnp.bfloat16).reshape(rows, H, HD)
    )
    deltas = jnp.sum(grad_attended.astype(jnp.float32) * heads_out, axis=2).T

    def block_back(key_rows, value_rows, allowed):
        scores = scores_of(queries, key_rows, allowed)
        probs = jnp.where(allowed[None], jnp.exp(scores - log_total[:, :, None]), 0.0)
        grad_probs = jnp.einsum(
            "qhd,khd->hqk", grad_attended, value_rows, preferred_element_type=jnp.float32
        )
        grad_scores = (probs * (grad_probs - deltas[:, :, None])).astype(jnp.bfloat16)
        return (probs.astype(jnp.bfloat16), grad_scores)

    def query_term(grad_scores, key_rows):
        return jnp.einsum("hqk,khd->qhd", grad_scores, key_rows, preferred_element_type=jnp.float32)

    def whole_step(grad_queries, block):
        pair, key_place, key_segment = block
        key_rows, value_rows = split_pair(pair, key_step)
        allowed = visible(query_places, query_segments, key_place, key_segment)
        probs_low, grad_scores = block_back(key_rows, value_rows, allowed)
        grad_queries = grad_queries + query_term(grad_scores, key_rows)
        return (
            grad_queries,
            key_terms(probs_low, grad_scores, queries, grad_attended, key_step, width),
        )

    grad_queries, terms = lax.scan(
        whole_step,
        jnp.zeros((rows, H, HD), jnp.float32),
        (pair_blocks, place_blocks, segment_blocks),
    )
    key_grads = lax.psum_scatter(
        terms.reshape(total_keys, 2 * width), "ctx", scatter_dimension=0, tiled=True
    )
    key_grads_low = key_grads.astype(jnp.bfloat16)
    grad_queries_low = grad_queries.reshape(rows, width).astype(jnp.bfloat16)
    grad_projected = jnp.concatenate([grad_queries_low, key_grads_low], axis=1)
    in_grad_raw = inner_rows(normed_one, grad_projected)
    in_grad = jnp.concatenate([in_grad_raw[:, :width] * scale, in_grad_raw[:, width:]], axis=1)
    query_bias_grad = jnp.sum(grad_queries_low.astype(jnp.float32), axis=0) * scale
    value_bias_grad = jnp.sum(key_grads_low[:, width:].astype(jnp.float32), axis=0)
    grad_normed_one = times_transposed(
        grad_queries_low, in_full[:, :width]
    ) * scale + times_transposed(key_grads_low, in_full[:, width:])
    unused, first_back = jax.vjp(normalize, inputs, gain_first, shift_first)
    grad_inputs_norm, gain_one_grad, shift_one_grad = first_back(grad_normed_one)
    input_grad = (grad_middle + grad_inputs_norm).astype(jnp.bfloat16)[None]
    grads = (
        in_grad,
        query_bias_grad,
        value_bias_grad,
        out_grad,
        out_bias_grad,
        up_grad,
        up_bias_grad,
        down_grad,
        down_bias_grad,
        gain_one_grad,
        shift_one_grad,
        gain_two_grad,
        shift_two_grad,
    )
    summed = (
        lax.psum_scatter(grads[0], ("ctx", "fsdp"), scatter_dimension=0, tiled=True),
        lax.psum_scatter(grads[1], ("ctx", "fsdp"), scatter_dimension=0, tiled=True),
        lax.psum_scatter(grads[2], ("ctx", "fsdp"), scatter_dimension=0, tiled=True),
        lax.psum_scatter(grads[3], ("ctx", "fsdp"), scatter_dimension=0, tiled=True),
        lax.psum_scatter(grads[4], ("ctx", "fsdp"), scatter_dimension=0, tiled=True),
        lax.psum_scatter(grads[5], ("ctx", "fsdp"), scatter_dimension=0, tiled=True),
        lax.psum_scatter(grads[6], ("ctx", "fsdp"), scatter_dimension=0, tiled=True),
        lax.psum_scatter(grads[7], ("ctx", "fsdp"), scatter_dimension=0, tiled=True),
        lax.psum_scatter(grads[8], ("ctx", "fsdp"), scatter_dimension=0, tiled=True),
        lax.psum_scatter(grads[9], ("ctx", "fsdp"), scatter_dimension=0, tiled=True),
        lax.psum_scatter(grads[10], ("ctx", "fsdp"), scatter_dimension=0, tiled=True),
        lax.psum_scatter(grads[11], ("ctx", "fsdp"), scatter_dimension=0, tiled=True),
        lax.psum_scatter(grads[12], ("ctx", "fsdp"), scatter_dimension=0, tiled=True),
    )
    (
        in_weight_grad,
        query_bias_grad_out,
        value_bias_grad_out,
        out_weight_grad,
        out_bias_grad_out,
        up_weight_grad,
        up_bias_grad_out,
        down_weight_grad,
        down_bias_grad_out,
        first_gain_grad,
        first_shift_grad,
        second_gain_grad,
        second_shift_grad,
    ) = summed
    return (
        layer_out,
        input_grad,
        in_weight_grad,
        query_bias_grad_out,
        value_bias_grad_out,
        out_weight_grad,
        out_bias_grad_out,
        up_weight_grad,
        up_bias_grad_out,
        down_weight_grad,
        down_bias_grad_out,
        first_gain_grad,
        first_shift_grad,
        second_gain_grad,
        second_shift_grad,
    )


MESH_ID = pl.DeviceIdType.MESH
LOW = jnp.bfloat16
F32 = jnp.float32
T = 128


def dot(left, right):
    return jnp.dot(left, right, preferred_element_type=jnp.float32)


def dot_nt(left, right):
    return lax.dot_general(left, right, (((1,), (1,)), ((), ())), preferred_element_type=F32)


def dot_tn(left, right):
    return lax.dot_general(left, right, (((0,), (0,)), ((), ())), preferred_element_type=F32)


def turned(block):
    return block.astype(F32).T


def standard(values):
    center = values - jnp.mean(values, axis=1, keepdims=True)
    spread = lax.rsqrt(jnp.mean(center * center, axis=1, keepdims=True) + epsilon)
    return center * spread, spread


def standard_back(grad, gain, unit, spread):
    e = grad * gain
    return spread * (
        e - jnp.mean(e, axis=1, keepdims=True) - unit * jnp.mean(e * unit, axis=1, keepdims=True)
    )


def gelu_pair(hidden):
    phi = 0.5 * (1.0 + lax.erf(hidden * 0.7071067811865476))
    density = jnp.exp(hidden * hidden * -0.5) * 0.3989422804014327
    return hidden * phi, phi + hidden * density


def lanes(index, size):
    return pl.ds(pl.multiple_of(index * size, size), size)


def column_sum(values):
    return jnp.sum(values, axis=0, keepdims=True)


class Sems(NamedTuple):
    send: Any
    recv: Any


class Scratch(NamedTuple):
    vec: Any
    bias: Any
    key: Any
    query: Any
    in_full: Any
    out_full: Any
    up_full: Any
    down_full: Any
    normed_one: Any
    send_qkv: Any
    qkv_t: Any
    kv: Any
    scores: Any
    lse: Any
    delta: Any
    head_out: Any
    send_head: Any
    att_t: Any
    att_all: Any
    att: Any
    middle: Any
    grad_middle: Any
    cot_all: Any
    two_all: Any
    branch_all: Any
    acc_out: Any
    acc_grad: Any
    grad_hidden: Any
    early_grad: Any
    late_grad: Any
    dq: Any
    do_t: Any
    q_rows: Any
    do_rows: Any
    down_mine: Any
    down_theirs: Any
    down_pair: Any
    down_line: Any
    up_mine: Any
    up_theirs: Any
    up_pair: Any
    up_line: Any
    up_piece: Any
    out_mine: Any
    out_theirs: Any
    out_pair: Any
    out_line: Any
    dqkv: Any
    gp_t: Any
    in_mine: Any
    in_theirs: Any
    in_pair: Any
    in_send: Any
    in_recv: Any
    early_send: Any
    early_recv: Any
    late_send: Any
    late_recv: Any
    vec_mine: Any
    vec_pair: Any
    sem_load: Any
    sem_pair: Any
    sem_qkv: Any
    sem_one: Any
    sem_relay: Any
    sem_cot: Any
    sem_head: Any
    sem_att: Any
    sem_two: Any
    sem_back: Any
    sem_branch: Any
    sem_line: Any
    sem_grads: Any
    sem_up: Any
    sem_in: Any
    sem_early: Any
    sem_late: Any
    sem_dq: Any
    sem_in_w: Any
    sem_one_load: Any


def scratch():
    def v(shape, kind):
        return pltpu.VMEM(shape, kind)

    def sems(count):
        return Sems(pltpu.SemaphoreType.DMA((count,)), pltpu.SemaphoreType.DMA((count,)))

    return Scratch(
        vec=v((2, 12, 1, 512), F32),
        bias=v((2, 1, 1024), F32),
        key=v((2048, 128), F32),
        query=v((8, 2048), F32),
        in_full=v((1024, 3072), LOW),
        out_full=v((1024, 1024), LOW),
        up_full=v((1024, 4096), LOW),
        down_full=v((4096, 1024), LOW),
        normed_one=v((128, 1024), LOW),
        send_qkv=v((16, 192, 128), LOW),
        qkv_t=v((192, 2048), LOW),
        kv=v((2048, 128), LOW),
        scores=v((2048, 256), F32),
        lse=v((1, 2048), F32),
        delta=v((1, 2048), F32),
        head_out=v((64, 2048), F32),
        send_head=v((16, 64, 128), LOW),
        att_t=v((16, 64, 128), LOW),
        att_all=v((4, 4, 64, 128), LOW),
        att=v((128, 1024), LOW),
        middle=v((128, 1024), F32),
        grad_middle=v((128, 1024), F32),
        cot_all=v((4, 128, 1024), LOW),
        two_all=v((4, 128, 1024), LOW),
        branch_all=v((4, 128, 1024), LOW),
        acc_out=v((128, 1024), F32),
        acc_grad=v((128, 1024), F32),
        grad_hidden=v((512, 1024), LOW),
        early_grad=v((8, 1024), F32),
        late_grad=v((8, 1024), F32),
        dq=v((64, 2048), F32),
        do_t=v((64, 2048), LOW),
        q_rows=v((2048, 128), LOW),
        do_rows=v((2048, 128), LOW),
        down_mine=v((4, 128, 1024), F32),
        down_theirs=v((4, 128, 1024), LOW),
        down_pair=v((4, 128, 1024), LOW),
        down_line=v((3, 128, 1024), LOW),
        up_mine=v((4, 128, 1024), F32),
        up_theirs=v((4, 128, 1024), LOW),
        up_pair=v((4, 128, 1024), LOW),
        up_line=v((3, 128, 1024), LOW),
        up_piece=v((4, 32, 1024), F32),
        out_mine=v((4, 32, 1024), F32),
        out_theirs=v((4, 32, 1024), LOW),
        out_pair=v((4, 32, 1024), LOW),
        out_line=v((3, 32, 1024), LOW),
        dqkv=v((16, 192, 128), LOW),
        gp_t=v((3072, 128), LOW),
        in_mine=v((16, 48, 128), F32),
        in_theirs=v((16, 48, 128), LOW),
        in_pair=v((16, 48, 128), LOW),
        in_send=v((16, 48, 128), LOW),
        in_recv=v((16, 48, 128), LOW),
        early_send=v((8, 8, 128), F32),
        early_recv=v((16, 8, 128), F32),
        late_send=v((8, 8, 128), F32),
        late_recv=v((16, 8, 128), F32),
        vec_mine=v((24, 128), F32),
        vec_pair=v((24, 128), F32),
        sem_load=sems(6),
        sem_pair=sems(10),
        sem_qkv=sems(16),
        sem_one=sems(16),
        sem_relay=sems(12),
        sem_cot=sems(3),
        sem_head=sems(16),
        sem_att=sems(3),
        sem_two=sems(3),
        sem_back=sems(16),
        sem_branch=sems(3),
        sem_line=sems(9),
        sem_grads=sems(16),
        sem_up=sems(12),
        sem_in=sems(16),
        sem_early=sems(16),
        sem_late=sems(16),
        sem_dq=sems(16),
        sem_in_w=sems(12),
        sem_one_load=pltpu.SemaphoreType.DMA((16,)),
    )


def layer_kernel(
    tok_ref,
    cot_ref,
    place_ref,
    length_ref,
    *rest,
):
    vec_refs, rest = rest[:9], rest[9:]
    in_hbm, out_hbm, up_hbm, down_hbm = rest[:4]
    layer_out, input_grad, in_out, out_out, up_out, down_out, vec_out, one_hbm, s = rest[4:]
    n = 16
    scale = HD ** (-0.5)
    c, f = lax.axis_index("ctx"), lax.axis_index("fsdp")
    z, p = c // 4, c % 4
    y, x = p // 2, p % 2
    home = c - p
    sibling = (c, 1 - f)
    plane_places = [2 * y + 1 - x, 2 * (1 - y) + x, 2 * (1 - y) + 1 - x]
    planes = [(home + place, f) for place in plane_places]
    near = z + 1 - 2 * (z % 2)
    far = (z + 2) % 4
    first_core = f == 0

    def remote(src, dst, sems, i, j, device):
        return pltpu.make_async_remote_copy(
            src_ref=src,
            dst_ref=dst,
            send_sem=sems.send.at[i],
            recv_sem=sems.recv.at[j],
            device_id=device,
            device_id_type=MESH_ID,
        )

    def each_peer(step):
        def one(k, carry):
            step((c + k) % n)
            return carry

        lax.fori_loop(1, n, one, 0)

    def to_planes(src_of, dst, sems):
        copies = []
        for i in range(3):
            copy = remote(src_of(i), dst.at[1 + i], sems, i, i, planes[i])
            copy.start()
            copies.append(copy)
        return copies

    barrier = pltpu.get_barrier_semaphore()

    def greet(peer):
        pl.semaphore_signal(barrier, inc=1, device_id=(peer, f), device_id_type=MESH_ID)

    each_peer(greet)
    pl.semaphore_signal(barrier, inc=1, device_id=sibling, device_id_type=MESH_ID)
    for i in range(8):
        s.vec[f, i] = vec_refs[i][...].astype(F32).reshape(1, 512)
    for i in range(4):
        s.vec[f, 8 + i] = vec_refs[8][i * 512 : i * 512 + 512].astype(F32).reshape(1, 512)
    in_load = pltpu.make_async_copy(in_hbm, s.in_full.at[pl.ds(f * 512, 512)], s.sem_load.send.at[0])
    in_load.start()
    pl.semaphore_wait(barrier, n)
    vec_copy = remote(s.vec.at[f], s.vec.at[f], s.sem_pair, 4, 4, sibling)
    vec_copy.start()

    def in_copy_of(g, part):
        at = pl.ds(pl.multiple_of(part * 1024 + (z + g) % 4 * 256, 256), 256)
        return remote(
            in_hbm.at[:, at],
            s.in_full.at[pl.ds(f * 512, 512), at],
            s.sem_in_w,
            g * 3 + part,
            g * 3 + part,
            sibling,
        )

    for g in range(4):
        for part in range(3):
            in_copy_of(g, part).start()
    sent = [vec_copy]
    cot_copies = to_planes(lambda i: cot_ref, s.cot_all, s.sem_cot)
    sent += cot_copies

    weights = [
        (out_hbm, s.out_full, 512),
        (up_hbm, s.up_full, 512),
        (down_hbm, s.down_full, 2048),
    ]
    loads, pairs = [None], [None]
    for i, (src, dst, size) in enumerate(weights):
        load = pltpu.make_async_copy(src, dst.at[pl.ds(f * size, size)], s.sem_load.send.at[1 + i])
        loads.append(load)
        pair = remote(src, dst.at[pl.ds(f * size, size)], s.sem_pair, 1 + i, 1 + i, sibling)
        pairs.append(pair)
    sent += pairs[1:]

    def row(i):
        return jnp.concatenate([s.vec[0, i], s.vec[1, i]], axis=1)

    unit_one, unused = standard(tok_ref[...].astype(F32))
    s.cot_all[0] = cot_ref[...]
    vec_copy.wait_recv()
    s.normed_one[...] = (unit_one * row(4) + row(5)).astype(LOW)
    s.bias[0] = row(0)
    s.bias[1] = row(1)
    in_load.wait()

    def qkv_copy(dst):
        return remote(
            s.send_qkv.at[dst], s.qkv_t.at[:, lanes(c, T)], s.sem_qkv, dst, c, (dst, f)
        )

    def project(g, carry):
        group = (z + g) % 4
        for part in range(3):
            in_copy_of(g, part).wait_recv()
            at = pl.ds(pl.multiple_of(part * 1024 + group * 256, 256), 256)
            acc = dot(s.normed_one[...], s.in_full[:, at])
            if part == 0:
                acc = (acc + s.bias[0, :, lanes(group, 256)]) * scale
            if part == 2:
                acc = acc + s.bias[1, :, lanes(group, 256)]
            for u in range(2):
                block = acc[:, u * T : (u + 1) * T].T.astype(LOW)
                for w in range(2):
                    s.send_qkv[group * 4 + 2 * u + w, part * 64 : part * 64 + 64, :] = block[
                        w * 64 : w * 64 + 64
                    ]
        for u in range(4):
            dst = group * 4 + u

            @pl.when(dst != c)
            def _():
                qkv_copy(dst).start()

            @pl.when(dst == c)
            def _():
                s.qkv_t[:, lanes(c, T)] = s.send_qkv[dst]

        return carry

    lax.fori_loop(0, 4, project, 0)
    for i in range(1, 4):
        loads[i].start()
        pairs[i].start()
    keep = pltpu.make_async_copy(s.normed_one, one_hbm.at[c], s.sem_load.send.at[4])
    keep.start()

    place = place_ref[...]
    first, begun = jnp.zeros((1, 2048), jnp.int32), 0
    for i in range(length_ref.shape[1]):
        first = jnp.where(place >= begun, begun, first)
        begun = begun + length_ref[0, i]
    s.query[0:1] = place.astype(F32)
    s.query[1:2] = first.astype(F32)
    for i in range(n):
        at = slice(i * T, i * T + T)
        s.key[at] = jnp.broadcast_to(s.query[0:1, at], (T, T)).T

    def qkv_arrived(src):
        remote(
            s.send_qkv.at[src], s.qkv_t.at[:, lanes(src, T)], s.sem_qkv, src, src, (src, f)
        ).wait_recv()

    each_peer(qkv_arrived)

    def one_copy(slot, sems, i, device):
        return remote(one_hbm.at[slot], one_hbm.at[slot], Sems(sems.send, s.sem_one.recv), i, slot, device)

    keep.wait()
    far_slot = far * 4 + p
    one_far = one_copy(c, s.sem_one, 0, (far_slot, f))
    one_far.start()
    sent.append(one_far)

    def relay(k, slot):
        for i in range(3):
            copy = one_copy(slot, s.sem_relay, k * 3 + i, planes[i])
            copy.start()
            sent.append(copy)


    for i in range(n):
        at = slice(i * T, i * T + T)
        s.kv[at] = turned(s.qkv_t[64:192, at]).astype(LOW)
    nothing = jnp.zeros((64, 256), LOW)

    def seen(keys, at):
        place = jnp.concatenate([s.key[keys], s.key[keys]], axis=1)
        return (place >= s.query[1:2, at]) & (place <= s.query[0:1, at])

    def head_copy(dst):
        return remote(s.send_head.at[dst], s.att_t.at[p * 4 + z], s.sem_head, dst, c, (dst, f))

    def forward(i, carry):
        block = (c // 2 + i) % 8
        at = lanes(block, 256)
        query = jnp.concatenate([s.qkv_t[0:64, at], nothing], axis=0)
        top = jnp.full((8, 256), far_below, F32)
        for k in range(8):
            keys = slice(k * 256, k * 256 + 256)
            score = jnp.where(seen(keys, at), dot(s.kv[keys], query), far_below)
            s.scores[keys] = score
            top = jnp.maximum(top, jnp.max(score.reshape(32, 8, 256), axis=0))
        top = jnp.max(top, axis=0, keepdims=True)
        total = jnp.zeros((8, 256), F32)
        acc = jnp.zeros((64, 256), F32)
        for k in range(8):
            keys = slice(k * 256, k * 256 + 256)
            grown = jnp.exp(s.scores[keys] - top)
            total = total + jnp.sum(grown.reshape(32, 8, 256), axis=0)
            acc = acc + dot(s.qkv_t[128:192, keys], grown.astype(LOW))
        total = column_sum(total)
        s.lse[:, at] = top + jnp.log(total)
        result = acc / total
        s.head_out[:, at] = result
        for u in range(2):
            dst = block * 2 + u
            s.send_head[dst] = result[:, u * T : u * T + T].astype(LOW)

            @pl.when(dst != c)
            def _():
                head_copy(dst).start()

            @pl.when(dst == c)
            def _():
                s.att_t[p * 4 + z] = s.send_head[dst]

        return carry

    lax.fori_loop(0, 8, forward, 0)

    def head_arrived(src):
        slot = (src % 4) * 4 + src // 4
        remote(s.send_head.at[src], s.att_t.at[slot], s.sem_head, src, src, (src, f)).wait_recv()

    each_peer(head_arrived)

    def one_arrived(slot):
        one_copy(slot, s.sem_one, 0, (slot, f)).wait_recv()

    one_arrived(far_slot)
    near_device = (near * 4 + p, f)
    for i, slot in enumerate((c, far_slot)):
        copy = one_copy(slot, s.sem_one, 1 + i, near_device)
        copy.start()
        sent.append(copy)
    s.att_all[0] = s.att_t[pl.ds(p * 4, 4)]
    att_copies = to_planes(
        lambda i: s.att_t.at[pl.ds(plane_places[i] * 4, 4)], s.att_all, s.sem_att
    )
    sent += att_copies
    for i in range(8):
        slots = [(h % 4) * 4 + h // 4 for h in (2 * i, 2 * i + 1)]
        block = jnp.concatenate([s.att_t[slots[0]], s.att_t[slots[1]]], axis=0)
        s.att[:, i * T : i * T + T] = turned(block).astype(LOW)

    loads[1].wait()
    pairs[1].wait_recv()
    middle = tok_ref[...].astype(F32) + dot(s.att[...], s.out_full[...]) + row(2)
    s.middle[...] = middle
    unit_two, unused = standard(middle)
    s.two_all[0] = (unit_two * row(6) + row(7)).astype(LOW)
    two_copies = to_planes(lambda i: s.two_all.at[0], s.two_all, s.sem_two)
    sent += two_copies
    for i in (2, 3):
        loads[i].wait()
        pairs[i].wait_recv()
    s.acc_out[...] = jnp.zeros((T, 1024), F32)
    s.acc_grad[...] = jnp.zeros((T, 1024), F32)
    s.late_grad[...] = jnp.zeros((8, 1024), F32)

    def feed(j, carry):
        at = lanes(j, 512)
        hidden = dot(s.two_all[0], s.up_full[:, at]) + s.vec[j // 4, 8 + j % 4]
        active, slope = gelu_pair(hidden)
        grad_active = dot_nt(cot_ref[...], s.down_full[at, :])
        grad_hidden = (grad_active * slope).astype(LOW)
        s.acc_out[...] += dot(active.astype(LOW), s.down_full[at, :])
        s.acc_grad[...] += dot_nt(grad_hidden, s.up_full[:, at])
        summed = column_sum(grad_hidden.astype(F32))
        for q in range(4):
            s.early_grad[4 + q : 5 + q, lanes(j, T)] = summed[:, q * T : q * T + T]
        return carry

    lax.fori_loop(0, 8, feed, 0)
    layer_out[...] = (s.middle[...] + s.acc_out[...] + row(3)).astype(LOW)
    grad_result = cot_ref[...].astype(F32)
    s.early_grad[1:2] = column_sum(grad_result)
    unit_two, spread_two = standard(s.middle[...])
    grad_two = s.acc_grad[...]
    s.early_grad[2:3] = column_sum(grad_two * unit_two)
    s.early_grad[3:4] = column_sum(grad_two)
    grad_middle = grad_result + standard_back(grad_two, row(6), unit_two, spread_two)
    s.grad_middle[...] = grad_middle
    branch = grad_middle.astype(LOW)
    s.branch_all[0] = branch
    s.early_grad[0:1] = column_sum(branch.astype(F32))

    def head_done(dst):
        head_copy(dst).wait_send()

    each_peer(head_done)
    for i in range(4):
        at = slice(i * 256, i * 256 + 256)
        part = dot_nt(s.out_full[at, :], branch).astype(LOW)
        s.send_head[4 * i : 4 * i + 4] = part.reshape(4, 64, T)

    def back_copy(dst):
        return remote(s.send_head.at[dst], s.do_t.at[:, lanes(c, T)], s.sem_back, dst, c, (dst, f))

    each_peer(lambda dst: back_copy(dst).start())
    s.do_t[:, lanes(c, T)] = s.send_head[c]
    branch_copies = to_planes(lambda i: s.branch_all.at[0], s.branch_all, s.sem_branch)
    sent += branch_copies

    def to_owners(grad, send, recv, sems):
        def copy_to(dst):
            return remote(send.at[dst // 2], recv.at[c], sems, dst, c, (dst, f))

        for i in range(8):
            send[i] = grad[:, i * T : i * T + T]
        each_peer(lambda dst: copy_to(dst).start())
        recv[c] = send[c // 2]
        return copy_to

    def from_owners(send, recv, sems):
        each_peer(
            lambda src: remote(
                send.at[src // 2], recv.at[src], sems, src, src, (src, f)
            ).wait_recv()
        )
        return jnp.sum(recv[...], axis=0)

    near_slots = (near * 4 + p, (near + 2) % 4 * 4 + p)
    for slot in near_slots:
        one_arrived(slot)
    for k, slot in enumerate((c, far_slot) + near_slots):
        relay(k, slot)

    for i in range(3):
        cot_copies[i].wait_recv()
        two_copies[i].wait_recv()

    def plane_rows(ref):
        return ref[...].reshape(512, 1024)

    def strip(q, carry):
        at = pl.ds(pl.multiple_of(q * 1024 + p * 256, 256), 256)
        shift = s.vec[q // 2, 8 + (q % 2) * 2 + p // 2, :, lanes(p % 2, 256)]
        hidden = dot(plane_rows(s.two_all), s.up_full[:, at]) + shift
        active, slope = gelu_pair(hidden)
        grad_active = dot_nt(plane_rows(s.cot_all), s.down_full[at, :])
        s.grad_hidden[:, lanes(q, 256)] = (grad_active * slope).astype(LOW)
        part = dot_tn(active.astype(LOW), plane_rows(s.cot_all))
        s.down_mine[q] = jnp.where(first_core, part[:T], part[T:])
        s.down_theirs[q] = jnp.where(first_core, part[T:], part[:T]).astype(LOW)
        return carry

    lax.fori_loop(0, 4, strip, 0)
    down_pair = remote(s.down_theirs, s.down_pair, s.sem_pair, 5, 5, sibling)
    down_pair.start()

    def split_rows(part):
        parts = part.reshape(4, 2, 32, 1024)
        mine = jnp.where(first_core, parts[:, 0], parts[:, 1])
        theirs = jnp.where(first_core, parts[:, 1], parts[:, 0])
        return mine, theirs.astype(LOW)

    def up_rows(q, carry):
        left = s.two_all[:, :, lanes(q, 256)].reshape(512, 256)
        mine, theirs = split_rows(dot_tn(left, s.grad_hidden[...]))
        s.up_mine[q] = mine.reshape(T, 1024)
        s.up_theirs[q] = theirs.reshape(T, 1024)
        return carry

    lax.fori_loop(0, 4, up_rows, 0)
    up_pair = remote(s.up_theirs, s.up_pair, s.sem_pair, 6, 6, sibling)
    up_pair.start()

    def to_near(mine, theirs, pair, line, base):
        copies = []
        for j in range(2):
            at = (near + 2 * j) % 4
            theirs[at] = (mine[at] + pair[at].astype(F32)).astype(LOW)
            copy = remote(
                theirs.at[at], line.at[j], s.sem_line, base + j, base + j, (near * 4 + p, f)
            )
            copy.start()
            copies.append(copy)
        for at in (z, far):
            mine[at] += pair[at].astype(F32)
        return copies

    def to_far(mine, theirs, line, base, copies):
        for copy in copies:
            copy.wait_recv()
        mine[z] += line[0].astype(F32)
        theirs[far] = (mine[far] + line[1].astype(F32)).astype(LOW)
        copy = remote(
            theirs.at[far], line.at[2], s.sem_line, base + 2, base + 2, (far_slot, f)
        )
        copy.start()
        return copies + [copy]

    down_pair.wait()
    down_line = to_near(s.down_mine, s.down_theirs, s.down_pair, s.down_line, 0)
    up_pair.wait()
    up_line = to_near(s.up_mine, s.up_theirs, s.up_pair, s.up_line, 3)
    early_to = to_owners(s.early_grad, s.early_send, s.early_recv, s.sem_early)

    def qkv_done(dst):
        qkv_copy(dst).wait_send()

    each_peer(qkv_done)

    def back_arrived(src):
        remote(
            s.send_head.at[src], s.do_t.at[:, lanes(src, T)], s.sem_back, src, src, (src, f)
        ).wait_recv()

    each_peer(back_arrived)
    small_nothing = jnp.zeros((64, T), LOW)
    for i in range(n):
        at = slice(i * T, i * T + T)
        s.q_rows[at] = turned(
            jnp.concatenate([s.qkv_t[0:64, at], small_nothing], axis=0)
        ).astype(LOW)
        s.do_rows[at] = turned(
            jnp.concatenate([small_nothing, s.do_t[:, at]], axis=0)
        ).astype(LOW)
    s.delta[...] = column_sum(s.do_t[...].astype(F32) * s.head_out[...])
    s.dq[...] = jnp.zeros((64, 2048), F32)

    def grads_copy(dst):
        return remote(
            s.send_qkv.at[dst, pl.ds(64, 128)],
            s.dqkv.at[c, pl.ds(64, 128)],
            s.sem_grads,
            dst,
            c,
            (dst, f),
        )

    def dq_copy(dst):
        return remote(
            s.send_qkv.at[dst, pl.ds(0, 64)],
            s.dqkv.at[c, pl.ds(0, 64)],
            s.sem_dq,
            dst,
            c,
            (dst, f),
        )

    def backward(i, carry):
        block = (c // 2 + i) % 8
        keys = pl.ds(pl.multiple_of(block * 256, 256), 256)
        key_t = s.qkv_t[64:128, keys]
        both = s.kv[keys]
        dkv = jnp.zeros((256, 128), F32)
        for q in range(8):
            at = slice(q * 256, q * 256 + 256)
            query = jnp.concatenate([s.qkv_t[0:64, at], nothing], axis=0)
            grad = jnp.concatenate([nothing, s.do_t[:, at]], axis=0)
            score = dot(both, query)
            prob = jnp.where(seen(keys, at), jnp.exp(score - s.lse[:, at]), 0.0)
            grad_prob = dot(both, grad)
            grad_score = (prob * (grad_prob - s.delta[:, at])).astype(LOW)
            dkv = dkv + (
                dot(grad_score, s.q_rows[at]) + dot(prob.astype(LOW), s.do_rows[at])
            )
            s.dq[:, at] += dot(key_t, grad_score)
        for u in range(2):
            dst = block * 2 + u
            s.send_qkv[dst, 64:192] = dkv[u * T : u * T + T].T.astype(LOW)

            @pl.when(dst != c)
            def _():
                grads_copy(dst).start()

        return carry

    lax.fori_loop(0, 4, backward, 0)
    down_line = to_far(s.down_mine, s.down_theirs, s.down_line, 0, down_line)
    lax.fori_loop(4, 8, backward, 0)
    for i in range(n):
        s.send_qkv[i, 0:64] = s.dq[:, i * T : i * T + T].astype(LOW)
    each_peer(lambda dst: dq_copy(dst).start())
    s.dqkv[c] = s.send_qkv[c]
    up_line = to_far(s.up_mine, s.up_theirs, s.up_line, 3, up_line)
    for i in range(3):
        att_copies[i].wait_recv()
        branch_copies[i].wait_recv()
    part = jnp.zeros((256, 1024), F32)
    for i in range(4):
        part = part + dot(s.att_all[i].reshape(256, T), s.branch_all[i])
    mine, theirs = split_rows(part)
    s.out_mine[...] = mine
    s.out_theirs[...] = theirs
    out_pair = remote(s.out_theirs, s.out_pair, s.sem_pair, 7, 7, sibling)
    out_pair.start()
    out_pair.wait()
    out_line = to_near(s.out_mine, s.out_theirs, s.out_pair, s.out_line, 6)

    for k in range(4):
        for i in range(3):
            one_arrived((z + k) % 4 * 4 + plane_places[i])
    one_loads = []
    for i in range(n):
        load = pltpu.make_async_copy(
            one_hbm.at[i], s.down_full.at[pl.ds(i * T, T)], s.sem_one_load.at[i]
        )
        load.start()
        one_loads.append(load)
    for load in one_loads:
        load.wait()
    head_grad = jnp.concatenate([s.send_qkv[i] for i in range(n)], axis=1)
    bias_sums = dot_nt(jnp.ones((8, 2048), LOW), head_grad)
    s.vec_mine[16:24] = jnp.concatenate([bias_sums[:, 0:64] * scale, bias_sums[:, 128:192]], axis=1)

    def packed(rows):
        tail = jnp.concatenate([rows[:, 0:16, 128:192], rows[:, 16:32, 128:192]], axis=2)
        return jnp.concatenate([rows[:, :, 0:128], tail], axis=1)

    for i in range(4):
        part = dot(head_grad, s.down_full[0:2048, i * 256 : i * 256 + 256])
        part = jnp.concatenate(
            [part[0:64] * scale, part[64:192], jnp.zeros((64, 256), F32)], axis=0
        )
        for u in range(2):
            parts = part[:, u * T : u * T + T].T.reshape(2, 2, 32, 256)
            at = slice(4 * i + 2 * u, 4 * i + 2 * u + 2)
            s.in_mine[at] = packed(jnp.where(first_core, parts[:, 0], parts[:, 1]))
            s.in_theirs[at] = packed(jnp.where(first_core, parts[:, 1], parts[:, 0])).astype(LOW)
    in_pair = remote(s.in_theirs, s.in_pair, s.sem_pair, 8, 8, sibling)
    in_pair.start()

    def grads_arrived(src):
        remote(
            s.send_qkv.at[src, pl.ds(64, 128)],
            s.dqkv.at[src, pl.ds(64, 128)],
            s.sem_grads,
            src,
            src,
            (src, f),
        ).wait_recv()

    def dq_arrived(src):
        remote(
            s.send_qkv.at[src, pl.ds(0, 64)],
            s.dqkv.at[src, pl.ds(0, 64)],
            s.sem_dq,
            src,
            src,
            (src, f),
        ).wait_recv()

    in_pair.wait()
    s.in_send[...] = (s.in_mine[...] + s.in_pair[...].astype(F32)).astype(LOW)

    def in_copy(dst):
        return remote(s.in_send.at[dst], s.in_recv.at[c], s.sem_in, dst, c, (dst, f))

    each_peer(lambda dst: in_copy(dst).start())
    s.in_recv[c] = s.in_send[c]
    each_peer(grads_arrived)
    for h in range(n):
        s.gp_t[1024 + h * 64 : 1088 + h * 64] = s.dqkv[h, 64:128]
        s.gp_t[2048 + h * 64 : 2112 + h * 64] = s.dqkv[h, 128:192]
    for i in range(4):
        at = slice(i * 256, i * 256 + 256)
        s.acc_grad[:, at] = dot(s.in_full[at, 1024:3072], s.gp_t[1024:3072]).T
    each_peer(dq_arrived)
    for h in range(n):
        s.gp_t[h * 64 : h * 64 + 64] = s.dqkv[h, 0:64] * jnp.asarray(scale, LOW)
    for i in range(4):
        at = slice(i * 256, i * 256 + 256)
        s.acc_grad[:, at] += dot(s.in_full[at, 0:1024], s.gp_t[0:1024]).T
    unit_one, spread_one = standard(tok_ref[...].astype(F32))
    grad_one = s.acc_grad[...]
    s.late_grad[0:1] = column_sum(grad_one * unit_one)
    s.late_grad[1:2] = column_sum(grad_one)
    late_to = to_owners(s.late_grad, s.late_send, s.late_recv, s.sem_late)
    input_grad[...] = (
        s.grad_middle[...] + standard_back(grad_one, row(4), unit_one, spread_one)
    ).astype(LOW)

    out_line = to_far(s.out_mine, s.out_theirs, s.out_line, 6, out_line)
    up_line[2].wait_recv()
    up_sum = s.up_mine[z] + s.up_line[2].astype(F32)
    s.up_piece[...] = up_sum.reshape(4, 32, 1024)
    up_copies = []
    for i in range(3):
        for q in range(4):
            copy = remote(
                s.up_piece.at[plane_places[i], :, pl.ds(q * 256, 256)],
                up_out.at[:, pl.ds(pl.multiple_of(q * 1024 + p * 256, 256), 256)],
                s.sem_up,
                i * 4 + q,
                i * 4 + q,
                planes[i],
            )
            copy.start()
            up_copies.append(copy)
    for q in range(4):
        up_out[:, pl.ds(pl.multiple_of(q * 1024 + p * 256, 256), 256)] = s.up_piece[
            p, :, q * 256 : q * 256 + 256
        ]
    down_line[2].wait_recv()
    down_out[...] = s.down_mine[z] + s.down_line[2].astype(F32)
    out_line[2].wait_recv()
    out_out[...] = s.out_mine[z] + s.out_line[2].astype(F32)

    s.vec_mine[0:8] = from_owners(s.early_send, s.early_recv, s.sem_early)
    s.vec_mine[8:16] = from_owners(s.late_send, s.late_recv, s.sem_late)
    vec_pair = remote(s.vec_mine, s.vec_pair, s.sem_pair, 9, 9, sibling)
    vec_pair.start()

    def in_arrived(src):
        remote(s.in_send.at[src], s.in_recv.at[src], s.sem_in, src, src, (src, f)).wait_recv()

    each_peer(in_arrived)
    for i in range(8):
        a, b = s.in_recv[2 * i].astype(F32), s.in_recv[2 * i + 1].astype(F32)
        at = i * T
        in_out[:, at : at + T] = jnp.concatenate([a[0:32, 0:64], b[0:32, 0:64]], axis=1)
        at = 1024 + i * T
        in_out[:, at : at + T] = jnp.concatenate([a[0:32, 64:T], b[0:32, 64:T]], axis=1)
        at = 2048 + i * T
        in_out[0:16, at : at + T] = jnp.concatenate([a[32:48, 0:64], b[32:48, 0:64]], axis=1)
        in_out[16:32, at : at + T] = jnp.concatenate([a[32:48, 64:T], b[32:48, 64:T]], axis=1)
    vec_pair.wait()
    total = s.vec_mine[...] + s.vec_pair[...]
    place = (c * 2 + f) % 4
    picked, up_row = total[0:16, 0:32], total[4:5]
    for i in range(1, 4):
        picked = jnp.where(place == i, total[0:16, 32 * i : 32 * i + 32], picked)
        up_row = jnp.where(place == i, total[4 + i : 5 + i], up_row)
    vec_out[0:16, 0:32] = picked
    vec_out[16:24, 0:32] = jnp.where(first_core, total[16:24, 0:32], total[16:24, 32:64])
    vec_out[24:32, 0:32] = jnp.where(first_core, total[16:24, 64:96], total[16:24, 96:128])
    vec_out[32:40] = jnp.broadcast_to(up_row, (8, T))
    for copy in up_copies:
        copy.wait()
    for g in range(4):
        for part in range(3):
            in_copy_of(g, part).wait_send()
    sent += [copy for line in (down_line, up_line, out_line) for copy in line]
    for copy in sent:
        copy.wait_send()

    def all_sent(dst):
        back_copy(dst).wait_send()
        grads_copy(dst).wait_send()
        dq_copy(dst).wait_send()
        in_copy(dst).wait_send()
        early_to(dst).wait_send()
        late_to(dst).wait_send()

    each_peer(all_sent)


def finish_kernel(*refs):
    vec = refs[6]
    for src, dst in zip(refs[:6], refs[7:13]):
        dst[...] = src[...]
    for i, dst in zip((16, 24, 0, 1, 8, 9, 2, 3), refs[13:21]):
        dst[...] = vec[i : i + 1, 0:32].reshape(32)
    refs[21][...] = vec[32:33].reshape(T)


def body_fused(
    tokens,
    in_weight,
    query_bias,
    value_bias,
    out_weight,
    out_bias,
    up_weight,
    up_bias,
    down_weight,
    down_bias,
    first_gain,
    first_shift,
    second_gain,
    second_shift,
    lengths,
    slot_places,
    cotangent,
):
    vectors = (
        query_bias,
        value_bias,
        out_bias,
        down_bias,
        first_gain,
        first_shift,
        second_gain,
        second_shift,
        up_bias,
    )
    hbm = pl.BlockSpec(memory_space=pl.ANY)
    vmem = pl.BlockSpec(memory_space=pltpu.VMEM)
    outs = pl.pallas_call(
        layer_kernel,
        out_shape=(
            jax.ShapeDtypeStruct((T, 1024), LOW),
            jax.ShapeDtypeStruct((T, 1024), LOW),
            jax.ShapeDtypeStruct((32, 3072), F32),
            jax.ShapeDtypeStruct((32, 1024), F32),
            jax.ShapeDtypeStruct((32, 4096), F32),
            jax.ShapeDtypeStruct((128, 1024), F32),
            jax.ShapeDtypeStruct((40, 128), F32),
            jax.ShapeDtypeStruct((16, T, 1024), LOW),
        ),
        in_specs=[vmem] * 3 + [pl.BlockSpec(memory_space=pltpu.SMEM)] + [vmem] * 9 + [hbm] * 4,
        out_specs=(vmem,) * 7 + (hbm,),
        scratch_shapes=[scratch()],
        compiler_params=pltpu.CompilerParams(
            collective_id=0, has_side_effects=True, vmem_limit_bytes=60 * 2**20
        ),
        cost_estimate=pl.CostEstimate(
            flops=16 * 10**9, bytes_accessed=40 * 2**20, transcendentals=10**7
        ),
    )(
        tokens[0],
        cotangent[0],
        slot_places,
        lengths,
        *vectors,
        in_weight,
        out_weight,
        up_weight,
        down_weight,
    )
    small = [jax.ShapeDtypeStruct((32,), F32)] * 8 + [jax.ShapeDtypeStruct((T,), F32)]
    outs = pl.pallas_call(
        finish_kernel,
        out_shape=[jax.ShapeDtypeStruct(one.shape, one.dtype) for one in outs[:6]] + small,
        in_specs=[vmem] * 7,
        out_specs=[vmem] * 15,
    )(*outs[:7])
    layer_out, input_grad, in_grad, out_grad, up_grad, down_grad = outs[:6]
    query_sum, value_sum, out_sum, down_sum = outs[6:10]
    gain_one, shift_one, gain_two, shift_two, up_sum = outs[10:]
    return (
        layer_out[None],
        input_grad[None],
        in_grad,
        query_sum,
        value_sum,
        out_grad,
        out_sum,
        up_grad,
        up_sum,
        down_grad,
        down_sum,
        gain_one,
        shift_one,
        gain_two,
        shift_two,
    )


def solution(mesh):
    placed = (
        P("fsdp", "ctx", None),
        P("fsdp", None),
        P("fsdp"),
        P("fsdp"),
        P("fsdp", None),
        P("fsdp"),
        P("fsdp", None),
        P("fsdp"),
        P("fsdp", None),
        P("fsdp"),
        P("fsdp"),
        P("fsdp"),
        P("fsdp"),
        P("fsdp"),
        P("fsdp", None),
        P("fsdp", None),
        P("fsdp", "ctx", None),
    )
    return jax.shard_map(
        body_fused if mesh.shape["ctx"] == H else body_general,
        mesh=mesh,
        in_specs=placed,
        out_specs=(
            P("fsdp", "ctx", None),
            P("fsdp", "ctx", None),
            P(("ctx", "fsdp"), None),
            P(("ctx", "fsdp")),
            P(("ctx", "fsdp")),
            P(("ctx", "fsdp"), None),
            P(("ctx", "fsdp")),
            P(("ctx", "fsdp"), None),
            P(("ctx", "fsdp")),
            P(("ctx", "fsdp"), None),
            P(("ctx", "fsdp")),
            P(("ctx", "fsdp")),
            P(("ctx", "fsdp")),
            P(("ctx", "fsdp")),
            P(("ctx", "fsdp")),
        ),
        check_vma=False,
    )
```

```python
import jax
import jax.numpy as jnp
from jax import lax
from typing import Any, NamedTuple
from jax.experimental import pallas as pl
from jax.experimental.pallas import tpu as pltpu
from jax.sharding import PartitionSpec as P

H = 16
HD = 64


epsilon = 1e-05
far_below = -1e30


def normalize(values, gain, shift):
    center = values - jnp.mean(values, axis=-1, keepdims=True)
    spread = jnp.mean(center * center, axis=-1, keepdims=True)
    return center * lax.rsqrt(spread + epsilon) * gain + shift


def gelu_exact(values):
    return jax.nn.gelu(values, approximate=False)


def block_size(total):
    for size in range(min(2048, total), 0, -1):
        if total % size == 0:
            return size
    return total


def segment_of(places, starts):
    return jnp.sum((starts[None, :] <= places[:, None]).astype(jnp.int32), axis=1) - 1


def visible(query_place, query_segment, key_place, key_segment):
    return (key_segment[None, :] == query_segment[:, None]) & (
        key_place[None, :] <= query_place[:, None]
    )


def scores_of(queries, key_rows, allowed):
    scores = jnp.einsum("qhd,khd->hqk", queries, key_rows, preferred_element_type=jnp.float32)
    return jnp.where(allowed[None], scores, far_below)


def inner_rows(left, right):
    return jnp.einsum("tf,tg->fg", left, right, preferred_element_type=jnp.float32)


def times_transposed(left, right):
    return jnp.einsum("tg,fg->tf", left, right, preferred_element_type=jnp.float32)


def key_terms(probs_low, grad_scores, query_rows, grad_rows, size, width):
    grad_keys = jnp.einsum(
        "hqk,qhd->khd", grad_scores, query_rows, preferred_element_type=jnp.float32
    )
    grad_values = jnp.einsum(
        "hqk,qhd->khd", probs_low, grad_rows, preferred_element_type=jnp.float32
    )
    return jnp.concatenate(
        [grad_keys.reshape(size, width), grad_values.reshape(size, width)], axis=1
    )


def body_general(
    tokens,
    in_weight,
    query_bias,
    value_bias,
    out_weight,
    out_bias,
    up_weight,
    up_bias,
    down_weight,
    down_bias,
    first_gain,
    first_shift,
    second_gain,
    second_shift,
    lengths,
    slot_places,
    cotangent,
):
    gathered_params = (
        lax.all_gather(in_weight, "fsdp", axis=0, tiled=True),
        lax.all_gather(query_bias, "fsdp", axis=0, tiled=True),
        lax.all_gather(value_bias, "fsdp", axis=0, tiled=True),
        lax.all_gather(out_weight, "fsdp", axis=0, tiled=True),
        lax.all_gather(out_bias, "fsdp", axis=0, tiled=True),
        lax.all_gather(up_weight, "fsdp", axis=0, tiled=True),
        lax.all_gather(up_bias, "fsdp", axis=0, tiled=True),
        lax.all_gather(down_weight, "fsdp", axis=0, tiled=True),
        lax.all_gather(down_bias, "fsdp", axis=0, tiled=True),
        lax.all_gather(first_gain, "fsdp", axis=0, tiled=True),
        lax.all_gather(first_shift, "fsdp", axis=0, tiled=True),
        lax.all_gather(second_gain, "fsdp", axis=0, tiled=True),
        lax.all_gather(second_shift, "fsdp", axis=0, tiled=True),
    )
    (
        in_full,
        query_shift,
        value_shift,
        out_full,
        out_shift,
        up_full,
        up_shift,
        down_full,
        down_shift,
        gain_first,
        shift_first,
        gain_second,
        shift_second,
    ) = gathered_params
    query_shift = query_shift.astype(jnp.float32)
    value_shift = value_shift.astype(jnp.float32)
    out_shift = out_shift.astype(jnp.float32)
    up_shift = up_shift.astype(jnp.float32)
    down_shift = down_shift.astype(jnp.float32)
    gain_first = gain_first.astype(jnp.float32)
    shift_first = shift_first.astype(jnp.float32)
    gain_second = gain_second.astype(jnp.float32)
    shift_second = shift_second.astype(jnp.float32)
    inputs = tokens[0].astype(jnp.float32)
    rows = inputs.shape[0]
    width = inputs.shape[1]
    scale = HD ** (-0.5)
    places = slot_places[0]
    seq_lengths = lengths[0]
    starts = jnp.cumsum(seq_lengths) - seq_lengths
    key_segments = segment_of(places, starts)
    first_slot = lax.axis_index("ctx") * rows
    query_places = lax.dynamic_slice_in_dim(places, first_slot, rows)
    query_segments = lax.dynamic_slice_in_dim(key_segments, first_slot, rows)
    total_keys = places.shape[0]
    key_step = block_size(total_keys)
    block_count = total_keys // key_step
    place_blocks = places.reshape(block_count, key_step)
    segment_blocks = key_segments.reshape(block_count, key_step)
    normed_one = normalize(inputs, gain_first, shift_first).astype(jnp.bfloat16)
    projected = jnp.dot(normed_one, in_full, preferred_element_type=jnp.float32)
    queries = (
        ((projected[:, :width] + query_shift) * scale).astype(jnp.bfloat16).reshape(rows, H, HD)
    )
    key_value = jnp.concatenate(
        [projected[:, width : 2 * width], projected[:, 2 * width :] + value_shift], axis=1
    ).astype(jnp.bfloat16)
    gathered = lax.all_gather(key_value, "ctx", axis=0, tiled=True)
    pair_blocks = gathered.reshape(block_count, key_step, 2 * width)

    def split_pair(pair, size):
        return (pair[:, :width].reshape(size, H, HD), pair[:, width:].reshape(size, H, HD))

    def max_step(carry, block):
        top, total = carry
        pair, key_place, key_segment = block
        key_rows, value_rows = split_pair(pair, key_step)
        allowed = visible(query_places, query_segments, key_place, key_segment)
        scores = scores_of(queries, key_rows, allowed)
        new_top = jnp.maximum(top, jnp.max(scores, axis=2))
        expand = jnp.where(allowed[None], jnp.exp(scores - new_top[:, :, None]), 0.0)
        total = total * jnp.exp(top - new_top) + jnp.sum(expand, axis=2)
        return ((new_top, total), None)

    start_top = jnp.full((H, rows), far_below, jnp.float32)
    (top, total), unused = lax.scan(
        max_step,
        (start_top, jnp.zeros((H, rows), jnp.float32)),
        (pair_blocks, place_blocks, segment_blocks),
    )
    log_total = top + jnp.log(total)

    def value_step(summed, block):
        pair, key_place, key_segment = block
        key_rows, value_rows = split_pair(pair, key_step)
        allowed = visible(query_places, query_segments, key_place, key_segment)
        scores = scores_of(queries, key_rows, allowed)
        weights = jnp.where(allowed[None], jnp.exp(scores - log_total[:, :, None]), 0.0).astype(
            jnp.bfloat16
        )
        summed = summed + jnp.einsum(
            "hqk,khd->qhd", weights, value_rows, preferred_element_type=jnp.float32
        )
        return (summed, None)

    heads_out, unused = lax.scan(
        value_step,
        jnp.zeros((rows, H, HD), jnp.float32),
        (pair_blocks, place_blocks, segment_blocks),
    )
    attended = heads_out.reshape(rows, width).astype(jnp.bfloat16)
    middle = inputs + jnp.dot(attended, out_full, preferred_element_type=jnp.float32) + out_shift
    normed_two = normalize(middle, gain_second, shift_second).astype(jnp.bfloat16)
    hidden = jnp.dot(normed_two, up_full, preferred_element_type=jnp.float32) + up_shift
    active_full, gelu_back = jax.vjp(gelu_exact, hidden)
    active = active_full.astype(jnp.bfloat16)
    result = middle + jnp.dot(active, down_full, preferred_element_type=jnp.float32) + down_shift
    layer_out = result.astype(jnp.bfloat16)[None]
    grad_low = cotangent[0]
    grad_result = grad_low.astype(jnp.float32)
    down_grad = inner_rows(active, grad_low)
    down_bias_grad = jnp.sum(grad_result, axis=0)
    grad_active = times_transposed(grad_low, down_full)
    grad_hidden = gelu_back(grad_active)[0].astype(jnp.bfloat16)
    up_grad = inner_rows(normed_two, grad_hidden)
    up_bias_grad = jnp.sum(grad_hidden.astype(jnp.float32), axis=0)
    grad_normed_two = times_transposed(grad_hidden, up_full)
    unused, second_back = jax.vjp(normalize, middle, gain_second, shift_second)
    grad_middle_norm, gain_two_grad, shift_two_grad = second_back(grad_normed_two)
    grad_middle = grad_result + grad_middle_norm
    grad_branch = grad_middle.astype(jnp.bfloat16)
    out_grad = inner_rows(attended, grad_branch)
    out_bias_grad = jnp.sum(grad_branch.astype(jnp.float32), axis=0)
    grad_attended = (
        times_transposed(grad_branch, out_full).astype(jnp.bfloat16).reshape(rows, H, HD)
    )
    deltas = jnp.sum(grad_attended.astype(jnp.float32) * heads_out, axis=2).T

    def block_back(key_rows, value_rows, allowed):
        scores = scores_of(queries, key_rows, allowed)
        probs = jnp.where(allowed[None], jnp.exp(scores - log_total[:, :, None]), 0.0)
        grad_probs = jnp.einsum(
            "qhd,khd->hqk", grad_attended, value_rows, preferred_element_type=jnp.float32
        )
        grad_scores = (probs * (grad_probs - deltas[:, :, None])).astype(jnp.bfloat16)
        return (probs.astype(jnp.bfloat16), grad_scores)

    def query_term(grad_scores, key_rows):
        return jnp.einsum("hqk,khd->qhd", grad_scores, key_rows, preferred_element_type=jnp.float32)

    def whole_step(grad_queries, block):
        pair, key_place, key_segment = block
        key_rows, value_rows = split_pair(pair, key_step)
        allowed = visible(query_places, query_segments, key_place, key_segment)
        probs_low, grad_scores = block_back(key_rows, value_rows, allowed)
        grad_queries = grad_queries + query_term(grad_scores, key_rows)
        return (
            grad_queries,
            key_terms(probs_low, grad_scores, queries, grad_attended, key_step, width),
        )

    grad_queries, terms = lax.scan(
        whole_step,
        jnp.zeros((rows, H, HD), jnp.float32),
        (pair_blocks, place_blocks, segment_blocks),
    )
    key_grads = lax.psum_scatter(
        terms.reshape(total_keys, 2 * width), "ctx", scatter_dimension=0, tiled=True
    )
    key_grads_low = key_grads.astype(jnp.bfloat16)
    grad_queries_low = grad_queries.reshape(rows, width).astype(jnp.bfloat16)
    grad_projected = jnp.concatenate([grad_queries_low, key_grads_low], axis=1)
    in_grad_raw = inner_rows(normed_one, grad_projected)
    in_grad = jnp.concatenate([in_grad_raw[:, :width] * scale, in_grad_raw[:, width:]], axis=1)
    query_bias_grad = jnp.sum(grad_queries_low.astype(jnp.float32), axis=0) * scale
    value_bias_grad = jnp.sum(key_grads_low[:, width:].astype(jnp.float32), axis=0)
    grad_normed_one = times_transposed(
        grad_queries_low, in_full[:, :width]
    ) * scale + times_transposed(key_grads_low, in_full[:, width:])
    unused, first_back = jax.vjp(normalize, inputs, gain_first, shift_first)
    grad_inputs_norm, gain_one_grad, shift_one_grad = first_back(grad_normed_one)
    input_grad = (grad_middle + grad_inputs_norm).astype(jnp.bfloat16)[None]
    grads = (
        in_grad,
        query_bias_grad,
        value_bias_grad,
        out_grad,
        out_bias_grad,
        up_grad,
        up_bias_grad,
        down_grad,
        down_bias_grad,
        gain_one_grad,
        shift_one_grad,
        gain_two_grad,
        shift_two_grad,
    )
    summed = (
        lax.psum_scatter(grads[0], ("ctx", "fsdp"), scatter_dimension=0, tiled=True),
        lax.psum_scatter(grads[1], ("ctx", "fsdp"), scatter_dimension=0, tiled=True),
        lax.psum_scatter(grads[2], ("ctx", "fsdp"), scatter_dimension=0, tiled=True),
        lax.psum_scatter(grads[3], ("ctx", "fsdp"), scatter_dimension=0, tiled=True),
        lax.psum_scatter(grads[4], ("ctx", "fsdp"), scatter_dimension=0, tiled=True),
        lax.psum_scatter(grads[5], ("ctx", "fsdp"), scatter_dimension=0, tiled=True),
        lax.psum_scatter(grads[6], ("ctx", "fsdp"), scatter_dimension=0, tiled=True),
        lax.psum_scatter(grads[7], ("ctx", "fsdp"), scatter_dimension=0, tiled=True),
        lax.psum_scatter(grads[8], ("ctx", "fsdp"), scatter_dimension=0, tiled=True),
        lax.psum_scatter(grads[9], ("ctx", "fsdp"), scatter_dimension=0, tiled=True),
        lax.psum_scatter(grads[10], ("ctx", "fsdp"), scatter_dimension=0, tiled=True),
        lax.psum_scatter(grads[11], ("ctx", "fsdp"), scatter_dimension=0, tiled=True),
        lax.psum_scatter(grads[12], ("ctx", "fsdp"), scatter_dimension=0, tiled=True),
    )
    (
        in_weight_grad,
        query_bias_grad_out,
        value_bias_grad_out,
        out_weight_grad,
        out_bias_grad_out,
        up_weight_grad,
        up_bias_grad_out,
        down_weight_grad,
        down_bias_grad_out,
        first_gain_grad,
        first_shift_grad,
        second_gain_grad,
        second_shift_grad,
    ) = summed
    return (
        layer_out,
        input_grad,
        in_weight_grad,
        query_bias_grad_out,
        value_bias_grad_out,
        out_weight_grad,
        out_bias_grad_out,
        up_weight_grad,
        up_bias_grad_out,
        down_weight_grad,
        down_bias_grad_out,
        first_gain_grad,
        first_shift_grad,
        second_gain_grad,
        second_shift_grad,
    )


MESH_ID = pl.DeviceIdType.MESH
LOW = jnp.bfloat16
F32 = jnp.float32
T = 128


def dot(left, right):
    return jnp.dot(left, right, preferred_element_type=jnp.float32)


def dot_nt(left, right):
    return lax.dot_general(left, right, (((1,), (1,)), ((), ())), preferred_element_type=F32)


def dot_tn(left, right):
    return lax.dot_general(left, right, (((0,), (0,)), ((), ())), preferred_element_type=F32)


def turned(block):
    return block.astype(F32).T


def standard(values):
    center = values - jnp.mean(values, axis=1, keepdims=True)
    spread = lax.rsqrt(jnp.mean(center * center, axis=1, keepdims=True) + epsilon)
    return center * spread, spread


def standard_back(grad, gain, unit, spread):
    e = grad * gain
    return spread * (
        e - jnp.mean(e, axis=1, keepdims=True) - unit * jnp.mean(e * unit, axis=1, keepdims=True)
    )


def gelu_pair(hidden):
    phi = 0.5 * (1.0 + lax.erf(hidden * 0.7071067811865476))
    density = jnp.exp(hidden * hidden * -0.5) * 0.3989422804014327
    return hidden * phi, phi + hidden * density


def lanes(index, size):
    return pl.ds(pl.multiple_of(index * size, size), size)


def column_sum(values):
    return jnp.sum(values, axis=0, keepdims=True)


class Sems(NamedTuple):
    send: Any
    recv: Any


class Scratch(NamedTuple):
    vec: Any
    bias: Any
    key: Any
    query: Any
    in_full: Any
    out_full: Any
    up_full: Any
    down_full: Any
    normed_one: Any
    send_qkv: Any
    qkv_t: Any
    kv: Any
    pool: Any
    lse: Any
    delta: Any
    head_out: Any
    send_head: Any
    att_t: Any
    att_all: Any
    att: Any
    middle: Any
    grad_middle: Any
    cot_all: Any
    two_all: Any
    branch_all: Any
    acc_out: Any
    acc_grad: Any
    grad_hidden: Any
    early_grad: Any
    late_grad: Any
    dq: Any
    do_t: Any
    q_rows: Any
    do_rows: Any
    down_theirs: Any
    down_pair: Any
    down_line: Any
    up_mine: Any
    up_pair: Any
    up_line: Any
    up_piece: Any
    out_mine: Any
    out_theirs: Any
    out_pair: Any
    out_line: Any
    dqkv: Any
    gp_t: Any
    one_all: Any
    col: Any
    in_mine: Any
    in_pair: Any
    in_plane: Any
    in_own: Any
    in_line: Any
    in_recv: Any
    early_send: Any
    early_recv: Any
    late_send: Any
    late_recv: Any
    vec_mine: Any
    vec_pair: Any
    sem_load: Any
    sem_pair: Any
    sem_qkv: Any
    sem_one: Any
    sem_col: Any
    sem_col_dq: Any
    sem_in_plane: Any
    sem_cot: Any
    sem_head: Any
    sem_att: Any
    sem_two: Any
    sem_back: Any
    sem_branch: Any
    sem_line: Any
    sem_grads: Any
    sem_up: Any
    sem_in: Any
    sem_early: Any
    sem_late: Any
    sem_dq: Any
    sem_in_w: Any


def scratch():
    def v(shape, kind):
        return pltpu.VMEM(shape, kind)

    def sems(count):
        return Sems(pltpu.SemaphoreType.DMA((count,)), pltpu.SemaphoreType.DMA((count,)))

    return Scratch(
        vec=v((2, 12, 1, 512), F32),
        bias=v((2, 1, 1024), F32),
        key=v((2048, 128), F32),
        query=v((8, 2048), F32),
        in_full=v((1024, 3072), LOW),
        out_full=v((1024, 1024), LOW),
        up_full=v((1024, 4096), LOW),
        down_full=v((4096, 1024), LOW),
        normed_one=v((128, 1024), LOW),
        send_qkv=v((16, 192, 128), LOW),
        qkv_t=v((192, 2048), LOW),
        kv=v((2048, 128), LOW),
        pool=v((512, 1024), F32),
        lse=v((1, 2048), F32),
        delta=v((1, 2048), F32),
        head_out=v((64, 2048), F32),
        send_head=v((16, 64, 128), LOW),
        att_t=v((16, 64, 128), LOW),
        att_all=v((4, 4, 64, 128), LOW),
        att=v((128, 1024), LOW),
        middle=v((128, 1024), F32),
        grad_middle=v((128, 1024), F32),
        cot_all=v((4, 128, 1024), LOW),
        two_all=v((4, 128, 1024), LOW),
        branch_all=v((4, 128, 1024), LOW),
        acc_out=v((128, 1024), F32),
        acc_grad=v((128, 1024), F32),
        grad_hidden=v((512, 1024), LOW),
        early_grad=v((8, 1024), F32),
        late_grad=v((8, 1024), F32),
        dq=v((64, 2048), F32),
        do_t=v((64, 2048), LOW),
        q_rows=v((2048, 128), LOW),
        do_rows=v((2048, 128), LOW),
        down_theirs=v((512, 1024), LOW),
        down_pair=v((512, 1024), LOW),
        down_line=v((3, 128, 1024), LOW),
        up_mine=v((512, 1024), F32),
        up_pair=v((512, 1024), LOW),
        up_line=v((3, 128, 1024), LOW),
        up_piece=v((4, 32, 1024), F32),
        out_mine=v((128, 1024), F32),
        out_theirs=v((128, 1024), LOW),
        out_pair=v((128, 1024), LOW),
        out_line=v((3, 32, 1024), LOW),
        dqkv=v((16, 192, 128), LOW),
        gp_t=v((3072, 128), LOW),
        one_all=v((4, 128, 1024), LOW),
        col=v((4, 4, 192, 128), LOW),
        in_mine=v((4, 4, 32, 768), F32),
        in_pair=v((512, 768), LOW),
        in_plane=v((3, 128, 768), LOW),
        in_own=v((4, 32, 768), F32),
        in_line=v((3, 32, 768), LOW),
        in_recv=v((4, 32, 768), LOW),
        early_send=v((8, 8, 128), F32),
        early_recv=v((16, 8, 128), F32),
        late_send=v((8, 8, 128), F32),
        late_recv=v((16, 8, 128), F32),
        vec_mine=v((24, 128), F32),
        vec_pair=v((24, 128), F32),
        sem_load=sems(6),
        sem_pair=sems(10),
        sem_qkv=sems(16),
        sem_one=sems(16),
        sem_col=sems(16),
        sem_col_dq=sems(16),
        sem_in_plane=sems(3),
        sem_cot=sems(3),
        sem_head=sems(16),
        sem_att=sems(3),
        sem_two=sems(3),
        sem_back=sems(16),
        sem_branch=sems(3),
        sem_line=sems(9),
        sem_grads=sems(16),
        sem_up=sems(12),
        sem_in=sems(16),
        sem_early=sems(16),
        sem_late=sems(16),
        sem_dq=sems(16),
        sem_in_w=sems(12),
    )


def layer_kernel(
    tok_ref,
    cot_ref,
    place_ref,
    length_ref,
    *rest,
):
    vec_refs, rest = rest[:9], rest[9:]
    in_hbm, out_hbm, up_hbm, down_hbm = rest[:4]
    layer_out, input_grad, in_out, out_out, up_out, down_out, vec_out, s = rest[4:]
    n = 16
    scale = HD ** (-0.5)
    c, f = lax.axis_index("ctx"), lax.axis_index("fsdp")
    z, p = c // 4, c % 4
    y, x = p // 2, p % 2
    home = c - p
    sibling = (c, 1 - f)
    plane_places = [2 * y + 1 - x, 2 * (1 - y) + x, 2 * (1 - y) + 1 - x]
    planes = [(home + place, f) for place in plane_places]
    near = z + 1 - 2 * (z % 2)
    far = (z + 2) % 4
    first_core = f == 0

    def remote(src, dst, sems, i, j, device):
        return pltpu.make_async_remote_copy(
            src_ref=src,
            dst_ref=dst,
            send_sem=sems.send.at[i],
            recv_sem=sems.recv.at[j],
            device_id=device,
            device_id_type=MESH_ID,
        )

    def each_peer(step):
        def one(k, carry):
            step((c + k) % n)
            return carry

        lax.fori_loop(1, n, one, 0)

    def to_planes(src_of, dst, sems):
        copies = []
        for i in range(3):
            copy = remote(src_of(i), dst.at[1 + i], sems, i, i, planes[i])
            copy.start()
            copies.append(copy)
        return copies

    barrier = pltpu.get_barrier_semaphore()

    def greet(peer):
        pl.semaphore_signal(barrier, inc=1, device_id=(peer, f), device_id_type=MESH_ID)

    each_peer(greet)
    pl.semaphore_signal(barrier, inc=1, device_id=sibling, device_id_type=MESH_ID)
    for i in range(8):
        s.vec[f, i] = vec_refs[i][...].astype(F32).reshape(1, 512)
    for i in range(4):
        s.vec[f, 8 + i] = vec_refs[8][i * 512 : i * 512 + 512].astype(F32).reshape(1, 512)
    in_load = pltpu.make_async_copy(in_hbm, s.in_full.at[pl.ds(f * 512, 512)], s.sem_load.send.at[0])
    in_load.start()
    pl.semaphore_wait(barrier, n)
    vec_copy = remote(s.vec.at[f], s.vec.at[f], s.sem_pair, 4, 4, sibling)
    vec_copy.start()

    def in_copy_of(g, part):
        at = pl.ds(pl.multiple_of(part * 1024 + (z + g) % 4 * 256, 256), 256)
        return remote(
            in_hbm.at[:, at],
            s.in_full.at[pl.ds(f * 512, 512), at],
            s.sem_in_w,
            g * 3 + part,
            g * 3 + part,
            sibling,
        )

    for g in range(4):
        for part in range(3):
            in_copy_of(g, part).start()
    sent = [vec_copy]
    cot_copies = to_planes(lambda i: cot_ref, s.cot_all, s.sem_cot)
    sent += cot_copies

    weights = [
        (out_hbm, s.out_full, 512),
        (up_hbm, s.up_full, 512),
        (down_hbm, s.down_full, 2048),
    ]
    loads, pairs = [None], [None]
    for i, (src, dst, size) in enumerate(weights):
        load = pltpu.make_async_copy(src, dst.at[pl.ds(f * size, size)], s.sem_load.send.at[1 + i])
        loads.append(load)
        pair = remote(src, dst.at[pl.ds(f * size, size)], s.sem_pair, 1 + i, 1 + i, sibling)
        pairs.append(pair)
    sent += pairs[1:]

    def row(i):
        return jnp.concatenate([s.vec[0, i], s.vec[1, i]], axis=1)

    unit_one, unused = standard(tok_ref[...].astype(F32))
    s.cot_all[0] = cot_ref[...]
    vec_copy.wait_recv()
    s.normed_one[...] = (unit_one * row(4) + row(5)).astype(LOW)
    s.bias[0] = row(0)
    s.bias[1] = row(1)
    in_load.wait()

    def qkv_copy(dst):
        return remote(
            s.send_qkv.at[dst], s.qkv_t.at[:, lanes(c, T)], s.sem_qkv, dst, c, (dst, f)
        )

    def project(g, carry):
        group = (z + g) % 4
        for part in range(3):
            in_copy_of(g, part).wait_recv()
            at = pl.ds(pl.multiple_of(part * 1024 + group * 256, 256), 256)
            acc = dot(s.normed_one[...], s.in_full[:, at])
            if part == 0:
                acc = (acc + s.bias[0, :, lanes(group, 256)]) * scale
            if part == 2:
                acc = acc + s.bias[1, :, lanes(group, 256)]
            for u in range(2):
                block = acc[:, u * T : (u + 1) * T].T.astype(LOW)
                for w in range(2):
                    s.send_qkv[group * 4 + 2 * u + w, part * 64 : part * 64 + 64, :] = block[
                        w * 64 : w * 64 + 64
                    ]
        for u in range(4):
            dst = group * 4 + u

            @pl.when(dst != c)
            def _():
                qkv_copy(dst).start()

            @pl.when(dst == c)
            def _():
                s.qkv_t[:, lanes(c, T)] = s.send_qkv[dst]

        return carry

    lax.fori_loop(0, 4, project, 0)
    for i in range(1, 4):
        loads[i].start()
        pairs[i].start()
    s.one_all[z] = s.normed_one[...]

    place = place_ref[...]
    first, begun = jnp.zeros((1, 2048), jnp.int32), 0
    for i in range(length_ref.shape[1]):
        first = jnp.where(place >= begun, begun, first)
        begun = begun + length_ref[0, i]
    s.query[0:1] = place.astype(F32)
    s.query[1:2] = first.astype(F32)
    for i in range(n):
        at = slice(i * T, i * T + T)
        s.key[at] = jnp.broadcast_to(s.query[0:1, at], (T, T)).T

    def qkv_arrived(src):
        remote(
            s.send_qkv.at[src], s.qkv_t.at[:, lanes(src, T)], s.sem_qkv, src, src, (src, f)
        ).wait_recv()

    each_peer(qkv_arrived)

    far_slot = far * 4 + p

    def one_copy(slot, i, device):
        return remote(s.one_all.at[slot], s.one_all.at[slot], s.sem_one, i, slot, device)

    one_far = one_copy(z, 0, (far_slot, f))
    one_far.start()
    sent.append(one_far)

    for i in range(n):
        at = slice(i * T, i * T + T)
        s.kv[at] = turned(s.qkv_t[64:192, at]).astype(LOW)
    nothing = jnp.zeros((64, 256), LOW)

    def seen(keys, at):
        place = jnp.concatenate([s.key[keys], s.key[keys]], axis=1)
        return (place >= s.query[1:2, at]) & (place <= s.query[0:1, at])

    def head_copy(dst):
        return remote(s.send_head.at[dst], s.att_t.at[p * 4 + z], s.sem_head, dst, c, (dst, f))

    def score_at(k):
        return s.pool.at[pl.ds(k // 4 * 256, 256), pl.ds(k % 4 * 256, 256)]

    def forward(i, carry):
        block = (c // 2 + i) % 8
        at = lanes(block, 256)
        query = jnp.concatenate([s.qkv_t[0:64, at], nothing], axis=0)
        top = jnp.full((8, 256), far_below, F32)
        for k in range(8):
            keys = slice(k * 256, k * 256 + 256)
            score = jnp.where(seen(keys, at), dot(s.kv[keys], query), far_below)
            score_at(k)[...] = score
            top = jnp.maximum(top, jnp.max(score.reshape(32, 8, 256), axis=0))
        top = jnp.max(top, axis=0, keepdims=True)
        total = jnp.zeros((8, 256), F32)
        acc = jnp.zeros((64, 256), F32)
        for k in range(8):
            keys = slice(k * 256, k * 256 + 256)
            grown = jnp.exp(score_at(k)[...] - top)
            total = total + jnp.sum(grown.reshape(32, 8, 256), axis=0)
            acc = acc + dot(s.qkv_t[128:192, keys], grown.astype(LOW))
        total = column_sum(total)
        s.lse[:, at] = top + jnp.log(total)
        result = acc / total
        s.head_out[:, at] = result
        for u in range(2):
            dst = block * 2 + u
            s.send_head[dst] = result[:, u * T : u * T + T].astype(LOW)

            @pl.when(dst != c)
            def _():
                head_copy(dst).start()

            @pl.when(dst == c)
            def _():
                s.att_t[p * 4 + z] = s.send_head[dst]

        return carry

    lax.fori_loop(0, 8, forward, 0)

    def head_arrived(src):
        slot = (src % 4) * 4 + src // 4
        remote(s.send_head.at[src], s.att_t.at[slot], s.sem_head, src, src, (src, f)).wait_recv()

    each_peer(head_arrived)

    def one_arrived(slot):
        one_copy(slot, 0, (far_slot, f)).wait_recv()

    one_arrived(far)
    near_device = (near * 4 + p, f)
    for i, slot in enumerate((z, far)):
        copy = one_copy(slot, 1 + i, near_device)
        copy.start()
        sent.append(copy)

    s.att_all[0] = s.att_t[pl.ds(p * 4, 4)]
    att_copies = to_planes(
        lambda i: s.att_t.at[pl.ds(plane_places[i] * 4, 4)], s.att_all, s.sem_att
    )
    sent += att_copies
    for i in range(8):
        slots = [(h % 4) * 4 + h // 4 for h in (2 * i, 2 * i + 1)]
        block = jnp.concatenate([s.att_t[slots[0]], s.att_t[slots[1]]], axis=0)
        s.att[:, i * T : i * T + T] = turned(block).astype(LOW)

    loads[1].wait()
    pairs[1].wait_recv()
    middle = tok_ref[...].astype(F32) + dot(s.att[...], s.out_full[...]) + row(2)
    s.middle[...] = middle
    unit_two, unused = standard(middle)
    s.two_all[0] = (unit_two * row(6) + row(7)).astype(LOW)
    two_copies = to_planes(lambda i: s.two_all.at[0], s.two_all, s.sem_two)
    sent += two_copies
    for i in (2, 3):
        loads[i].wait()
        pairs[i].wait_recv()
    s.acc_out[...] = jnp.zeros((T, 1024), F32)
    s.acc_grad[...] = jnp.zeros((T, 1024), F32)
    s.late_grad[...] = jnp.zeros((8, 1024), F32)

    def feed(j, carry):
        at = lanes(j, 512)
        hidden = dot(s.two_all[0], s.up_full[:, at]) + s.vec[j // 4, 8 + j % 4]
        active, slope = gelu_pair(hidden)
        grad_active = dot_nt(cot_ref[...], s.down_full[at, :])
        grad_hidden = (grad_active * slope).astype(LOW)
        s.acc_out[...] += dot(active.astype(LOW), s.down_full[at, :])
        s.acc_grad[...] += dot_nt(grad_hidden, s.up_full[:, at])
        summed = column_sum(grad_hidden.astype(F32))
        for q in range(4):
            s.early_grad[4 + q : 5 + q, lanes(j, T)] = summed[:, q * T : q * T + T]
        return carry

    lax.fori_loop(0, 8, feed, 0)
    layer_out[...] = (s.middle[...] + s.acc_out[...] + row(3)).astype(LOW)
    grad_result = cot_ref[...].astype(F32)
    s.early_grad[1:2] = column_sum(grad_result)
    unit_two, spread_two = standard(s.middle[...])
    grad_two = s.acc_grad[...]
    s.early_grad[2:3] = column_sum(grad_two * unit_two)
    s.early_grad[3:4] = column_sum(grad_two)
    grad_middle = grad_result + standard_back(grad_two, row(6), unit_two, spread_two)
    s.grad_middle[...] = grad_middle
    branch = grad_middle.astype(LOW)
    s.branch_all[0] = branch
    s.early_grad[0:1] = column_sum(branch.astype(F32))

    def head_done(dst):
        head_copy(dst).wait_send()

    each_peer(head_done)
    for i in range(4):
        at = slice(i * 256, i * 256 + 256)
        part = dot_nt(s.out_full[at, :], branch).astype(LOW)
        s.send_head[4 * i : 4 * i + 4] = part.reshape(4, 64, T)

    def back_copy(dst):
        return remote(s.send_head.at[dst], s.do_t.at[:, lanes(c, T)], s.sem_back, dst, c, (dst, f))

    each_peer(lambda dst: back_copy(dst).start())
    s.do_t[:, lanes(c, T)] = s.send_head[c]
    branch_copies = to_planes(lambda i: s.branch_all.at[0], s.branch_all, s.sem_branch)
    sent += branch_copies

    def to_owners(grad, send, recv, sems):
        def copy_to(dst):
            return remote(send.at[dst // 2], recv.at[c], sems, dst, c, (dst, f))

        for i in range(8):
            send[i] = grad[:, i * T : i * T + T]
        each_peer(lambda dst: copy_to(dst).start())
        recv[c] = send[c // 2]
        return copy_to

    def from_owners(send, recv, sems):
        each_peer(
            lambda src: remote(
                send.at[src // 2], recv.at[src], sems, src, src, (src, f)
            ).wait_recv()
        )
        return jnp.sum(recv[...], axis=0)

    for i in range(3):
        cot_copies[i].wait_recv()
        two_copies[i].wait_recv()

    def plane_rows(ref):
        return ref[...].reshape(512, 1024)

    def strip(q, carry):
        at = pl.ds(pl.multiple_of(q * 1024 + p * 256, 256), 256)
        shift = s.vec[q // 2, 8 + (q % 2) * 2 + p // 2, :, lanes(p % 2, 256)]
        hidden = dot(plane_rows(s.two_all), s.up_full[:, at]) + shift
        active, slope = gelu_pair(hidden)
        grad_active = dot_nt(plane_rows(s.cot_all), s.down_full[at, :])
        s.grad_hidden[:, lanes(q, 256)] = (grad_active * slope).astype(LOW)
        part = dot_tn(active.astype(LOW), plane_rows(s.cot_all))
        s.pool[lanes(q, T)] = jnp.where(first_core, part[:T], part[T:])
        s.down_theirs[lanes(q, T)] = jnp.where(first_core, part[T:], part[:T]).astype(LOW)
        return carry

    lax.fori_loop(0, 4, strip, 0)
    down_pair = remote(s.down_theirs, s.down_pair, s.sem_pair, 5, 5, sibling)
    down_pair.start()

    def split_rows(part):
        parts = part.reshape(4, 2, 32, 1024)
        mine = jnp.where(first_core, parts[:, 0], parts[:, 1])
        theirs = jnp.where(first_core, parts[:, 1], parts[:, 0])
        return mine, theirs.astype(LOW)

    up_theirs = s.down_full.at[pl.ds(0, 512)]

    def up_rows(q, carry):
        left = s.two_all[:, :, lanes(q, 256)].reshape(512, 256)
        mine, theirs = split_rows(dot_tn(left, s.grad_hidden[...]))
        s.up_mine[lanes(q, T)] = mine.reshape(T, 1024)
        up_theirs[lanes(q, T)] = theirs.reshape(T, 1024)
        return carry

    lax.fori_loop(0, 4, up_rows, 0)
    up_pair = remote(up_theirs, s.up_pair, s.sem_pair, 6, 6, sibling)
    up_pair.start()

    def to_near(mine, theirs, pair, line, base):
        size = line.shape[1]
        copies = []
        for j in range(2):
            at = lanes((near + 2 * j) % 4, size)
            theirs[at] = (mine[at] + pair[at].astype(F32)).astype(LOW)
            copy = remote(
                theirs.at[at], line.at[j], s.sem_line, base + j, base + j, (near * 4 + p, f)
            )
            copy.start()
            copies.append(copy)
        for at in (lanes(z, size), lanes(far, size)):
            mine[at] += pair[at].astype(F32)
        return copies

    def to_far(mine, theirs, line, base, copies):
        size = line.shape[1]
        for copy in copies:
            copy.wait_recv()
        mine[lanes(z, size)] += line[0].astype(F32)
        at = lanes(far, size)
        theirs[at] = (mine[at] + line[1].astype(F32)).astype(LOW)
        copy = remote(theirs.at[at], line.at[2], s.sem_line, base + 2, base + 2, (far_slot, f))
        copy.start()
        return copies + [copy]

    down_pair.wait()
    down_line = to_near(s.pool, s.down_theirs, s.down_pair, s.down_line, 0)
    up_pair.wait()
    up_line = to_near(s.up_mine, up_theirs, s.up_pair, s.up_line, 3)
    early_to = to_owners(s.early_grad, s.early_send, s.early_recv, s.sem_early)

    def qkv_done(dst):
        qkv_copy(dst).wait_send()

    each_peer(qkv_done)

    def back_arrived(src):
        remote(
            s.send_head.at[src], s.do_t.at[:, lanes(src, T)], s.sem_back, src, src, (src, f)
        ).wait_recv()

    each_peer(back_arrived)
    small_nothing = jnp.zeros((64, T), LOW)
    for i in range(n):
        at = slice(i * T, i * T + T)
        s.q_rows[at] = turned(
            jnp.concatenate([s.qkv_t[0:64, at], small_nothing], axis=0)
        ).astype(LOW)
        s.do_rows[at] = turned(
            jnp.concatenate([small_nothing, s.do_t[:, at]], axis=0)
        ).astype(LOW)
    s.delta[...] = column_sum(s.do_t[...].astype(F32) * s.head_out[...])
    s.dq[...] = jnp.zeros((64, 2048), F32)

    def grads_copy(dst):
        return remote(
            s.send_qkv.at[dst, pl.ds(64, 128)],
            s.dqkv.at[c, pl.ds(64, 128)],
            s.sem_grads,
            dst,
            c,
            (dst, f),
        )

    def dq_copy(dst):
        return remote(
            s.send_qkv.at[dst, pl.ds(0, 64)],
            s.dqkv.at[c, pl.ds(0, 64)],
            s.sem_dq,
            dst,
            c,
            (dst, f),
        )

    def col_copy(t, at, size, sems):
        return remote(
            s.send_qkv.at[t, pl.ds(at, size)],
            s.col.at[p, t // 4, pl.ds(at, size)],
            sems,
            t,
            p * 4 + t // 4,
            (home + t % 4, f),
        )

    def each_column(step):
        for k in range(1, 4):
            for i in range(4):
                step(i * 4 + (p + k) % 4)

    def backward(i, carry):
        block = (c // 2 + i) % 8
        keys = pl.ds(pl.multiple_of(block * 256, 256), 256)
        key_t = s.qkv_t[64:128, keys]
        both = s.kv[keys]
        dkv = jnp.zeros((256, 128), F32)
        for q in range(8):
            at = slice(q * 256, q * 256 + 256)
            query = jnp.concatenate([s.qkv_t[0:64, at], nothing], axis=0)
            grad = jnp.concatenate([nothing, s.do_t[:, at]], axis=0)
            score = dot(both, query)
            prob = jnp.where(seen(keys, at), jnp.exp(score - s.lse[:, at]), 0.0)
            grad_prob = dot(both, grad)
            grad_score = (prob * (grad_prob - s.delta[:, at])).astype(LOW)
            dkv = dkv + (
                dot(grad_score, s.q_rows[at]) + dot(prob.astype(LOW), s.do_rows[at])
            )
            s.dq[:, at] += dot(key_t, grad_score)
        for u in range(2):
            dst = block * 2 + u
            s.send_qkv[dst, 64:192] = dkv[u * T : u * T + T].T.astype(LOW)

            @pl.when(dst != c)
            def _():
                grads_copy(dst).start()

            @pl.when(dst % 4 != p)
            def _():
                col_copy(dst, 64, 128, s.sem_col).start()

        return carry

    lax.fori_loop(0, 4, backward, 0)
    down_line = to_far(s.pool, s.down_theirs, s.down_line, 0, down_line)
    lax.fori_loop(4, 8, backward, 0)
    for i in range(n):
        s.send_qkv[i, 0:64] = s.dq[:, i * T : i * T + T].astype(LOW)
    each_column(lambda t: col_copy(t, 0, 64, s.sem_col_dq).start())
    each_peer(lambda dst: dq_copy(dst).start())
    for i in range(4):
        s.col[p, i] = s.send_qkv[i * 4 + p]
    s.dqkv[c] = s.send_qkv[c]
    up_line = to_far(s.up_mine, up_theirs, s.up_line, 3, up_line)
    for i in range(3):
        att_copies[i].wait_recv()
        branch_copies[i].wait_recv()
    part = jnp.zeros((256, 1024), F32)
    for i in range(4):
        part = part + dot(s.att_all[i].reshape(256, T), s.branch_all[i])
    mine, theirs = split_rows(part)
    s.out_mine[...] = mine.reshape(T, 1024)
    s.out_theirs[...] = theirs.reshape(T, 1024)
    out_pair = remote(s.out_theirs, s.out_pair, s.sem_pair, 7, 7, sibling)
    out_pair.start()
    out_pair.wait()
    out_line = to_near(s.out_mine, s.out_theirs, s.out_pair, s.out_line, 6)

    for slot in (near, (near + 2) % 4):
        one_arrived(slot)
    for at, size, sems in ((64, 128, s.sem_col), (0, 64, s.sem_col_dq)):
        for k in range(1, 4):
            for i in range(4):
                q = (p + k) % 4
                here = s.col.at[q, i, pl.ds(at, size)]
                remote(here, here, sems, 0, q * 4 + i, (home + q, f)).wait_recv()
    col_rows = s.up_full.at[pl.ds(0, 768), pl.ds(2048, 512)]
    in_theirs = s.up_full.at[pl.ds(0, 512), pl.ds(0, 768)]
    in_send = [s.up_full.at[pl.ds(i * T, T), pl.ds(1024, 768)] for i in range(3)]
    for q in range(4):
        for i in range(4):
            for part in range(3):
                col_rows[part * 256 + q * 64 : part * 256 + q * 64 + 64, i * T : i * T + T] = (
                    s.col[q, i, part * 64 : part * 64 + 64]
                )
    head_grad = jnp.concatenate([s.send_qkv[i] for i in range(n)], axis=1)
    bias_sums = dot_nt(jnp.ones((8, 2048), LOW), head_grad)
    s.vec_mine[16:24] = jnp.concatenate([bias_sums[:, 0:64] * scale, bias_sums[:, 128:192]], axis=1)

    for i in range(4):
        right = s.one_all[:, :, i * 256 : i * 256 + 256].reshape(512, 256)
        part = dot(col_rows[...], right)
        part = jnp.concatenate([part[0:256] * scale, part[256:768]], axis=0)
        parts = part.T.reshape(4, 2, 32, 768)
        s.in_mine[i] = jnp.where(first_core, parts[:, 0], parts[:, 1])
        theirs = jnp.where(first_core, parts[:, 1], parts[:, 0])
        in_theirs[i * T : i * T + T] = theirs.reshape(T, 768).astype(LOW)
    in_pair = remote(in_theirs, s.in_pair, s.sem_pair, 8, 8, sibling)
    in_pair.start()

    def grads_arrived(src):
        remote(
            s.send_qkv.at[src, pl.ds(64, 128)],
            s.dqkv.at[src, pl.ds(64, 128)],
            s.sem_grads,
            src,
            src,
            (src, f),
        ).wait_recv()

    def dq_arrived(src):
        remote(
            s.send_qkv.at[src, pl.ds(0, 64)],
            s.dqkv.at[src, pl.ds(0, 64)],
            s.sem_dq,
            src,
            src,
            (src, f),
        ).wait_recv()

    each_peer(grads_arrived)
    for h in range(n):
        s.gp_t[1024 + h * 64 : 1088 + h * 64] = s.dqkv[h, 64:128]
        s.gp_t[2048 + h * 64 : 2112 + h * 64] = s.dqkv[h, 128:192]
    for i in range(4):
        at = slice(i * 256, i * 256 + 256)
        s.acc_grad[:, at] = dot(s.in_full[at, 1024:3072], s.gp_t[1024:3072]).T
    each_peer(dq_arrived)
    for h in range(n):
        s.gp_t[h * 64 : h * 64 + 64] = s.dqkv[h, 0:64] * jnp.asarray(scale, LOW)
    for i in range(4):
        at = slice(i * 256, i * 256 + 256)
        s.acc_grad[:, at] += dot(s.in_full[at, 0:1024], s.gp_t[0:1024]).T
    unit_one, spread_one = standard(tok_ref[...].astype(F32))
    grad_one = s.acc_grad[...]
    s.late_grad[0:1] = column_sum(grad_one * unit_one)
    s.late_grad[1:2] = column_sum(grad_one)
    late_to = to_owners(s.late_grad, s.late_send, s.late_recv, s.sem_late)
    input_grad[...] = (
        s.grad_middle[...] + standard_back(grad_one, row(4), unit_one, spread_one)
    ).astype(LOW)

    in_pair.wait()

    def in_total(q, at):
        rows = pl.ds(pl.multiple_of(q * T + at * 32, 32), 32)
        return s.in_mine[q, at] + s.in_pair[rows].astype(F32)

    in_copies = []
    for i in range(3):
        for q in range(4):
            at = plane_places[i]
            in_send[i][q * 32 : q * 32 + 32] = in_total(q, at).astype(LOW)
        copy = remote(in_send[i], s.in_plane.at[i], s.sem_in_plane, i, i, planes[i])
        copy.start()
        in_copies.append(copy)
    for q in range(4):
        s.in_own[q] = in_total(q, p)

    out_line = to_far(s.out_mine, s.out_theirs, s.out_line, 6, out_line)
    up_line[2].wait_recv()
    up_sum = s.up_mine[lanes(z, T)] + s.up_line[2].astype(F32)
    s.up_piece[...] = up_sum.reshape(4, 32, 1024)
    up_copies = []
    for i in range(3):
        for q in range(4):
            copy = remote(
                s.up_piece.at[plane_places[i], :, pl.ds(q * 256, 256)],
                up_out.at[:, pl.ds(pl.multiple_of(q * 1024 + p * 256, 256), 256)],
                s.sem_up,
                i * 4 + q,
                i * 4 + q,
                planes[i],
            )
            copy.start()
            up_copies.append(copy)
    for q in range(4):
        up_out[:, pl.ds(pl.multiple_of(q * 1024 + p * 256, 256), 256)] = s.up_piece[
            p, :, q * 256 : q * 256 + 256
        ]
    down_line[2].wait_recv()
    down_out[...] = s.pool[lanes(z, T)] + s.down_line[2].astype(F32)
    out_line[2].wait_recv()
    out_out[...] = s.out_mine[lanes(z, 32)] + s.out_line[2].astype(F32)

    for copy in in_copies:
        copy.wait_recv()
    in_line = []
    for k in range(1, 4):
        at = (z + k) % 4
        total = s.in_own[at]
        for i in range(3):
            total = total + s.in_plane[i, pl.ds(pl.multiple_of(at * 32, 32), 32)].astype(F32)
        s.in_line[k - 1] = total.astype(LOW)
        copy = remote(
            s.in_line.at[k - 1], s.in_recv.at[z], s.sem_in, k - 1, z, (at * 4 + p, f)
        )
        copy.start()
        in_line.append(copy)

    def put_in(at, block):
        for part in range(3):
            columns = pl.ds(pl.multiple_of(part * 1024 + at * 256, 256), 256)
            in_out[:, columns] = block[:, part * 256 : part * 256 + 256]

    total = s.in_own[z]
    for i in range(3):
        total = total + s.in_plane[i, pl.ds(pl.multiple_of(z * 32, 32), 32)].astype(F32)
    put_in(z, total)

    s.vec_mine[0:8] = from_owners(s.early_send, s.early_recv, s.sem_early)
    s.vec_mine[8:16] = from_owners(s.late_send, s.late_recv, s.sem_late)
    vec_pair = remote(s.vec_mine, s.vec_pair, s.sem_pair, 9, 9, sibling)
    vec_pair.start()

    for k in range(1, 4):
        at = (z + k) % 4
        here = s.in_recv.at[at]
        remote(here, here, s.sem_in, 0, at, (at * 4 + p, f)).wait_recv()
        put_in(at, s.in_recv[at].astype(F32))
    vec_pair.wait()
    total = s.vec_mine[...] + s.vec_pair[...]
    place = (c * 2 + f) % 4
    picked, up_row = total[0:16, 0:32], total[4:5]
    for i in range(1, 4):
        picked = jnp.where(place == i, total[0:16, 32 * i : 32 * i + 32], picked)
        up_row = jnp.where(place == i, total[4 + i : 5 + i], up_row)
    vec_out[0:16, 0:32] = picked
    vec_out[16:24, 0:32] = jnp.where(first_core, total[16:24, 0:32], total[16:24, 32:64])
    vec_out[24:32, 0:32] = jnp.where(first_core, total[16:24, 64:96], total[16:24, 96:128])
    vec_out[32:40] = jnp.broadcast_to(up_row, (8, T))
    for copy in up_copies:
        copy.wait()
    for g in range(4):
        for part in range(3):
            in_copy_of(g, part).wait_send()
    sent += [copy for line in (down_line, up_line, out_line) for copy in line]
    sent += in_copies + in_line
    each_column(lambda t: col_copy(t, 64, 128, s.sem_col).wait_send())
    each_column(lambda t: col_copy(t, 0, 64, s.sem_col_dq).wait_send())
    for copy in sent:
        copy.wait_send()

    def all_sent(dst):
        back_copy(dst).wait_send()
        grads_copy(dst).wait_send()
        dq_copy(dst).wait_send()
        early_to(dst).wait_send()
        late_to(dst).wait_send()

    each_peer(all_sent)


def finish_kernel(*refs):
    vec = refs[6]
    for src, dst in zip(refs[:6], refs[7:13]):
        dst[...] = src[...]
    for i, dst in zip((16, 24, 0, 1, 8, 9, 2, 3), refs[13:21]):
        dst[...] = vec[i : i + 1, 0:32].reshape(32)
    refs[21][...] = vec[32:33].reshape(T)


def body_fused(
    tokens,
    in_weight,
    query_bias,
    value_bias,
    out_weight,
    out_bias,
    up_weight,
    up_bias,
    down_weight,
    down_bias,
    first_gain,
    first_shift,
    second_gain,
    second_shift,
    lengths,
    slot_places,
    cotangent,
):
    vectors = (
        query_bias,
        value_bias,
        out_bias,
        down_bias,
        first_gain,
        first_shift,
        second_gain,
        second_shift,
        up_bias,
    )
    hbm = pl.BlockSpec(memory_space=pl.ANY)
    vmem = pl.BlockSpec(memory_space=pltpu.VMEM)
    outs = pl.pallas_call(
        layer_kernel,
        out_shape=(
            jax.ShapeDtypeStruct((T, 1024), LOW),
            jax.ShapeDtypeStruct((T, 1024), LOW),
            jax.ShapeDtypeStruct((32, 3072), F32),
            jax.ShapeDtypeStruct((32, 1024), F32),
            jax.ShapeDtypeStruct((32, 4096), F32),
            jax.ShapeDtypeStruct((128, 1024), F32),
            jax.ShapeDtypeStruct((40, 128), F32),
        ),
        in_specs=[vmem] * 3 + [pl.BlockSpec(memory_space=pltpu.SMEM)] + [vmem] * 9 + [hbm] * 4,
        out_specs=(vmem,) * 7,
        scratch_shapes=[scratch()],
        compiler_params=pltpu.CompilerParams(
            collective_id=0, has_side_effects=True, vmem_limit_bytes=59 * 2**20
        ),
        cost_estimate=pl.CostEstimate(
            flops=16 * 10**9, bytes_accessed=40 * 2**20, transcendentals=10**7
        ),
    )(
        tokens[0],
        cotangent[0],
        slot_places,
        lengths,
        *vectors,
        in_weight,
        out_weight,
        up_weight,
        down_weight,
    )
    small = [jax.ShapeDtypeStruct((32,), F32)] * 8 + [jax.ShapeDtypeStruct((T,), F32)]
    outs = pl.pallas_call(
        finish_kernel,
        out_shape=[jax.ShapeDtypeStruct(one.shape, one.dtype) for one in outs[:6]] + small,
        in_specs=[vmem] * 7,
        out_specs=[vmem] * 15,
    )(*outs[:7])
    layer_out, input_grad, in_grad, out_grad, up_grad, down_grad = outs[:6]
    query_sum, value_sum, out_sum, down_sum = outs[6:10]
    gain_one, shift_one, gain_two, shift_two, up_sum = outs[10:]
    return (
        layer_out[None],
        input_grad[None],
        in_grad,
        query_sum,
        value_sum,
        out_grad,
        out_sum,
        up_grad,
        up_sum,
        down_grad,
        down_sum,
        gain_one,
        shift_one,
        gain_two,
        shift_two,
    )


def solution(mesh):
    placed = (
        P("fsdp", "ctx", None),
        P("fsdp", None),
        P("fsdp"),
        P("fsdp"),
        P("fsdp", None),
        P("fsdp"),
        P("fsdp", None),
        P("fsdp"),
        P("fsdp", None),
        P("fsdp"),
        P("fsdp"),
        P("fsdp"),
        P("fsdp"),
        P("fsdp"),
        P("fsdp", None),
        P("fsdp", None),
        P("fsdp", "ctx", None),
    )
    return jax.shard_map(
        body_fused if mesh.shape["ctx"] == H else body_general,
        mesh=mesh,
        in_specs=placed,
        out_specs=(
            P("fsdp", "ctx", None),
            P("fsdp", "ctx", None),
            P(("ctx", "fsdp"), None),
            P(("ctx", "fsdp")),
            P(("ctx", "fsdp")),
            P(("ctx", "fsdp"), None),
            P(("ctx", "fsdp")),
            P(("ctx", "fsdp"), None),
            P(("ctx", "fsdp")),
            P(("ctx", "fsdp"), None),
            P(("ctx", "fsdp")),
            P(("ctx", "fsdp")),
            P(("ctx", "fsdp")),
            P(("ctx", "fsdp")),
            P(("ctx", "fsdp")),
        ),
        check_vma=False,
    )
```

```python
import jax
import jax.numpy as jnp
from jax import lax
from typing import Any, NamedTuple
from jax.experimental import pallas as pl
from jax.experimental.pallas import tpu as pltpu
from jax.sharding import PartitionSpec as P

H = 16
HD = 64


epsilon = 1e-05
far_below = -1e30


def normalize(values, gain, shift):
    center = values - jnp.mean(values, axis=-1, keepdims=True)
    spread = jnp.mean(center * center, axis=-1, keepdims=True)
    return center * lax.rsqrt(spread + epsilon) * gain + shift


def gelu_exact(values):
    return jax.nn.gelu(values, approximate=False)


def block_size(total):
    for size in range(min(2048, total), 0, -1):
        if total % size == 0:
            return size
    return total


def segment_of(places, starts):
    return jnp.sum((starts[None, :] <= places[:, None]).astype(jnp.int32), axis=1) - 1


def visible(query_place, query_segment, key_place, key_segment):
    return (key_segment[None, :] == query_segment[:, None]) & (
        key_place[None, :] <= query_place[:, None]
    )


def scores_of(queries, key_rows, allowed):
    scores = jnp.einsum("qhd,khd->hqk", queries, key_rows, preferred_element_type=jnp.float32)
    return jnp.where(allowed[None], scores, far_below)


def inner_rows(left, right):
    return jnp.einsum("tf,tg->fg", left, right, preferred_element_type=jnp.float32)


def times_transposed(left, right):
    return jnp.einsum("tg,fg->tf", left, right, preferred_element_type=jnp.float32)


def key_terms(probs_low, grad_scores, query_rows, grad_rows, size, width):
    grad_keys = jnp.einsum(
        "hqk,qhd->khd", grad_scores, query_rows, preferred_element_type=jnp.float32
    )
    grad_values = jnp.einsum(
        "hqk,qhd->khd", probs_low, grad_rows, preferred_element_type=jnp.float32
    )
    return jnp.concatenate(
        [grad_keys.reshape(size, width), grad_values.reshape(size, width)], axis=1
    )


def body_general(
    tokens,
    in_weight,
    query_bias,
    value_bias,
    out_weight,
    out_bias,
    up_weight,
    up_bias,
    down_weight,
    down_bias,
    first_gain,
    first_shift,
    second_gain,
    second_shift,
    lengths,
    slot_places,
    cotangent,
):
    gathered_params = (
        lax.all_gather(in_weight, "fsdp", axis=0, tiled=True),
        lax.all_gather(query_bias, "fsdp", axis=0, tiled=True),
        lax.all_gather(value_bias, "fsdp", axis=0, tiled=True),
        lax.all_gather(out_weight, "fsdp", axis=0, tiled=True),
        lax.all_gather(out_bias, "fsdp", axis=0, tiled=True),
        lax.all_gather(up_weight, "fsdp", axis=0, tiled=True),
        lax.all_gather(up_bias, "fsdp", axis=0, tiled=True),
        lax.all_gather(down_weight, "fsdp", axis=0, tiled=True),
        lax.all_gather(down_bias, "fsdp", axis=0, tiled=True),
        lax.all_gather(first_gain, "fsdp", axis=0, tiled=True),
        lax.all_gather(first_shift, "fsdp", axis=0, tiled=True),
        lax.all_gather(second_gain, "fsdp", axis=0, tiled=True),
        lax.all_gather(second_shift, "fsdp", axis=0, tiled=True),
    )
    (
        in_full,
        query_shift,
        value_shift,
        out_full,
        out_shift,
        up_full,
        up_shift,
        down_full,
        down_shift,
        gain_first,
        shift_first,
        gain_second,
        shift_second,
    ) = gathered_params
    query_shift = query_shift.astype(jnp.float32)
    value_shift = value_shift.astype(jnp.float32)
    out_shift = out_shift.astype(jnp.float32)
    up_shift = up_shift.astype(jnp.float32)
    down_shift = down_shift.astype(jnp.float32)
    gain_first = gain_first.astype(jnp.float32)
    shift_first = shift_first.astype(jnp.float32)
    gain_second = gain_second.astype(jnp.float32)
    shift_second = shift_second.astype(jnp.float32)
    inputs = tokens[0].astype(jnp.float32)
    rows = inputs.shape[0]
    width = inputs.shape[1]
    scale = HD ** (-0.5)
    places = slot_places[0]
    seq_lengths = lengths[0]
    starts = jnp.cumsum(seq_lengths) - seq_lengths
    key_segments = segment_of(places, starts)
    first_slot = lax.axis_index("ctx") * rows
    query_places = lax.dynamic_slice_in_dim(places, first_slot, rows)
    query_segments = lax.dynamic_slice_in_dim(key_segments, first_slot, rows)
    total_keys = places.shape[0]
    key_step = block_size(total_keys)
    block_count = total_keys // key_step
    place_blocks = places.reshape(block_count, key_step)
    segment_blocks = key_segments.reshape(block_count, key_step)
    normed_one = normalize(inputs, gain_first, shift_first).astype(jnp.bfloat16)
    projected = jnp.dot(normed_one, in_full, preferred_element_type=jnp.float32)
    queries = (
        ((projected[:, :width] + query_shift) * scale).astype(jnp.bfloat16).reshape(rows, H, HD)
    )
    key_value = jnp.concatenate(
        [projected[:, width : 2 * width], projected[:, 2 * width :] + value_shift], axis=1
    ).astype(jnp.bfloat16)
    gathered = lax.all_gather(key_value, "ctx", axis=0, tiled=True)
    pair_blocks = gathered.reshape(block_count, key_step, 2 * width)

    def split_pair(pair, size):
        return (pair[:, :width].reshape(size, H, HD), pair[:, width:].reshape(size, H, HD))

    def max_step(carry, block):
        top, total = carry
        pair, key_place, key_segment = block
        key_rows, value_rows = split_pair(pair, key_step)
        allowed = visible(query_places, query_segments, key_place, key_segment)
        scores = scores_of(queries, key_rows, allowed)
        new_top = jnp.maximum(top, jnp.max(scores, axis=2))
        expand = jnp.where(allowed[None], jnp.exp(scores - new_top[:, :, None]), 0.0)
        total = total * jnp.exp(top - new_top) + jnp.sum(expand, axis=2)
        return ((new_top, total), None)

    start_top = jnp.full((H, rows), far_below, jnp.float32)
    (top, total), unused = lax.scan(
        max_step,
        (start_top, jnp.zeros((H, rows), jnp.float32)),
        (pair_blocks, place_blocks, segment_blocks),
    )
    log_total = top + jnp.log(total)

    def value_step(summed, block):
        pair, key_place, key_segment = block
        key_rows, value_rows = split_pair(pair, key_step)
        allowed = visible(query_places, query_segments, key_place, key_segment)
        scores = scores_of(queries, key_rows, allowed)
        weights = jnp.where(allowed[None], jnp.exp(scores - log_total[:, :, None]), 0.0).astype(
            jnp.bfloat16
        )
        summed = summed + jnp.einsum(
            "hqk,khd->qhd", weights, value_rows, preferred_element_type=jnp.float32
        )
        return (summed, None)

    heads_out, unused = lax.scan(
        value_step,
        jnp.zeros((rows, H, HD), jnp.float32),
        (pair_blocks, place_blocks, segment_blocks),
    )
    attended = heads_out.reshape(rows, width).astype(jnp.bfloat16)
    middle = inputs + jnp.dot(attended, out_full, preferred_element_type=jnp.float32) + out_shift
    normed_two = normalize(middle, gain_second, shift_second).astype(jnp.bfloat16)
    hidden = jnp.dot(normed_two, up_full, preferred_element_type=jnp.float32) + up_shift
    active_full, gelu_back = jax.vjp(gelu_exact, hidden)
    active = active_full.astype(jnp.bfloat16)
    result = middle + jnp.dot(active, down_full, preferred_element_type=jnp.float32) + down_shift
    layer_out = result.astype(jnp.bfloat16)[None]
    grad_low = cotangent[0]
    grad_result = grad_low.astype(jnp.float32)
    down_grad = inner_rows(active, grad_low)
    down_bias_grad = jnp.sum(grad_result, axis=0)
    grad_active = times_transposed(grad_low, down_full)
    grad_hidden = gelu_back(grad_active)[0].astype(jnp.bfloat16)
    up_grad = inner_rows(normed_two, grad_hidden)
    up_bias_grad = jnp.sum(grad_hidden.astype(jnp.float32), axis=0)
    grad_normed_two = times_transposed(grad_hidden, up_full)
    unused, second_back = jax.vjp(normalize, middle, gain_second, shift_second)
    grad_middle_norm, gain_two_grad, shift_two_grad = second_back(grad_normed_two)
    grad_middle = grad_result + grad_middle_norm
    grad_branch = grad_middle.astype(jnp.bfloat16)
    out_grad = inner_rows(attended, grad_branch)
    out_bias_grad = jnp.sum(grad_branch.astype(jnp.float32), axis=0)
    grad_attended = (
        times_transposed(grad_branch, out_full).astype(jnp.bfloat16).reshape(rows, H, HD)
    )
    deltas = jnp.sum(grad_attended.astype(jnp.float32) * heads_out, axis=2).T

    def block_back(key_rows, value_rows, allowed):
        scores = scores_of(queries, key_rows, allowed)
        probs = jnp.where(allowed[None], jnp.exp(scores - log_total[:, :, None]), 0.0)
        grad_probs = jnp.einsum(
            "qhd,khd->hqk", grad_attended, value_rows, preferred_element_type=jnp.float32
        )
        grad_scores = (probs * (grad_probs - deltas[:, :, None])).astype(jnp.bfloat16)
        return (probs.astype(jnp.bfloat16), grad_scores)

    def query_term(grad_scores, key_rows):
        return jnp.einsum("hqk,khd->qhd", grad_scores, key_rows, preferred_element_type=jnp.float32)

    def whole_step(grad_queries, block):
        pair, key_place, key_segment = block
        key_rows, value_rows = split_pair(pair, key_step)
        allowed = visible(query_places, query_segments, key_place, key_segment)
        probs_low, grad_scores = block_back(key_rows, value_rows, allowed)
        grad_queries = grad_queries + query_term(grad_scores, key_rows)
        return (
            grad_queries,
            key_terms(probs_low, grad_scores, queries, grad_attended, key_step, width),
        )

    grad_queries, terms = lax.scan(
        whole_step,
        jnp.zeros((rows, H, HD), jnp.float32),
        (pair_blocks, place_blocks, segment_blocks),
    )
    key_grads = lax.psum_scatter(
        terms.reshape(total_keys, 2 * width), "ctx", scatter_dimension=0, tiled=True
    )
    key_grads_low = key_grads.astype(jnp.bfloat16)
    grad_queries_low = grad_queries.reshape(rows, width).astype(jnp.bfloat16)
    grad_projected = jnp.concatenate([grad_queries_low, key_grads_low], axis=1)
    in_grad_raw = inner_rows(normed_one, grad_projected)
    in_grad = jnp.concatenate([in_grad_raw[:, :width] * scale, in_grad_raw[:, width:]], axis=1)
    query_bias_grad = jnp.sum(grad_queries_low.astype(jnp.float32), axis=0) * scale
    value_bias_grad = jnp.sum(key_grads_low[:, width:].astype(jnp.float32), axis=0)
    grad_normed_one = times_transposed(
        grad_queries_low, in_full[:, :width]
    ) * scale + times_transposed(key_grads_low, in_full[:, width:])
    unused, first_back = jax.vjp(normalize, inputs, gain_first, shift_first)
    grad_inputs_norm, gain_one_grad, shift_one_grad = first_back(grad_normed_one)
    input_grad = (grad_middle + grad_inputs_norm).astype(jnp.bfloat16)[None]
    grads = (
        in_grad,
        query_bias_grad,
        value_bias_grad,
        out_grad,
        out_bias_grad,
        up_grad,
        up_bias_grad,
        down_grad,
        down_bias_grad,
        gain_one_grad,
        shift_one_grad,
        gain_two_grad,
        shift_two_grad,
    )
    summed = (
        lax.psum_scatter(grads[0], ("ctx", "fsdp"), scatter_dimension=0, tiled=True),
        lax.psum_scatter(grads[1], ("ctx", "fsdp"), scatter_dimension=0, tiled=True),
        lax.psum_scatter(grads[2], ("ctx", "fsdp"), scatter_dimension=0, tiled=True),
        lax.psum_scatter(grads[3], ("ctx", "fsdp"), scatter_dimension=0, tiled=True),
        lax.psum_scatter(grads[4], ("ctx", "fsdp"), scatter_dimension=0, tiled=True),
        lax.psum_scatter(grads[5], ("ctx", "fsdp"), scatter_dimension=0, tiled=True),
        lax.psum_scatter(grads[6], ("ctx", "fsdp"), scatter_dimension=0, tiled=True),
        lax.psum_scatter(grads[7], ("ctx", "fsdp"), scatter_dimension=0, tiled=True),
        lax.psum_scatter(grads[8], ("ctx", "fsdp"), scatter_dimension=0, tiled=True),
        lax.psum_scatter(grads[9], ("ctx", "fsdp"), scatter_dimension=0, tiled=True),
        lax.psum_scatter(grads[10], ("ctx", "fsdp"), scatter_dimension=0, tiled=True),
        lax.psum_scatter(grads[11], ("ctx", "fsdp"), scatter_dimension=0, tiled=True),
        lax.psum_scatter(grads[12], ("ctx", "fsdp"), scatter_dimension=0, tiled=True),
    )
    (
        in_weight_grad,
        query_bias_grad_out,
        value_bias_grad_out,
        out_weight_grad,
        out_bias_grad_out,
        up_weight_grad,
        up_bias_grad_out,
        down_weight_grad,
        down_bias_grad_out,
        first_gain_grad,
        first_shift_grad,
        second_gain_grad,
        second_shift_grad,
    ) = summed
    return (
        layer_out,
        input_grad,
        in_weight_grad,
        query_bias_grad_out,
        value_bias_grad_out,
        out_weight_grad,
        out_bias_grad_out,
        up_weight_grad,
        up_bias_grad_out,
        down_weight_grad,
        down_bias_grad_out,
        first_gain_grad,
        first_shift_grad,
        second_gain_grad,
        second_shift_grad,
    )


MESH_ID = pl.DeviceIdType.MESH
LOW = jnp.bfloat16
F32 = jnp.float32
T = 128


def dot(left, right):
    return jnp.dot(left, right, preferred_element_type=jnp.float32)


def dot_nt(left, right):
    return lax.dot_general(left, right, (((1,), (1,)), ((), ())), preferred_element_type=F32)


def dot_tn(left, right):
    return lax.dot_general(left, right, (((0,), (0,)), ((), ())), preferred_element_type=F32)


def turned(block):
    return block.astype(F32).T


def standard(values):
    center = values - jnp.mean(values, axis=1, keepdims=True)
    spread = lax.rsqrt(jnp.mean(center * center, axis=1, keepdims=True) + epsilon)
    return center * spread, spread


def standard_back(grad, gain, unit, spread):
    e = grad * gain
    return spread * (
        e - jnp.mean(e, axis=1, keepdims=True) - unit * jnp.mean(e * unit, axis=1, keepdims=True)
    )


def gelu_pair(hidden):
    phi = 0.5 * (1.0 + lax.erf(hidden * 0.7071067811865476))
    density = jnp.exp(hidden * hidden * -0.5) * 0.3989422804014327
    return hidden * phi, phi + hidden * density


def lanes(index, size):
    return pl.ds(pl.multiple_of(index * size, size), size)


def column_sum(values):
    return jnp.sum(values, axis=0, keepdims=True)


class Sems(NamedTuple):
    send: Any
    recv: Any


class Scratch(NamedTuple):
    vec: Any
    bias: Any
    key: Any
    query: Any
    in_full: Any
    out_full: Any
    up_full: Any
    down_full: Any
    normed_one: Any
    send_qkv: Any
    qkv_t: Any
    kv: Any
    pool: Any
    lse: Any
    delta: Any
    head_out: Any
    send_head: Any
    att_t: Any
    att_all: Any
    att: Any
    middle: Any
    grad_middle: Any
    cot_all: Any
    two_all: Any
    branch_all: Any
    acc_out: Any
    acc_grad: Any
    grad_hidden: Any
    early_grad: Any
    late_grad: Any
    dq: Any
    do_t: Any
    q_rows: Any
    do_rows: Any
    down_theirs: Any
    down_pair: Any
    down_line: Any
    up_mine: Any
    up_pair: Any
    up_line: Any
    up_piece: Any
    out_mine: Any
    out_theirs: Any
    out_pair: Any
    out_line: Any
    dqkv: Any
    gp_t: Any
    one_all: Any
    col: Any
    in_mine: Any
    in_pair: Any
    in_plane: Any
    in_own: Any
    in_line: Any
    in_recv: Any
    early_send: Any
    early_recv: Any
    late_send: Any
    late_recv: Any
    vec_mine: Any
    vec_pair: Any
    sem_load: Any
    sem_pair: Any
    sem_qkv: Any
    sem_one: Any
    sem_down_pair: Any
    sem_up_pair: Any
    sem_col: Any
    sem_col_dq: Any
    sem_in_plane: Any
    sem_cot: Any
    sem_head: Any
    sem_att: Any
    sem_two: Any
    sem_back: Any
    sem_branch: Any
    sem_line: Any
    sem_grads: Any
    sem_up: Any
    sem_in: Any
    sem_early: Any
    sem_late: Any
    sem_dq: Any
    sem_in_w: Any


def scratch():
    def v(shape, kind):
        return pltpu.VMEM(shape, kind)

    def sems(count):
        return Sems(pltpu.SemaphoreType.DMA((count,)), pltpu.SemaphoreType.DMA((count,)))

    return Scratch(
        vec=v((2, 12, 1, 512), F32),
        bias=v((2, 1, 1024), F32),
        key=v((2048, 128), F32),
        query=v((8, 2048), F32),
        in_full=v((1024, 3072), LOW),
        out_full=v((1024, 1024), LOW),
        up_full=v((1024, 4096), LOW),
        down_full=v((4096, 1024), LOW),
        normed_one=v((128, 1024), LOW),
        send_qkv=v((16, 192, 128), LOW),
        qkv_t=v((192, 2048), LOW),
        kv=v((2048, 128), LOW),
        pool=v((512, 1024), F32),
        lse=v((1, 2048), F32),
        delta=v((1, 2048), F32),
        head_out=v((64, 2048), F32),
        send_head=v((16, 64, 128), LOW),
        att_t=v((16, 64, 128), LOW),
        att_all=v((4, 4, 64, 128), LOW),
        att=v((128, 1024), LOW),
        middle=v((128, 1024), F32),
        grad_middle=v((128, 1024), F32),
        cot_all=v((4, 128, 1024), LOW),
        two_all=v((4, 128, 1024), LOW),
        branch_all=v((4, 128, 1024), LOW),
        acc_out=v((128, 1024), F32),
        acc_grad=v((128, 1024), F32),
        grad_hidden=v((512, 1024), LOW),
        early_grad=v((8, 1024), F32),
        late_grad=v((8, 1024), F32),
        dq=v((64, 2048), F32),
        do_t=v((64, 2048), LOW),
        q_rows=v((2048, 128), LOW),
        do_rows=v((2048, 128), LOW),
        down_theirs=v((512, 1024), LOW),
        down_pair=v((512, 1024), LOW),
        down_line=v((3, 128, 1024), LOW),
        up_mine=v((512, 1024), F32),
        up_pair=v((512, 1024), LOW),
        up_line=v((3, 128, 1024), LOW),
        up_piece=v((4, 32, 1024), F32),
        out_mine=v((128, 1024), F32),
        out_theirs=v((128, 1024), LOW),
        out_pair=v((128, 1024), LOW),
        out_line=v((3, 32, 1024), LOW),
        dqkv=v((16, 192, 128), LOW),
        gp_t=v((3072, 128), LOW),
        one_all=v((4, 128, 1024), LOW),
        col=v((4, 4, 192, 128), LOW),
        in_mine=v((4, 4, 32, 768), F32),
        in_pair=v((512, 768), LOW),
        in_plane=v((3, 128, 768), LOW),
        in_own=v((4, 32, 768), F32),
        in_line=v((3, 32, 768), LOW),
        in_recv=v((4, 32, 768), LOW),
        early_send=v((8, 8, 128), F32),
        early_recv=v((16, 8, 128), F32),
        late_send=v((8, 8, 128), F32),
        late_recv=v((16, 8, 128), F32),
        vec_mine=v((24, 128), F32),
        vec_pair=v((24, 128), F32),
        sem_load=sems(6),
        sem_pair=sems(10),
        sem_qkv=sems(16),
        sem_one=sems(16),
        sem_down_pair=sems(4),
        sem_up_pair=sems(4),
        sem_col=sems(16),
        sem_col_dq=sems(16),
        sem_in_plane=sems(3),
        sem_cot=sems(3),
        sem_head=sems(16),
        sem_att=sems(3),
        sem_two=sems(3),
        sem_back=sems(16),
        sem_branch=sems(3),
        sem_line=sems(9),
        sem_grads=sems(16),
        sem_up=sems(12),
        sem_in=sems(16),
        sem_early=sems(16),
        sem_late=sems(16),
        sem_dq=sems(16),
        sem_in_w=sems(12),
    )


def layer_kernel(
    tok_ref,
    cot_ref,
    place_ref,
    length_ref,
    *rest,
):
    vec_refs, rest = rest[:9], rest[9:]
    in_hbm, out_hbm, up_hbm, down_hbm = rest[:4]
    layer_out, input_grad, in_out, out_out, up_out, down_out, vec_out, s = rest[4:]
    n = 16
    scale = HD ** (-0.5)
    c, f = lax.axis_index("ctx"), lax.axis_index("fsdp")
    z, p = c // 4, c % 4
    y, x = p // 2, p % 2
    home = c - p
    sibling = (c, 1 - f)
    plane_places = [2 * y + 1 - x, 2 * (1 - y) + x, 2 * (1 - y) + 1 - x]
    planes = [(home + place, f) for place in plane_places]
    near = z + 1 - 2 * (z % 2)
    far = (z + 2) % 4
    first_core = f == 0

    def remote(src, dst, sems, i, j, device):
        return pltpu.make_async_remote_copy(
            src_ref=src,
            dst_ref=dst,
            send_sem=sems.send.at[i],
            recv_sem=sems.recv.at[j],
            device_id=device,
            device_id_type=MESH_ID,
        )

    def each_peer(step):
        def one(k, carry):
            step((c + k) % n)
            return carry

        lax.fori_loop(1, n, one, 0)

    def to_planes(src_of, dst, sems):
        copies = []
        for i in range(3):
            copy = remote(src_of(i), dst.at[1 + i], sems, i, i, planes[i])
            copy.start()
            copies.append(copy)
        return copies

    barrier = pltpu.get_barrier_semaphore()

    def greet(peer):
        pl.semaphore_signal(barrier, inc=1, device_id=(peer, f), device_id_type=MESH_ID)

    each_peer(greet)
    pl.semaphore_signal(barrier, inc=1, device_id=sibling, device_id_type=MESH_ID)
    for i in range(8):
        s.vec[f, i] = vec_refs[i][...].astype(F32).reshape(1, 512)
    for i in range(4):
        s.vec[f, 8 + i] = vec_refs[8][i * 512 : i * 512 + 512].astype(F32).reshape(1, 512)
    in_load = pltpu.make_async_copy(in_hbm, s.in_full.at[pl.ds(f * 512, 512)], s.sem_load.send.at[0])
    in_load.start()
    unit_one, unused = standard(tok_ref[...].astype(F32))
    pl.semaphore_wait(barrier, n)
    vec_copy = remote(s.vec.at[f], s.vec.at[f], s.sem_pair, 4, 4, sibling)
    vec_copy.start()

    def in_copy_of(g, part):
        at = pl.ds(pl.multiple_of(part * 1024 + (z + g) % 4 * 256, 256), 256)
        return remote(
            in_hbm.at[:, at],
            s.in_full.at[pl.ds(f * 512, 512), at],
            s.sem_in_w,
            g * 3 + part,
            g * 3 + part,
            sibling,
        )

    for g in range(4):
        for part in range(3):
            in_copy_of(g, part).start()
    sent = [vec_copy]
    cot_copies = to_planes(lambda i: cot_ref, s.cot_all, s.sem_cot)
    sent += cot_copies

    weights = [
        (out_hbm, s.out_full, 512),
        (up_hbm, s.up_full, 512),
        (down_hbm, s.down_full, 2048),
    ]
    loads, pairs = [None], [None]
    for i, (src, dst, size) in enumerate(weights):
        load = pltpu.make_async_copy(src, dst.at[pl.ds(f * size, size)], s.sem_load.send.at[1 + i])
        loads.append(load)
        pair = remote(src, dst.at[pl.ds(f * size, size)], s.sem_pair, 1 + i, 1 + i, sibling)
        pairs.append(pair)
    sent += pairs[1:]

    def row(i):
        return jnp.concatenate([s.vec[0, i], s.vec[1, i]], axis=1)

    s.cot_all[0] = cot_ref[...]
    vec_copy.wait_recv()
    s.normed_one[...] = (unit_one * row(4) + row(5)).astype(LOW)
    s.bias[0] = row(0)
    s.bias[1] = row(1)
    in_load.wait()

    def qkv_copy(dst):
        return remote(
            s.send_qkv.at[dst], s.qkv_t.at[:, lanes(c, T)], s.sem_qkv, dst, c, (dst, f)
        )

    def project(g, carry):
        group = (z + g) % 4
        for part in range(3):
            in_copy_of(g, part).wait_recv()
            at = pl.ds(pl.multiple_of(part * 1024 + group * 256, 256), 256)
            acc = dot(s.normed_one[...], s.in_full[:, at])
            if part == 0:
                acc = (acc + s.bias[0, :, lanes(group, 256)]) * scale
            if part == 2:
                acc = acc + s.bias[1, :, lanes(group, 256)]
            for u in range(2):
                block = acc[:, u * T : (u + 1) * T].T.astype(LOW)
                for w in range(2):
                    s.send_qkv[group * 4 + 2 * u + w, part * 64 : part * 64 + 64, :] = block[
                        w * 64 : w * 64 + 64
                    ]
        for u in range(4):
            dst = group * 4 + u

            @pl.when(dst != c)
            def _():
                qkv_copy(dst).start()

            @pl.when(dst == c)
            def _():
                s.qkv_t[:, lanes(c, T)] = s.send_qkv[dst]

        return carry

    lax.fori_loop(0, 4, project, 0)
    for i in range(1, 4):
        loads[i].start()
        pairs[i].start()
    s.one_all[z] = s.normed_one[...]

    place = place_ref[...]
    first, begun = jnp.zeros((1, 2048), jnp.int32), 0
    for i in range(length_ref.shape[1]):
        first = jnp.where(place >= begun, begun, first)
        begun = begun + length_ref[0, i]
    s.query[0:1] = place.astype(F32)
    s.query[1:2] = first.astype(F32)
    for i in range(n):
        at = slice(i * T, i * T + T)
        s.key[at] = jnp.broadcast_to(s.query[0:1, at], (T, T)).T

    def qkv_arrived(src):
        remote(
            s.send_qkv.at[src], s.qkv_t.at[:, lanes(src, T)], s.sem_qkv, src, src, (src, f)
        ).wait_recv()

    each_peer(qkv_arrived)

    far_slot = far * 4 + p

    def one_copy(slot, i, device):
        return remote(s.one_all.at[slot], s.one_all.at[slot], s.sem_one, i, slot, device)

    one_far = one_copy(z, 0, (far_slot, f))
    one_far.start()
    sent.append(one_far)

    for i in range(n):
        at = slice(i * T, i * T + T)
        s.kv[at] = turned(s.qkv_t[64:192, at]).astype(LOW)
    nothing = jnp.zeros((64, 256), LOW)

    def seen(keys, at):
        place = jnp.concatenate([s.key[keys], s.key[keys]], axis=1)
        return (place >= s.query[1:2, at]) & (place <= s.query[0:1, at])

    def head_copy(dst):
        return remote(s.send_head.at[dst], s.att_t.at[p * 4 + z], s.sem_head, dst, c, (dst, f))

    def score_at(k):
        return s.pool.at[pl.ds(k // 4 * 256, 256), pl.ds(k % 4 * 256, 256)]

    def forward(i, carry):
        block = (c // 2 + i) % 8
        at = lanes(block, 256)
        query = jnp.concatenate([s.qkv_t[0:64, at], nothing], axis=0)
        top = jnp.full((8, 256), far_below, F32)
        for k in range(8):
            keys = slice(k * 256, k * 256 + 256)
            score = jnp.where(seen(keys, at), dot(s.kv[keys], query), far_below)
            score_at(k)[...] = score
            top = jnp.maximum(top, jnp.max(score.reshape(32, 8, 256), axis=0))
        top = jnp.max(top, axis=0, keepdims=True)
        total = jnp.zeros((8, 256), F32)
        acc = jnp.zeros((64, 256), F32)
        for k in range(8):
            keys = slice(k * 256, k * 256 + 256)
            grown = jnp.exp(score_at(k)[...] - top)
            total = total + jnp.sum(grown.reshape(32, 8, 256), axis=0)
            acc = acc + dot(s.qkv_t[128:192, keys], grown.astype(LOW))
        total = column_sum(total)
        s.lse[:, at] = top + jnp.log(total)
        result = acc / total
        s.head_out[:, at] = result
        for u in range(2):
            dst = block * 2 + u
            s.send_head[dst] = result[:, u * T : u * T + T].astype(LOW)

            @pl.when(dst != c)
            def _():
                head_copy(dst).start()

            @pl.when(dst == c)
            def _():
                s.att_t[p * 4 + z] = s.send_head[dst]

        return carry

    lax.fori_loop(0, 8, forward, 0)

    def head_arrived(src):
        slot = (src % 4) * 4 + src // 4
        remote(s.send_head.at[src], s.att_t.at[slot], s.sem_head, src, src, (src, f)).wait_recv()

    each_peer(head_arrived)

    def one_arrived(slot):
        one_copy(slot, 0, (far_slot, f)).wait_recv()

    one_arrived(far)
    near_device = (near * 4 + p, f)
    for i, slot in enumerate((z, far)):
        copy = one_copy(slot, 1 + i, near_device)
        copy.start()
        sent.append(copy)

    s.att_all[0] = s.att_t[pl.ds(p * 4, 4)]
    for i in range(8):
        slots = [(h % 4) * 4 + h // 4 for h in (2 * i, 2 * i + 1)]
        block = jnp.concatenate([s.att_t[slots[0]], s.att_t[slots[1]]], axis=0)
        s.att[:, i * T : i * T + T] = turned(block).astype(LOW)

    loads[1].wait()
    pairs[1].wait_recv()
    middle = tok_ref[...].astype(F32) + dot(s.att[...], s.out_full[...]) + row(2)
    s.middle[...] = middle
    unit_two, unused = standard(middle)
    s.two_all[0] = (unit_two * row(6) + row(7)).astype(LOW)
    two_copies = to_planes(lambda i: s.two_all.at[0], s.two_all, s.sem_two)
    sent += two_copies
    for i in (2, 3):
        loads[i].wait()
        pairs[i].wait_recv()
    s.acc_out[...] = jnp.zeros((T, 1024), F32)
    s.acc_grad[...] = jnp.zeros((T, 1024), F32)
    s.late_grad[...] = jnp.zeros((8, 1024), F32)

    def feed(j, carry):
        at = lanes(j, 512)
        hidden = dot(s.two_all[0], s.up_full[:, at]) + s.vec[j // 4, 8 + j % 4]
        active, slope = gelu_pair(hidden)
        grad_active = dot_nt(cot_ref[...], s.down_full[at, :])
        grad_hidden = (grad_active * slope).astype(LOW)
        s.acc_out[...] += dot(active.astype(LOW), s.down_full[at, :])
        s.acc_grad[...] += dot_nt(grad_hidden, s.up_full[:, at])
        summed = column_sum(grad_hidden.astype(F32))
        for q in range(4):
            s.early_grad[4 + q : 5 + q, lanes(j, T)] = summed[:, q * T : q * T + T]
        return carry

    lax.fori_loop(0, 8, feed, 0)
    layer_out[...] = (s.middle[...] + s.acc_out[...] + row(3)).astype(LOW)
    grad_result = cot_ref[...].astype(F32)
    s.early_grad[1:2] = column_sum(grad_result)
    unit_two, spread_two = standard(s.middle[...])
    grad_two = s.acc_grad[...]
    s.early_grad[2:3] = column_sum(grad_two * unit_two)
    s.early_grad[3:4] = column_sum(grad_two)
    grad_middle = grad_result + standard_back(grad_two, row(6), unit_two, spread_two)
    s.grad_middle[...] = grad_middle
    branch = grad_middle.astype(LOW)
    s.branch_all[0] = branch
    s.early_grad[0:1] = column_sum(branch.astype(F32))

    def head_done(dst):
        head_copy(dst).wait_send()

    each_peer(head_done)
    for i in range(4):
        at = slice(i * 256, i * 256 + 256)
        part = dot_nt(s.out_full[at, :], branch).astype(LOW)
        s.send_head[4 * i : 4 * i + 4] = part.reshape(4, 64, T)

    def back_copy(dst):
        return remote(s.send_head.at[dst], s.do_t.at[:, lanes(c, T)], s.sem_back, dst, c, (dst, f))

    each_peer(lambda dst: back_copy(dst).start())
    s.do_t[:, lanes(c, T)] = s.send_head[c]
    branch_copies = to_planes(lambda i: s.branch_all.at[0], s.branch_all, s.sem_branch)
    sent += branch_copies
    att_copies = to_planes(
        lambda i: s.att_t.at[pl.ds(plane_places[i] * 4, 4)], s.att_all, s.sem_att
    )
    sent += att_copies

    def to_owners(grad, send, recv, sems):
        def copy_to(dst):
            return remote(send.at[dst // 2], recv.at[c], sems, dst, c, (dst, f))

        for i in range(8):
            send[i] = grad[:, i * T : i * T + T]
        each_peer(lambda dst: copy_to(dst).start())
        recv[c] = send[c // 2]
        return copy_to

    def from_owners(send, recv, sems):
        each_peer(
            lambda src: remote(
                send.at[src // 2], recv.at[src], sems, src, src, (src, f)
            ).wait_recv()
        )
        return jnp.sum(recv[...], axis=0)

    for i in range(3):
        cot_copies[i].wait_recv()
        two_copies[i].wait_recv()

    def plane_rows(ref):
        return ref[...].reshape(512, 1024)

    def block_of(i):
        return (near + (z - near) * (i // 2) + 2 * (i % 2)) % 4

    def pair_copy(theirs, pair, sems, i):
        at = lanes(block_of(i), T)
        return remote(theirs.at[at], pair.at[at], sems, i, i, sibling)

    def strip(i, carry):
        q = block_of(i)
        at = pl.ds(pl.multiple_of(q * 1024 + p * 256, 256), 256)
        shift = s.vec[q // 2, 8 + (q % 2) * 2 + p // 2, :, lanes(p % 2, 256)]
        hidden = dot(plane_rows(s.two_all), s.up_full[:, at]) + shift
        active, slope = gelu_pair(hidden)
        grad_active = dot_nt(plane_rows(s.cot_all), s.down_full[at, :])
        s.grad_hidden[:, lanes(q, 256)] = (grad_active * slope).astype(LOW)
        part = dot_tn(active.astype(LOW), plane_rows(s.cot_all))
        s.pool[lanes(q, T)] = jnp.where(first_core, part[:T], part[T:])
        s.down_theirs[lanes(q, T)] = jnp.where(first_core, part[T:], part[:T]).astype(LOW)
        pair_copy(s.down_theirs, s.down_pair, s.sem_down_pair, i).start()
        return carry

    def to_near(mine, theirs, pair, line, base, ready):
        size = line.shape[1]
        copies = []
        for j in range(2):
            ready(j)
            at = lanes((near + 2 * j) % 4, size)
            theirs[at] = (mine[at] + pair[at].astype(F32)).astype(LOW)
            copy = remote(
                theirs.at[at], line.at[j], s.sem_line, base + j, base + j, (near * 4 + p, f)
            )
            copy.start()
            copies.append(copy)
        return copies

    def to_far(mine, theirs, pair, line, base, ready, copies):
        size = line.shape[1]
        for j in (2, 3):
            ready(j)
        for copy in copies:
            copy.wait_recv()
        at = lanes(z, size)
        mine[at] += pair[at].astype(F32) + line[0].astype(F32)
        at = lanes(far, size)
        theirs[at] = (mine[at] + (pair[at].astype(F32) + line[1].astype(F32))).astype(LOW)
        copy = remote(theirs.at[at], line.at[2], s.sem_line, base + 2, base + 2, (far_slot, f))
        copy.start()
        return copies + [copy]

    up_theirs = s.down_full.at[pl.ds(0, 512)]

    def down_ready(i):
        pair_copy(s.down_theirs, s.down_pair, s.sem_down_pair, i).wait()

    def up_ready(i):
        pair_copy(up_theirs, s.up_pair, s.sem_up_pair, i).wait()

    lax.fori_loop(0, 4, strip, 0)
    down_line = to_near(s.pool, s.down_theirs, s.down_pair, s.down_line, 0, down_ready)

    def split_rows(part):
        parts = part.reshape(4, 2, 32, 1024)
        mine = jnp.where(first_core, parts[:, 0], parts[:, 1])
        theirs = jnp.where(first_core, parts[:, 1], parts[:, 0])
        return mine, theirs.astype(LOW)

    def up_rows(i, carry):
        q = block_of(i)
        left = s.two_all[:, :, lanes(q, 256)].reshape(512, 256)
        mine, theirs = split_rows(dot_tn(left, s.grad_hidden[...]))
        s.up_mine[lanes(q, T)] = mine.reshape(T, 1024)
        up_theirs[lanes(q, T)] = theirs.reshape(T, 1024)
        pair_copy(up_theirs, s.up_pair, s.sem_up_pair, i).start()
        return carry

    lax.fori_loop(0, 4, up_rows, 0)


    def qkv_done(dst):
        qkv_copy(dst).wait_send()

    each_peer(qkv_done)

    def back_arrived(src):
        remote(
            s.send_head.at[src], s.do_t.at[:, lanes(src, T)], s.sem_back, src, src, (src, f)
        ).wait_recv()

    each_peer(back_arrived)
    small_nothing = jnp.zeros((64, T), LOW)
    for i in range(n):
        at = slice(i * T, i * T + T)
        s.q_rows[at] = turned(
            jnp.concatenate([s.qkv_t[0:64, at], small_nothing], axis=0)
        ).astype(LOW)
        s.do_rows[at] = turned(
            jnp.concatenate([small_nothing, s.do_t[:, at]], axis=0)
        ).astype(LOW)
    s.delta[...] = column_sum(s.do_t[...].astype(F32) * s.head_out[...])
    s.dq[...] = jnp.zeros((64, 2048), F32)

    up_line = to_near(s.up_mine, up_theirs, s.up_pair, s.up_line, 3, up_ready)
    early_to = to_owners(s.early_grad, s.early_send, s.early_recv, s.sem_early)
    def grads_copy(dst):
        return remote(
            s.send_qkv.at[dst, pl.ds(64, 128)],
            s.dqkv.at[c, pl.ds(64, 128)],
            s.sem_grads,
            dst,
            c,
            (dst, f),
        )

    def dq_copy(dst):
        return remote(
            s.send_qkv.at[dst, pl.ds(0, 64)],
            s.dqkv.at[c, pl.ds(0, 64)],
            s.sem_dq,
            dst,
            c,
            (dst, f),
        )

    def col_copy(t, at, size, sems):
        return remote(
            s.send_qkv.at[t, pl.ds(at, size)],
            s.col.at[p, t // 4, pl.ds(at, size)],
            sems,
            t,
            p * 4 + t // 4,
            (home + t % 4, f),
        )

    def each_column(step):
        for k in range(1, 4):
            for i in range(4):
                step(i * 4 + (p + k) % 4)

    def backward(i, carry):
        block = (c // 2 + i) % 8
        keys = pl.ds(pl.multiple_of(block * 256, 256), 256)
        key_t = s.qkv_t[64:128, keys]
        both = s.kv[keys]
        dkv = jnp.zeros((256, 128), F32)
        for q in range(8):
            at = slice(q * 256, q * 256 + 256)
            query = jnp.concatenate([s.qkv_t[0:64, at], nothing], axis=0)
            grad = jnp.concatenate([nothing, s.do_t[:, at]], axis=0)
            score = dot(both, query)
            prob = jnp.where(seen(keys, at), jnp.exp(score - s.lse[:, at]), 0.0)
            grad_prob = dot(both, grad)
            grad_score = (prob * (grad_prob - s.delta[:, at])).astype(LOW)
            dkv = dkv + (
                dot(grad_score, s.q_rows[at]) + dot(prob.astype(LOW), s.do_rows[at])
            )
            s.dq[:, at] += dot(key_t, grad_score)
        for u in range(2):
            dst = block * 2 + u
            s.send_qkv[dst, 64:192] = dkv[u * T : u * T + T].T.astype(LOW)

            @pl.when(dst != c)
            def _():
                grads_copy(dst).start()

            @pl.when(dst % 4 != p)
            def _():
                col_copy(dst, 64, 128, s.sem_col).start()

        return carry

    lax.fori_loop(0, 6, backward, 0)
    down_line = to_far(s.pool, s.down_theirs, s.down_pair, s.down_line, 0, down_ready, down_line)
    lax.fori_loop(6, 8, backward, 0)
    for i in range(n):
        s.send_qkv[i, 0:64] = s.dq[:, i * T : i * T + T].astype(LOW)
    each_column(lambda t: col_copy(t, 0, 64, s.sem_col_dq).start())
    each_peer(lambda dst: dq_copy(dst).start())
    for i in range(4):
        s.col[p, i] = s.send_qkv[i * 4 + p]
    s.dqkv[c] = s.send_qkv[c]
    up_line = to_far(s.up_mine, up_theirs, s.up_pair, s.up_line, 3, up_ready, up_line)
    for i in range(3):
        att_copies[i].wait_recv()
        branch_copies[i].wait_recv()
    part = jnp.zeros((256, 1024), F32)
    for i in range(4):
        part = part + dot(s.att_all[i].reshape(256, T), s.branch_all[i])
    mine, theirs = split_rows(part)
    s.out_mine[...] = mine.reshape(T, 1024)
    s.out_theirs[...] = theirs.reshape(T, 1024)
    out_pair = remote(s.out_theirs, s.out_pair, s.sem_pair, 7, 7, sibling)
    out_pair.start()
    out_pair.wait()
    out_line = to_near(
        s.out_mine, s.out_theirs, s.out_pair, s.out_line, 6, lambda i: None
    )

    for slot in (near, (near + 2) % 4):
        one_arrived(slot)
    for at, size, sems in ((64, 128, s.sem_col), (0, 64, s.sem_col_dq)):
        for k in range(1, 4):
            for i in range(4):
                q = (p + k) % 4
                here = s.col.at[q, i, pl.ds(at, size)]
                remote(here, here, sems, 0, q * 4 + i, (home + q, f)).wait_recv()
    col_rows = s.up_full.at[pl.ds(0, 768), pl.ds(2048, 512)]
    in_theirs = s.up_full.at[pl.ds(0, 512), pl.ds(0, 768)]
    in_send = [s.up_full.at[pl.ds(i * T, T), pl.ds(1024, 768)] for i in range(3)]
    for q in range(4):
        for i in range(4):
            for part in range(3):
                col_rows[part * 256 + q * 64 : part * 256 + q * 64 + 64, i * T : i * T + T] = (
                    s.col[q, i, part * 64 : part * 64 + 64]
                )
    head_grad = jnp.concatenate([s.send_qkv[i] for i in range(n)], axis=1)
    bias_sums = dot_nt(jnp.ones((8, 2048), LOW), head_grad)
    s.vec_mine[16:24] = jnp.concatenate([bias_sums[:, 0:64] * scale, bias_sums[:, 128:192]], axis=1)

    for i in range(4):
        right = s.one_all[:, :, i * 256 : i * 256 + 256].reshape(512, 256)
        part = dot(col_rows[...], right)
        part = jnp.concatenate([part[0:256] * scale, part[256:768]], axis=0)
        parts = part.T.reshape(4, 2, 32, 768)
        s.in_mine[i] = jnp.where(first_core, parts[:, 0], parts[:, 1])
        theirs = jnp.where(first_core, parts[:, 1], parts[:, 0])
        in_theirs[i * T : i * T + T] = theirs.reshape(T, 768).astype(LOW)
    in_pair = remote(in_theirs, s.in_pair, s.sem_pair, 8, 8, sibling)
    in_pair.start()

    def grads_arrived(src):
        remote(
            s.send_qkv.at[src, pl.ds(64, 128)],
            s.dqkv.at[src, pl.ds(64, 128)],
            s.sem_grads,
            src,
            src,
            (src, f),
        ).wait_recv()

    def dq_arrived(src):
        remote(
            s.send_qkv.at[src, pl.ds(0, 64)],
            s.dqkv.at[src, pl.ds(0, 64)],
            s.sem_dq,
            src,
            src,
            (src, f),
        ).wait_recv()

    each_peer(grads_arrived)
    for h in range(n):
        s.gp_t[1024 + h * 64 : 1088 + h * 64] = s.dqkv[h, 64:128]
        s.gp_t[2048 + h * 64 : 2112 + h * 64] = s.dqkv[h, 128:192]
    for i in range(4):
        at = slice(i * 256, i * 256 + 256)
        s.acc_grad[:, at] = dot(s.in_full[at, 1024:3072], s.gp_t[1024:3072]).T
    each_peer(dq_arrived)
    for h in range(n):
        s.gp_t[h * 64 : h * 64 + 64] = s.dqkv[h, 0:64] * jnp.asarray(scale, LOW)
    for i in range(4):
        at = slice(i * 256, i * 256 + 256)
        s.acc_grad[:, at] += dot(s.in_full[at, 0:1024], s.gp_t[0:1024]).T
    unit_one, spread_one = standard(tok_ref[...].astype(F32))
    grad_one = s.acc_grad[...]
    s.late_grad[0:1] = column_sum(grad_one * unit_one)
    s.late_grad[1:2] = column_sum(grad_one)
    late_to = to_owners(s.late_grad, s.late_send, s.late_recv, s.sem_late)
    input_grad[...] = (
        s.grad_middle[...] + standard_back(grad_one, row(4), unit_one, spread_one)
    ).astype(LOW)

    in_pair.wait()

    def in_total(q, at):
        rows = pl.ds(pl.multiple_of(q * T + at * 32, 32), 32)
        return s.in_mine[q, at] + s.in_pair[rows].astype(F32)

    in_copies = []
    for i in range(3):
        for q in range(4):
            at = plane_places[i]
            in_send[i][q * 32 : q * 32 + 32] = in_total(q, at).astype(LOW)
        copy = remote(in_send[i], s.in_plane.at[i], s.sem_in_plane, i, i, planes[i])
        copy.start()
        in_copies.append(copy)
    for q in range(4):
        s.in_own[q] = in_total(q, p)

    out_line = to_far(s.out_mine, s.out_theirs, s.out_pair, s.out_line, 6, lambda i: None, out_line)
    up_line[2].wait_recv()
    up_sum = s.up_mine[lanes(z, T)] + s.up_line[2].astype(F32)
    s.up_piece[...] = up_sum.reshape(4, 32, 1024)
    up_copies = []
    for i in range(3):
        for q in range(4):
            copy = remote(
                s.up_piece.at[plane_places[i], :, pl.ds(q * 256, 256)],
                up_out.at[:, pl.ds(pl.multiple_of(q * 1024 + p * 256, 256), 256)],
                s.sem_up,
                i * 4 + q,
                i * 4 + q,
                planes[i],
            )
            copy.start()
            up_copies.append(copy)
    for q in range(4):
        up_out[:, pl.ds(pl.multiple_of(q * 1024 + p * 256, 256), 256)] = s.up_piece[
            p, :, q * 256 : q * 256 + 256
        ]
    down_line[2].wait_recv()
    down_out[...] = s.pool[lanes(z, T)] + s.down_line[2].astype(F32)
    out_line[2].wait_recv()
    out_out[...] = s.out_mine[lanes(z, 32)] + s.out_line[2].astype(F32)

    for copy in in_copies:
        copy.wait_recv()
    in_line = []
    for k in range(1, 4):
        at = (z + k) % 4
        total = s.in_own[at]
        for i in range(3):
            total = total + s.in_plane[i, pl.ds(pl.multiple_of(at * 32, 32), 32)].astype(F32)
        s.in_line[k - 1] = total.astype(LOW)
        copy = remote(
            s.in_line.at[k - 1], s.in_recv.at[z], s.sem_in, k - 1, z, (at * 4 + p, f)
        )
        copy.start()
        in_line.append(copy)

    def put_in(at, block):
        for part in range(3):
            columns = pl.ds(pl.multiple_of(part * 1024 + at * 256, 256), 256)
            in_out[:, columns] = block[:, part * 256 : part * 256 + 256]

    total = s.in_own[z]
    for i in range(3):
        total = total + s.in_plane[i, pl.ds(pl.multiple_of(z * 32, 32), 32)].astype(F32)
    put_in(z, total)

    s.vec_mine[0:8] = from_owners(s.early_send, s.early_recv, s.sem_early)
    s.vec_mine[8:16] = from_owners(s.late_send, s.late_recv, s.sem_late)
    vec_pair = remote(s.vec_mine, s.vec_pair, s.sem_pair, 9, 9, sibling)
    vec_pair.start()

    for k in range(1, 4):
        at = (z + k) % 4
        here = s.in_recv.at[at]
        remote(here, here, s.sem_in, 0, at, (at * 4 + p, f)).wait_recv()
        put_in(at, s.in_recv[at].astype(F32))
    vec_pair.wait()
    total = s.vec_mine[...] + s.vec_pair[...]
    place = (c * 2 + f) % 4
    picked, up_row = total[0:16, 0:32], total[4:5]
    for i in range(1, 4):
        picked = jnp.where(place == i, total[0:16, 32 * i : 32 * i + 32], picked)
        up_row = jnp.where(place == i, total[4 + i : 5 + i], up_row)
    vec_out[0:16, 0:32] = picked
    vec_out[16:24, 0:32] = jnp.where(first_core, total[16:24, 0:32], total[16:24, 32:64])
    vec_out[24:32, 0:32] = jnp.where(first_core, total[16:24, 64:96], total[16:24, 96:128])
    vec_out[32:40] = jnp.broadcast_to(up_row, (8, T))
    for copy in up_copies:
        copy.wait()
    for g in range(4):
        for part in range(3):
            in_copy_of(g, part).wait_send()
    sent += [copy for line in (down_line, up_line, out_line) for copy in line]
    sent += in_copies + in_line
    each_column(lambda t: col_copy(t, 64, 128, s.sem_col).wait_send())
    each_column(lambda t: col_copy(t, 0, 64, s.sem_col_dq).wait_send())
    for copy in sent:
        copy.wait_send()

    def all_sent(dst):
        back_copy(dst).wait_send()
        grads_copy(dst).wait_send()
        dq_copy(dst).wait_send()
        early_to(dst).wait_send()
        late_to(dst).wait_send()

    each_peer(all_sent)


def finish_kernel(*refs):
    vec = refs[6]
    for src, dst in zip(refs[:6], refs[7:13]):
        dst[...] = src[...]
    for i, dst in zip((16, 24, 0, 1, 8, 9, 2, 3), refs[13:21]):
        dst[...] = vec[i : i + 1, 0:32].reshape(32)
    refs[21][...] = vec[32:33].reshape(T)


def body_fused(
    tokens,
    in_weight,
    query_bias,
    value_bias,
    out_weight,
    out_bias,
    up_weight,
    up_bias,
    down_weight,
    down_bias,
    first_gain,
    first_shift,
    second_gain,
    second_shift,
    lengths,
    slot_places,
    cotangent,
):
    vectors = (
        query_bias,
        value_bias,
        out_bias,
        down_bias,
        first_gain,
        first_shift,
        second_gain,
        second_shift,
        up_bias,
    )
    hbm = pl.BlockSpec(memory_space=pl.ANY)
    vmem = pl.BlockSpec(memory_space=pltpu.VMEM)
    outs = pl.pallas_call(
        layer_kernel,
        out_shape=(
            jax.ShapeDtypeStruct((T, 1024), LOW),
            jax.ShapeDtypeStruct((T, 1024), LOW),
            jax.ShapeDtypeStruct((32, 3072), F32),
            jax.ShapeDtypeStruct((32, 1024), F32),
            jax.ShapeDtypeStruct((32, 4096), F32),
            jax.ShapeDtypeStruct((128, 1024), F32),
            jax.ShapeDtypeStruct((40, 128), F32),
        ),
        in_specs=[vmem] * 3 + [pl.BlockSpec(memory_space=pltpu.SMEM)] + [vmem] * 9 + [hbm] * 4,
        out_specs=(vmem,) * 7,
        scratch_shapes=[scratch()],
        compiler_params=pltpu.CompilerParams(
            collective_id=0, has_side_effects=True, vmem_limit_bytes=59 * 2**20
        ),
        cost_estimate=pl.CostEstimate(
            flops=16 * 10**9, bytes_accessed=40 * 2**20, transcendentals=10**7
        ),
    )(
        tokens[0],
        cotangent[0],
        slot_places,
        lengths,
        *vectors,
        in_weight,
        out_weight,
        up_weight,
        down_weight,
    )
    small = [jax.ShapeDtypeStruct((32,), F32)] * 8 + [jax.ShapeDtypeStruct((T,), F32)]
    outs = pl.pallas_call(
        finish_kernel,
        out_shape=[jax.ShapeDtypeStruct(one.shape, one.dtype) for one in outs[:6]] + small,
        in_specs=[vmem] * 7,
        out_specs=[vmem] * 15,
    )(*outs[:7])
    layer_out, input_grad, in_grad, out_grad, up_grad, down_grad = outs[:6]
    query_sum, value_sum, out_sum, down_sum = outs[6:10]
    gain_one, shift_one, gain_two, shift_two, up_sum = outs[10:]
    return (
        layer_out[None],
        input_grad[None],
        in_grad,
        query_sum,
        value_sum,
        out_grad,
        out_sum,
        up_grad,
        up_sum,
        down_grad,
        down_sum,
        gain_one,
        shift_one,
        gain_two,
        shift_two,
    )


def solution(mesh):
    placed = (
        P("fsdp", "ctx", None),
        P("fsdp", None),
        P("fsdp"),
        P("fsdp"),
        P("fsdp", None),
        P("fsdp"),
        P("fsdp", None),
        P("fsdp"),
        P("fsdp", None),
        P("fsdp"),
        P("fsdp"),
        P("fsdp"),
        P("fsdp"),
        P("fsdp"),
        P("fsdp", None),
        P("fsdp", None),
        P("fsdp", "ctx", None),
    )
    return jax.shard_map(
        body_fused if mesh.shape["ctx"] == H else body_general,
        mesh=mesh,
        in_specs=placed,
        out_specs=(
            P("fsdp", "ctx", None),
            P("fsdp", "ctx", None),
            P(("ctx", "fsdp"), None),
            P(("ctx", "fsdp")),
            P(("ctx", "fsdp")),
            P(("ctx", "fsdp"), None),
            P(("ctx", "fsdp")),
            P(("ctx", "fsdp"), None),
            P(("ctx", "fsdp")),
            P(("ctx", "fsdp"), None),
            P(("ctx", "fsdp")),
            P(("ctx", "fsdp")),
            P(("ctx", "fsdp")),
            P(("ctx", "fsdp")),
            P(("ctx", "fsdp")),
        ),
        check_vma=False,
    )
```

```python
import jax
import jax.numpy as jnp
from jax import lax
from typing import Any, NamedTuple
from jax.experimental import pallas as pl
from jax.experimental.pallas import tpu as pltpu
from jax.sharding import PartitionSpec as P

H = 16
HD = 64


epsilon = 1e-05
far_below = -1e30


def normalize(values, gain, shift):
    center = values - jnp.mean(values, axis=-1, keepdims=True)
    spread = jnp.mean(center * center, axis=-1, keepdims=True)
    return center * lax.rsqrt(spread + epsilon) * gain + shift


def gelu_exact(values):
    return jax.nn.gelu(values, approximate=False)


def block_size(total):
    for size in range(min(2048, total), 0, -1):
        if total % size == 0:
            return size
    return total


def segment_of(places, starts):
    return jnp.sum((starts[None, :] <= places[:, None]).astype(jnp.int32), axis=1) - 1


def visible(query_place, query_segment, key_place, key_segment):
    return (key_segment[None, :] == query_segment[:, None]) & (
        key_place[None, :] <= query_place[:, None]
    )


def scores_of(queries, key_rows, allowed):
    scores = jnp.einsum("qhd,khd->hqk", queries, key_rows, preferred_element_type=jnp.float32)
    return jnp.where(allowed[None], scores, far_below)


def inner_rows(left, right):
    return jnp.einsum("tf,tg->fg", left, right, preferred_element_type=jnp.float32)


def times_transposed(left, right):
    return jnp.einsum("tg,fg->tf", left, right, preferred_element_type=jnp.float32)


def key_terms(probs_low, grad_scores, query_rows, grad_rows, size, width):
    grad_keys = jnp.einsum(
        "hqk,qhd->khd", grad_scores, query_rows, preferred_element_type=jnp.float32
    )
    grad_values = jnp.einsum(
        "hqk,qhd->khd", probs_low, grad_rows, preferred_element_type=jnp.float32
    )
    return jnp.concatenate(
        [grad_keys.reshape(size, width), grad_values.reshape(size, width)], axis=1
    )


def body_general(
    tokens,
    in_weight,
    query_bias,
    value_bias,
    out_weight,
    out_bias,
    up_weight,
    up_bias,
    down_weight,
    down_bias,
    first_gain,
    first_shift,
    second_gain,
    second_shift,
    lengths,
    slot_places,
    cotangent,
):
    gathered_params = (
        lax.all_gather(in_weight, "fsdp", axis=0, tiled=True),
        lax.all_gather(query_bias, "fsdp", axis=0, tiled=True),
        lax.all_gather(value_bias, "fsdp", axis=0, tiled=True),
        lax.all_gather(out_weight, "fsdp", axis=0, tiled=True),
        lax.all_gather(out_bias, "fsdp", axis=0, tiled=True),
        lax.all_gather(up_weight, "fsdp", axis=0, tiled=True),
        lax.all_gather(up_bias, "fsdp", axis=0, tiled=True),
        lax.all_gather(down_weight, "fsdp", axis=0, tiled=True),
        lax.all_gather(down_bias, "fsdp", axis=0, tiled=True),
        lax.all_gather(first_gain, "fsdp", axis=0, tiled=True),
        lax.all_gather(first_shift, "fsdp", axis=0, tiled=True),
        lax.all_gather(second_gain, "fsdp", axis=0, tiled=True),
        lax.all_gather(second_shift, "fsdp", axis=0, tiled=True),
    )
    (
        in_full,
        query_shift,
        value_shift,
        out_full,
        out_shift,
        up_full,
        up_shift,
        down_full,
        down_shift,
        gain_first,
        shift_first,
        gain_second,
        shift_second,
    ) = gathered_params
    query_shift = query_shift.astype(jnp.float32)
    value_shift = value_shift.astype(jnp.float32)
    out_shift = out_shift.astype(jnp.float32)
    up_shift = up_shift.astype(jnp.float32)
    down_shift = down_shift.astype(jnp.float32)
    gain_first = gain_first.astype(jnp.float32)
    shift_first = shift_first.astype(jnp.float32)
    gain_second = gain_second.astype(jnp.float32)
    shift_second = shift_second.astype(jnp.float32)
    inputs = tokens[0].astype(jnp.float32)
    rows = inputs.shape[0]
    width = inputs.shape[1]
    scale = HD ** (-0.5)
    places = slot_places[0]
    seq_lengths = lengths[0]
    starts = jnp.cumsum(seq_lengths) - seq_lengths
    key_segments = segment_of(places, starts)
    first_slot = lax.axis_index("ctx") * rows
    query_places = lax.dynamic_slice_in_dim(places, first_slot, rows)
    query_segments = lax.dynamic_slice_in_dim(key_segments, first_slot, rows)
    total_keys = places.shape[0]
    key_step = block_size(total_keys)
    block_count = total_keys // key_step
    place_blocks = places.reshape(block_count, key_step)
    segment_blocks = key_segments.reshape(block_count, key_step)
    normed_one = normalize(inputs, gain_first, shift_first).astype(jnp.bfloat16)
    projected = jnp.dot(normed_one, in_full, preferred_element_type=jnp.float32)
    queries = (
        ((projected[:, :width] + query_shift) * scale).astype(jnp.bfloat16).reshape(rows, H, HD)
    )
    key_value = jnp.concatenate(
        [projected[:, width : 2 * width], projected[:, 2 * width :] + value_shift], axis=1
    ).astype(jnp.bfloat16)
    gathered = lax.all_gather(key_value, "ctx", axis=0, tiled=True)
    pair_blocks = gathered.reshape(block_count, key_step, 2 * width)

    def split_pair(pair, size):
        return (pair[:, :width].reshape(size, H, HD), pair[:, width:].reshape(size, H, HD))

    def max_step(carry, block):
        top, total = carry
        pair, key_place, key_segment = block
        key_rows, value_rows = split_pair(pair, key_step)
        allowed = visible(query_places, query_segments, key_place, key_segment)
        scores = scores_of(queries, key_rows, allowed)
        new_top = jnp.maximum(top, jnp.max(scores, axis=2))
        expand = jnp.where(allowed[None], jnp.exp(scores - new_top[:, :, None]), 0.0)
        total = total * jnp.exp(top - new_top) + jnp.sum(expand, axis=2)
        return ((new_top, total), None)

    start_top = jnp.full((H, rows), far_below, jnp.float32)
    (top, total), unused = lax.scan(
        max_step,
        (start_top, jnp.zeros((H, rows), jnp.float32)),
        (pair_blocks, place_blocks, segment_blocks),
    )
    log_total = top + jnp.log(total)

    def value_step(summed, block):
        pair, key_place, key_segment = block
        key_rows, value_rows = split_pair(pair, key_step)
        allowed = visible(query_places, query_segments, key_place, key_segment)
        scores = scores_of(queries, key_rows, allowed)
        weights = jnp.where(allowed[None], jnp.exp(scores - log_total[:, :, None]), 0.0).astype(
            jnp.bfloat16
        )
        summed = summed + jnp.einsum(
            "hqk,khd->qhd", weights, value_rows, preferred_element_type=jnp.float32
        )
        return (summed, None)

    heads_out, unused = lax.scan(
        value_step,
        jnp.zeros((rows, H, HD), jnp.float32),
        (pair_blocks, place_blocks, segment_blocks),
    )
    attended = heads_out.reshape(rows, width).astype(jnp.bfloat16)
    middle = inputs + jnp.dot(attended, out_full, preferred_element_type=jnp.float32) + out_shift
    normed_two = normalize(middle, gain_second, shift_second).astype(jnp.bfloat16)
    hidden = jnp.dot(normed_two, up_full, preferred_element_type=jnp.float32) + up_shift
    active_full, gelu_back = jax.vjp(gelu_exact, hidden)
    active = active_full.astype(jnp.bfloat16)
    result = middle + jnp.dot(active, down_full, preferred_element_type=jnp.float32) + down_shift
    layer_out = result.astype(jnp.bfloat16)[None]
    grad_low = cotangent[0]
    grad_result = grad_low.astype(jnp.float32)
    down_grad = inner_rows(active, grad_low)
    down_bias_grad = jnp.sum(grad_result, axis=0)
    grad_active = times_transposed(grad_low, down_full)
    grad_hidden = gelu_back(grad_active)[0].astype(jnp.bfloat16)
    up_grad = inner_rows(normed_two, grad_hidden)
    up_bias_grad = jnp.sum(grad_hidden.astype(jnp.float32), axis=0)
    grad_normed_two = times_transposed(grad_hidden, up_full)
    unused, second_back = jax.vjp(normalize, middle, gain_second, shift_second)
    grad_middle_norm, gain_two_grad, shift_two_grad = second_back(grad_normed_two)
    grad_middle = grad_result + grad_middle_norm
    grad_branch = grad_middle.astype(jnp.bfloat16)
    out_grad = inner_rows(attended, grad_branch)
    out_bias_grad = jnp.sum(grad_branch.astype(jnp.float32), axis=0)
    grad_attended = (
        times_transposed(grad_branch, out_full).astype(jnp.bfloat16).reshape(rows, H, HD)
    )
    deltas = jnp.sum(grad_attended.astype(jnp.float32) * heads_out, axis=2).T

    def block_back(key_rows, value_rows, allowed):
        scores = scores_of(queries, key_rows, allowed)
        probs = jnp.where(allowed[None], jnp.exp(scores - log_total[:, :, None]), 0.0)
        grad_probs = jnp.einsum(
            "qhd,khd->hqk", grad_attended, value_rows, preferred_element_type=jnp.float32
        )
        grad_scores = (probs * (grad_probs - deltas[:, :, None])).astype(jnp.bfloat16)
        return (probs.astype(jnp.bfloat16), grad_scores)

    def query_term(grad_scores, key_rows):
        return jnp.einsum("hqk,khd->qhd", grad_scores, key_rows, preferred_element_type=jnp.float32)

    def whole_step(grad_queries, block):
        pair, key_place, key_segment = block
        key_rows, value_rows = split_pair(pair, key_step)
        allowed = visible(query_places, query_segments, key_place, key_segment)
        probs_low, grad_scores = block_back(key_rows, value_rows, allowed)
        grad_queries = grad_queries + query_term(grad_scores, key_rows)
        return (
            grad_queries,
            key_terms(probs_low, grad_scores, queries, grad_attended, key_step, width),
        )

    grad_queries, terms = lax.scan(
        whole_step,
        jnp.zeros((rows, H, HD), jnp.float32),
        (pair_blocks, place_blocks, segment_blocks),
    )
    key_grads = lax.psum_scatter(
        terms.reshape(total_keys, 2 * width), "ctx", scatter_dimension=0, tiled=True
    )
    key_grads_low = key_grads.astype(jnp.bfloat16)
    grad_queries_low = grad_queries.reshape(rows, width).astype(jnp.bfloat16)
    grad_projected = jnp.concatenate([grad_queries_low, key_grads_low], axis=1)
    in_grad_raw = inner_rows(normed_one, grad_projected)
    in_grad = jnp.concatenate([in_grad_raw[:, :width] * scale, in_grad_raw[:, width:]], axis=1)
    query_bias_grad = jnp.sum(grad_queries_low.astype(jnp.float32), axis=0) * scale
    value_bias_grad = jnp.sum(key_grads_low[:, width:].astype(jnp.float32), axis=0)
    grad_normed_one = times_transposed(
        grad_queries_low, in_full[:, :width]
    ) * scale + times_transposed(key_grads_low, in_full[:, width:])
    unused, first_back = jax.vjp(normalize, inputs, gain_first, shift_first)
    grad_inputs_norm, gain_one_grad, shift_one_grad = first_back(grad_normed_one)
    input_grad = (grad_middle + grad_inputs_norm).astype(jnp.bfloat16)[None]
    grads = (
        in_grad,
        query_bias_grad,
        value_bias_grad,
        out_grad,
        out_bias_grad,
        up_grad,
        up_bias_grad,
        down_grad,
        down_bias_grad,
        gain_one_grad,
        shift_one_grad,
        gain_two_grad,
        shift_two_grad,
    )
    summed = (
        lax.psum_scatter(grads[0], ("ctx", "fsdp"), scatter_dimension=0, tiled=True),
        lax.psum_scatter(grads[1], ("ctx", "fsdp"), scatter_dimension=0, tiled=True),
        lax.psum_scatter(grads[2], ("ctx", "fsdp"), scatter_dimension=0, tiled=True),
        lax.psum_scatter(grads[3], ("ctx", "fsdp"), scatter_dimension=0, tiled=True),
        lax.psum_scatter(grads[4], ("ctx", "fsdp"), scatter_dimension=0, tiled=True),
        lax.psum_scatter(grads[5], ("ctx", "fsdp"), scatter_dimension=0, tiled=True),
        lax.psum_scatter(grads[6], ("ctx", "fsdp"), scatter_dimension=0, tiled=True),
        lax.psum_scatter(grads[7], ("ctx", "fsdp"), scatter_dimension=0, tiled=True),
        lax.psum_scatter(grads[8], ("ctx", "fsdp"), scatter_dimension=0, tiled=True),
        lax.psum_scatter(grads[9], ("ctx", "fsdp"), scatter_dimension=0, tiled=True),
        lax.psum_scatter(grads[10], ("ctx", "fsdp"), scatter_dimension=0, tiled=True),
        lax.psum_scatter(grads[11], ("ctx", "fsdp"), scatter_dimension=0, tiled=True),
        lax.psum_scatter(grads[12], ("ctx", "fsdp"), scatter_dimension=0, tiled=True),
    )
    (
        in_weight_grad,
        query_bias_grad_out,
        value_bias_grad_out,
        out_weight_grad,
        out_bias_grad_out,
        up_weight_grad,
        up_bias_grad_out,
        down_weight_grad,
        down_bias_grad_out,
        first_gain_grad,
        first_shift_grad,
        second_gain_grad,
        second_shift_grad,
    ) = summed
    return (
        layer_out,
        input_grad,
        in_weight_grad,
        query_bias_grad_out,
        value_bias_grad_out,
        out_weight_grad,
        out_bias_grad_out,
        up_weight_grad,
        up_bias_grad_out,
        down_weight_grad,
        down_bias_grad_out,
        first_gain_grad,
        first_shift_grad,
        second_gain_grad,
        second_shift_grad,
    )


MESH_ID = pl.DeviceIdType.MESH
LOW = jnp.bfloat16
F32 = jnp.float32
T = 128


def dot(left, right):
    return jnp.dot(left, right, preferred_element_type=jnp.float32)


def dot_nt(left, right):
    return lax.dot_general(left, right, (((1,), (1,)), ((), ())), preferred_element_type=F32)


def dot_tn(left, right):
    return lax.dot_general(left, right, (((0,), (0,)), ((), ())), preferred_element_type=F32)


def turned(block):
    return block.astype(F32).T


def standard(values):
    center = values - jnp.mean(values, axis=1, keepdims=True)
    spread = lax.rsqrt(jnp.mean(center * center, axis=1, keepdims=True) + epsilon)
    return center * spread, spread


def standard_back(grad, gain, unit, spread):
    e = grad * gain
    return spread * (
        e - jnp.mean(e, axis=1, keepdims=True) - unit * jnp.mean(e * unit, axis=1, keepdims=True)
    )


def gelu_pair(hidden):
    phi = 0.5 * (1.0 + lax.erf(hidden * 0.7071067811865476))
    density = jnp.exp(hidden * hidden * -0.5) * 0.3989422804014327
    return hidden * phi, phi + hidden * density


def lanes(index, size):
    return pl.ds(pl.multiple_of(index * size, size), size)


def column_sum(values):
    return jnp.sum(values, axis=0, keepdims=True)


class Sems(NamedTuple):
    send: Any
    recv: Any


class Scratch(NamedTuple):
    vec: Any
    bias: Any
    key: Any
    query: Any
    in_full: Any
    out_full: Any
    up_full: Any
    down_full: Any
    normed_one: Any
    send_qkv: Any
    qkv_t: Any
    kv: Any
    pool: Any
    lse: Any
    delta: Any
    head_out: Any
    send_head: Any
    att_t: Any
    att_all: Any
    att: Any
    middle: Any
    grad_middle: Any
    cot_all: Any
    two_all: Any
    branch_all: Any
    acc_out: Any
    acc_grad: Any
    grad_hidden: Any
    early_grad: Any
    late_grad: Any
    dq: Any
    do_t: Any
    q_rows: Any
    do_rows: Any
    down_theirs: Any
    down_pair: Any
    down_line: Any
    up_mine: Any
    up_pair: Any
    up_line: Any
    up_piece: Any
    out_mine: Any
    out_theirs: Any
    out_pair: Any
    out_line: Any
    dqkv: Any
    gp_t: Any
    one_all: Any
    col: Any
    in_mine: Any
    in_pair: Any
    in_plane: Any
    in_own: Any
    in_line: Any
    in_recv: Any
    early_send: Any
    early_recv: Any
    late_send: Any
    late_recv: Any
    vec_mine: Any
    vec_pair: Any
    sem_load: Any
    sem_pair: Any
    sem_qkv: Any
    sem_one: Any
    sem_down_pair: Any
    sem_up_pair: Any
    sem_col: Any
    sem_col_dq: Any
    sem_in_plane: Any
    sem_cot: Any
    sem_head: Any
    sem_att: Any
    sem_two: Any
    sem_back: Any
    sem_branch: Any
    sem_line: Any
    sem_grads: Any
    sem_up: Any
    sem_in: Any
    sem_early: Any
    sem_late: Any
    sem_dq: Any
    sem_in_w: Any


def scratch():
    def v(shape, kind):
        return pltpu.VMEM(shape, kind)

    def sems(count):
        return Sems(pltpu.SemaphoreType.DMA((count,)), pltpu.SemaphoreType.DMA((count,)))

    return Scratch(
        vec=v((2, 12, 1, 512), F32),
        bias=v((2, 1, 1024), F32),
        key=v((2048, 128), F32),
        query=v((8, 2048), F32),
        in_full=v((1024, 3072), LOW),
        out_full=v((1024, 1024), LOW),
        up_full=v((1024, 4096), LOW),
        down_full=v((4096, 1024), LOW),
        normed_one=v((128, 1024), LOW),
        send_qkv=v((16, 192, 128), LOW),
        qkv_t=v((192, 2048), LOW),
        kv=v((2048, 128), LOW),
        pool=v((512, 1024), F32),
        lse=v((1, 2048), F32),
        delta=v((1, 2048), F32),
        head_out=v((64, 2048), F32),
        send_head=v((16, 64, 128), LOW),
        att_t=v((16, 64, 128), LOW),
        att_all=v((4, 4, 64, 128), LOW),
        att=v((128, 1024), LOW),
        middle=v((128, 1024), F32),
        grad_middle=v((128, 1024), F32),
        cot_all=v((4, 128, 1024), LOW),
        two_all=v((4, 128, 1024), LOW),
        branch_all=v((4, 128, 1024), LOW),
        acc_out=v((128, 1024), F32),
        acc_grad=v((128, 1024), F32),
        grad_hidden=v((512, 1024), LOW),
        early_grad=v((8, 1024), F32),
        late_grad=v((8, 1024), F32),
        dq=v((64, 2048), F32),
        do_t=v((64, 2048), LOW),
        q_rows=v((2048, 128), LOW),
        do_rows=v((2048, 128), LOW),
        down_theirs=v((512, 1024), LOW),
        down_pair=v((512, 1024), LOW),
        down_line=v((3, 128, 1024), LOW),
        up_mine=v((512, 1024), F32),
        up_pair=v((512, 1024), LOW),
        up_line=v((3, 128, 1024), LOW),
        up_piece=v((4, 32, 1024), F32),
        out_mine=v((128, 1024), F32),
        out_theirs=v((128, 1024), LOW),
        out_pair=v((128, 1024), LOW),
        out_line=v((3, 32, 1024), LOW),
        dqkv=v((16, 192, 128), LOW),
        gp_t=v((3072, 128), LOW),
        one_all=v((4, 128, 1024), LOW),
        col=v((4, 4, 192, 128), LOW),
        in_mine=v((4, 4, 32, 768), F32),
        in_pair=v((512, 768), LOW),
        in_plane=v((3, 128, 768), LOW),
        in_own=v((4, 32, 768), F32),
        in_line=v((3, 32, 768), LOW),
        in_recv=v((4, 32, 768), LOW),
        early_send=v((8, 8, 128), F32),
        early_recv=v((16, 8, 128), F32),
        late_send=v((8, 8, 128), F32),
        late_recv=v((16, 8, 128), F32),
        vec_mine=v((24, 128), F32),
        vec_pair=v((24, 128), F32),
        sem_load=sems(6),
        sem_pair=sems(10),
        sem_qkv=sems(16),
        sem_one=sems(16),
        sem_down_pair=sems(4),
        sem_up_pair=sems(4),
        sem_col=sems(16),
        sem_col_dq=sems(16),
        sem_in_plane=sems(3),
        sem_cot=sems(3),
        sem_head=sems(16),
        sem_att=sems(3),
        sem_two=sems(3),
        sem_back=sems(16),
        sem_branch=sems(3),
        sem_line=sems(9),
        sem_grads=sems(16),
        sem_up=sems(12),
        sem_in=sems(16),
        sem_early=sems(16),
        sem_late=sems(16),
        sem_dq=sems(16),
        sem_in_w=sems(12),
    )


def layer_kernel(
    tok_ref,
    cot_ref,
    place_ref,
    length_ref,
    *rest,
):
    vec_refs, rest = rest[:9], rest[9:]
    in_hbm, out_hbm, up_hbm, down_hbm = rest[:4]
    layer_out, input_grad, in_out, out_out, up_out, down_out, vec_out, s = rest[4:]
    n = 16
    scale = HD ** (-0.5)
    c, f = lax.axis_index("ctx"), lax.axis_index("fsdp")
    z, p = c // 4, c % 4
    y, x = p // 2, p % 2
    home = c - p
    sibling = (c, 1 - f)
    plane_places = [2 * y + 1 - x, 2 * (1 - y) + x, 2 * (1 - y) + 1 - x]
    planes = [(home + place, f) for place in plane_places]
    near = z + 1 - 2 * (z % 2)
    far = (z + 2) % 4
    first_core = f == 0

    def remote(src, dst, sems, i, j, device):
        return pltpu.make_async_remote_copy(
            src_ref=src,
            dst_ref=dst,
            send_sem=sems.send.at[i],
            recv_sem=sems.recv.at[j],
            device_id=device,
            device_id_type=MESH_ID,
        )

    def each_peer(step):
        def one(k, carry):
            step((c + k) % n)
            return carry

        lax.fori_loop(1, n, one, 0)

    def to_planes(src_of, dst, sems):
        copies = []
        for i in range(3):
            copy = remote(src_of(i), dst.at[1 + i], sems, i, i, planes[i])
            copy.start()
            copies.append(copy)
        return copies

    barrier = pltpu.get_barrier_semaphore()

    def greet(peer):
        pl.semaphore_signal(barrier, inc=1, device_id=(peer, f), device_id_type=MESH_ID)

    each_peer(greet)
    pl.semaphore_signal(barrier, inc=1, device_id=sibling, device_id_type=MESH_ID)
    for i in range(8):
        s.vec[f, i] = vec_refs[i][...].astype(F32).reshape(1, 512)
    for i in range(4):
        s.vec[f, 8 + i] = vec_refs[8][i * 512 : i * 512 + 512].astype(F32).reshape(1, 512)
    in_load = pltpu.make_async_copy(in_hbm, s.in_full.at[pl.ds(f * 512, 512)], s.sem_load.send.at[0])
    in_load.start()
    unit_one, unused = standard(tok_ref[...].astype(F32))
    pl.semaphore_wait(barrier, n)
    vec_copy = remote(s.vec.at[f], s.vec.at[f], s.sem_pair, 4, 4, sibling)
    vec_copy.start()

    def in_copy_of(g, part):
        at = pl.ds(pl.multiple_of(part * 1024 + (z + g) % 4 * 256, 256), 256)
        return remote(
            in_hbm.at[:, at],
            s.in_full.at[pl.ds(f * 512, 512), at],
            s.sem_in_w,
            g * 3 + part,
            g * 3 + part,
            sibling,
        )

    for g in range(4):
        for part in range(3):
            in_copy_of(g, part).start()
    sent = [vec_copy]
    cot_copies = to_planes(lambda i: cot_ref, s.cot_all, s.sem_cot)
    sent += cot_copies

    weights = [
        (out_hbm, s.out_full, 512),
        (up_hbm, s.up_full, 512),
        (down_hbm, s.down_full, 2048),
    ]
    loads, pairs = [None], [None]
    for i, (src, dst, size) in enumerate(weights):
        load = pltpu.make_async_copy(src, dst.at[pl.ds(f * size, size)], s.sem_load.send.at[1 + i])
        loads.append(load)
        pair = remote(src, dst.at[pl.ds(f * size, size)], s.sem_pair, 1 + i, 1 + i, sibling)
        pairs.append(pair)
    sent += pairs[1:]

    def row(i):
        return jnp.concatenate([s.vec[0, i], s.vec[1, i]], axis=1)

    s.cot_all[0] = cot_ref[...]
    vec_copy.wait_recv()
    s.normed_one[...] = (unit_one * row(4) + row(5)).astype(LOW)
    s.bias[0] = row(0)
    s.bias[1] = row(1)
    in_load.wait()

    def qkv_copy(dst):
        return remote(
            s.send_qkv.at[dst], s.qkv_t.at[:, lanes(c, T)], s.sem_qkv, dst, c, (dst, f)
        )

    def project(g, carry):
        group = (z + g) % 4
        for part in range(3):
            in_copy_of(g, part).wait_recv()
            at = pl.ds(pl.multiple_of(part * 1024 + group * 256, 256), 256)
            acc = dot(s.normed_one[...], s.in_full[:, at])
            if part == 0:
                acc = (acc + s.bias[0, :, lanes(group, 256)]) * scale
            if part == 2:
                acc = acc + s.bias[1, :, lanes(group, 256)]
            for u in range(2):
                block = acc[:, u * T : (u + 1) * T].T.astype(LOW)
                for w in range(2):
                    s.send_qkv[group * 4 + 2 * u + w, part * 64 : part * 64 + 64, :] = block[
                        w * 64 : w * 64 + 64
                    ]
        for u in range(4):
            dst = group * 4 + u

            @pl.when(dst != c)
            def _():
                qkv_copy(dst).start()

            @pl.when(dst == c)
            def _():
                s.qkv_t[:, lanes(c, T)] = s.send_qkv[dst]

        return carry

    lax.fori_loop(0, 4, project, 0)
    for i in range(1, 4):
        loads[i].start()
        pairs[i].start()
    s.one_all[z] = s.normed_one[...]

    place = place_ref[...]
    first, begun = jnp.zeros((1, 2048), jnp.int32), 0
    for i in range(length_ref.shape[1]):
        first = jnp.where(place >= begun, begun, first)
        begun = begun + length_ref[0, i]
    s.query[0:1] = place.astype(F32)
    s.query[1:2] = first.astype(F32)
    for i in range(n):
        at = slice(i * T, i * T + T)
        s.key[at] = jnp.broadcast_to(s.query[0:1, at], (T, T)).T

    def qkv_arrived(src):
        remote(
            s.send_qkv.at[src], s.qkv_t.at[:, lanes(src, T)], s.sem_qkv, src, src, (src, f)
        ).wait_recv()

    each_peer(qkv_arrived)

    far_slot = far * 4 + p

    def one_copy(slot, i, device):
        return remote(s.one_all.at[slot], s.one_all.at[slot], s.sem_one, i, slot, device)

    one_far = one_copy(z, 0, (far_slot, f))
    one_far.start()
    sent.append(one_far)

    for i in range(n):
        at = slice(i * T, i * T + T)
        s.kv[at] = turned(s.qkv_t[64:192, at]).astype(LOW)
    nothing = jnp.zeros((64, 256), LOW)

    def seen(keys, at):
        place = jnp.concatenate([s.key[keys], s.key[keys]], axis=1)
        return (place >= s.query[1:2, at]) & (place <= s.query[0:1, at])

    def head_copy(dst):
        return remote(s.send_head.at[dst], s.att_t.at[p * 4 + z], s.sem_head, dst, c, (dst, f))

    def score_at(k):
        return s.pool.at[pl.ds(k // 4 * 256, 256), pl.ds(k % 4 * 256, 256)]

    def forward(i, carry):
        block = (c // 2 + i) % 8
        at = lanes(block, 256)
        query = jnp.concatenate([s.qkv_t[0:64, at], nothing], axis=0)
        top = jnp.full((8, 256), far_below, F32)
        for k in range(8):
            keys = slice(k * 256, k * 256 + 256)
            score = jnp.where(seen(keys, at), dot(s.kv[keys], query), far_below)
            score_at(k)[...] = score
            top = jnp.maximum(top, jnp.max(score.reshape(32, 8, 256), axis=0))
        top = jnp.max(top, axis=0, keepdims=True)
        total = jnp.zeros((8, 256), F32)
        acc = jnp.zeros((64, 256), F32)
        for k in range(8):
            keys = slice(k * 256, k * 256 + 256)
            grown = jnp.exp(score_at(k)[...] - top)
            total = total + jnp.sum(grown.reshape(32, 8, 256), axis=0)
            acc = acc + dot(s.qkv_t[128:192, keys], grown.astype(LOW))
        total = column_sum(total)
        s.lse[:, at] = top + jnp.log(total)
        result = acc / total
        s.head_out[:, at] = result
        for u in range(2):
            dst = block * 2 + u
            s.send_head[dst] = result[:, u * T : u * T + T].astype(LOW)

            @pl.when(dst != c)
            def _():
                head_copy(dst).start()

            @pl.when(dst == c)
            def _():
                s.att_t[p * 4 + z] = s.send_head[dst]

        return carry

    lax.fori_loop(0, 8, forward, 0)

    def head_arrived(src):
        slot = (src % 4) * 4 + src // 4
        remote(s.send_head.at[src], s.att_t.at[slot], s.sem_head, src, src, (src, f)).wait_recv()

    each_peer(head_arrived)

    def one_arrived(slot):
        one_copy(slot, 0, (far_slot, f)).wait_recv()

    one_arrived(far)
    near_device = (near * 4 + p, f)
    for i, slot in enumerate((z, far)):
        copy = one_copy(slot, 1 + i, near_device)
        copy.start()
        sent.append(copy)

    s.att_all[0] = s.att_t[pl.ds(p * 4, 4)]
    for i in range(8):
        slots = [(h % 4) * 4 + h // 4 for h in (2 * i, 2 * i + 1)]
        block = jnp.concatenate([s.att_t[slots[0]], s.att_t[slots[1]]], axis=0)
        s.att[:, i * T : i * T + T] = turned(block).astype(LOW)

    loads[1].wait()
    pairs[1].wait_recv()
    middle = tok_ref[...].astype(F32) + dot(s.att[...], s.out_full[...]) + row(2)
    s.middle[...] = middle
    unit_two, unused = standard(middle)
    s.two_all[0] = (unit_two * row(6) + row(7)).astype(LOW)
    two_copies = to_planes(lambda i: s.two_all.at[0], s.two_all, s.sem_two)
    sent += two_copies
    for i in (2, 3):
        loads[i].wait()
        pairs[i].wait_recv()
    s.acc_out[...] = jnp.zeros((T, 1024), F32)
    s.acc_grad[...] = jnp.zeros((T, 1024), F32)
    s.late_grad[...] = jnp.zeros((8, 1024), F32)

    def feed(j, carry):
        at = lanes(j, 512)
        hidden = dot(s.two_all[0], s.up_full[:, at]) + s.vec[j // 4, 8 + j % 4]
        active, slope = gelu_pair(hidden)
        grad_active = dot_nt(cot_ref[...], s.down_full[at, :])
        grad_hidden = (grad_active * slope).astype(LOW)
        s.acc_out[...] += dot(active.astype(LOW), s.down_full[at, :])
        s.acc_grad[...] += dot_nt(grad_hidden, s.up_full[:, at])
        summed = column_sum(grad_hidden.astype(F32))
        for q in range(4):
            s.early_grad[4 + q : 5 + q, lanes(j, T)] = summed[:, q * T : q * T + T]
        return carry

    lax.fori_loop(0, 8, feed, 0)
    layer_out[...] = (s.middle[...] + s.acc_out[...] + row(3)).astype(LOW)
    grad_result = cot_ref[...].astype(F32)
    s.early_grad[1:2] = column_sum(grad_result)
    unit_two, spread_two = standard(s.middle[...])
    grad_two = s.acc_grad[...]
    s.early_grad[2:3] = column_sum(grad_two * unit_two)
    s.early_grad[3:4] = column_sum(grad_two)
    grad_middle = grad_result + standard_back(grad_two, row(6), unit_two, spread_two)
    s.grad_middle[...] = grad_middle
    branch = grad_middle.astype(LOW)
    s.branch_all[0] = branch
    s.early_grad[0:1] = column_sum(branch.astype(F32))

    def head_done(dst):
        head_copy(dst).wait_send()

    each_peer(head_done)
    for i in range(4):
        at = slice(i * 256, i * 256 + 256)
        part = dot_nt(s.out_full[at, :], branch).astype(LOW)
        s.send_head[4 * i : 4 * i + 4] = part.reshape(4, 64, T)

    def back_copy(dst):
        return remote(s.send_head.at[dst], s.do_t.at[:, lanes(c, T)], s.sem_back, dst, c, (dst, f))

    each_peer(lambda dst: back_copy(dst).start())
    s.do_t[:, lanes(c, T)] = s.send_head[c]
    branch_copies = to_planes(lambda i: s.branch_all.at[0], s.branch_all, s.sem_branch)
    sent += branch_copies
    att_copies = to_planes(
        lambda i: s.att_t.at[pl.ds(plane_places[i] * 4, 4)], s.att_all, s.sem_att
    )
    sent += att_copies

    def to_owners(grad, send, recv, sems):
        def copy_to(dst):
            return remote(send.at[dst // 2], recv.at[c], sems, dst, c, (dst, f))

        for i in range(8):
            send[i] = grad[:, i * T : i * T + T]
        each_peer(lambda dst: copy_to(dst).start())
        recv[c] = send[c // 2]
        return copy_to

    def from_owners(send, recv, sems):
        each_peer(
            lambda src: remote(
                send.at[src // 2], recv.at[src], sems, src, src, (src, f)
            ).wait_recv()
        )
        return jnp.sum(recv[...], axis=0)

    for i in range(3):
        cot_copies[i].wait_recv()
        two_copies[i].wait_recv()

    def plane_rows(ref):
        return ref[...].reshape(512, 1024)

    def block_of(i):
        return (near + (z - near) * (i // 2) + 2 * (i % 2)) % 4

    def pair_copy(theirs, pair, sems, i):
        at = lanes(block_of(i), T)
        return remote(theirs.at[at], pair.at[at], sems, i, i, sibling)

    def strip(i, carry):
        q = block_of(i)
        at = pl.ds(pl.multiple_of(q * 1024 + p * 256, 256), 256)
        shift = s.vec[q // 2, 8 + (q % 2) * 2 + p // 2, :, lanes(p % 2, 256)]
        hidden = dot(plane_rows(s.two_all), s.up_full[:, at]) + shift
        active, slope = gelu_pair(hidden)
        grad_active = dot_nt(plane_rows(s.cot_all), s.down_full[at, :])
        s.grad_hidden[:, lanes(q, 256)] = (grad_active * slope).astype(LOW)
        part = dot_tn(active.astype(LOW), plane_rows(s.cot_all))
        s.pool[lanes(q, T)] = jnp.where(first_core, part[:T], part[T:])
        s.down_theirs[lanes(q, T)] = jnp.where(first_core, part[T:], part[:T]).astype(LOW)
        pair_copy(s.down_theirs, s.down_pair, s.sem_down_pair, i).start()
        return carry

    def to_near(mine, theirs, pair, line, base, ready):
        size = line.shape[1]
        copies = []
        for j in range(2):
            ready(j)
            at = lanes((near + 2 * j) % 4, size)
            theirs[at] = (mine[at] + pair[at].astype(F32)).astype(LOW)
            copy = remote(
                theirs.at[at], line.at[j], s.sem_line, base + j, base + j, (near * 4 + p, f)
            )
            copy.start()
            copies.append(copy)
        return copies

    def to_far(mine, theirs, pair, line, base, ready, copies):
        size = line.shape[1]
        for j in (2, 3):
            ready(j)
        for copy in copies:
            copy.wait_recv()
        at = lanes(z, size)
        mine[at] += pair[at].astype(F32) + line[0].astype(F32)
        at = lanes(far, size)
        theirs[at] = (mine[at] + (pair[at].astype(F32) + line[1].astype(F32))).astype(LOW)
        copy = remote(theirs.at[at], line.at[2], s.sem_line, base + 2, base + 2, (far_slot, f))
        copy.start()
        return copies + [copy]

    up_theirs = s.down_full.at[pl.ds(0, 512)]

    def down_ready(i):
        pair_copy(s.down_theirs, s.down_pair, s.sem_down_pair, i).wait()

    def up_ready(i):
        pair_copy(up_theirs, s.up_pair, s.sem_up_pair, i).wait()

    lax.fori_loop(0, 4, strip, 0)
    down_line = to_near(s.pool, s.down_theirs, s.down_pair, s.down_line, 0, down_ready)

    def split_rows(part):
        parts = part.reshape(4, 2, 32, 1024)
        mine = jnp.where(first_core, parts[:, 0], parts[:, 1])
        theirs = jnp.where(first_core, parts[:, 1], parts[:, 0])
        return mine, theirs.astype(LOW)

    def up_rows(i, carry):
        q = block_of(i)
        left = s.two_all[:, :, lanes(q, 256)].reshape(512, 256)
        mine, theirs = split_rows(dot_tn(left, s.grad_hidden[...]))
        s.up_mine[lanes(q, T)] = mine.reshape(T, 1024)
        up_theirs[lanes(q, T)] = theirs.reshape(T, 1024)
        pair_copy(up_theirs, s.up_pair, s.sem_up_pair, i).start()
        return carry

    lax.fori_loop(0, 4, up_rows, 0)


    def qkv_done(dst):
        qkv_copy(dst).wait_send()

    each_peer(qkv_done)

    def back_arrived(src):
        remote(
            s.send_head.at[src], s.do_t.at[:, lanes(src, T)], s.sem_back, src, src, (src, f)
        ).wait_recv()

    each_peer(back_arrived)
    small_nothing = jnp.zeros((64, T), LOW)
    for i in range(n):
        at = slice(i * T, i * T + T)
        s.q_rows[at] = turned(
            jnp.concatenate([s.qkv_t[0:64, at], small_nothing], axis=0)
        ).astype(LOW)
        s.do_rows[at] = turned(
            jnp.concatenate([small_nothing, s.do_t[:, at]], axis=0)
        ).astype(LOW)
    s.delta[...] = column_sum(s.do_t[...].astype(F32) * s.head_out[...])
    s.dq[...] = jnp.zeros((64, 2048), F32)

    up_line = to_near(s.up_mine, up_theirs, s.up_pair, s.up_line, 3, up_ready)
    early_to = to_owners(s.early_grad, s.early_send, s.early_recv, s.sem_early)
    def grads_copy(dst):
        return remote(
            s.send_qkv.at[dst, pl.ds(64, 128)],
            s.dqkv.at[c, pl.ds(64, 128)],
            s.sem_grads,
            dst,
            c,
            (dst, f),
        )

    def dq_copy(dst):
        return remote(
            s.send_qkv.at[dst, pl.ds(0, 64)],
            s.dqkv.at[c, pl.ds(0, 64)],
            s.sem_dq,
            dst,
            c,
            (dst, f),
        )

    def col_copy(t, at, size, sems):
        return remote(
            s.send_qkv.at[t, pl.ds(at, size)],
            s.col.at[p, t // 4, pl.ds(at, size)],
            sems,
            t,
            p * 4 + t // 4,
            (home + t % 4, f),
        )

    def each_column(step):
        for k in range(1, 4):
            for i in range(4):
                step(i * 4 + (p + k) % 4)

    def backward(i, carry):
        block = (c // 2 + i) % 8
        keys = pl.ds(pl.multiple_of(block * 256, 256), 256)
        key_t = s.qkv_t[64:128, keys]
        both = s.kv[keys]
        dkv = jnp.zeros((256, 128), F32)
        for q in range(8):
            at = slice(q * 256, q * 256 + 256)
            query = jnp.concatenate([s.qkv_t[0:64, at], nothing], axis=0)
            grad = jnp.concatenate([nothing, s.do_t[:, at]], axis=0)
            score = dot(both, query)
            prob = jnp.where(seen(keys, at), jnp.exp(score - s.lse[:, at]), 0.0)
            grad_prob = dot(both, grad)
            grad_score = (prob * (grad_prob - s.delta[:, at])).astype(LOW)
            dkv = dkv + (
                dot(grad_score, s.q_rows[at]) + dot(prob.astype(LOW), s.do_rows[at])
            )
            s.dq[:, at] += dot(key_t, grad_score)
        for u in range(2):
            dst = block * 2 + u
            s.send_qkv[dst, 64:192] = dkv[u * T : u * T + T].T.astype(LOW)

            @pl.when(dst != c)
            def _():
                grads_copy(dst).start()

            @pl.when(dst % 4 != p)
            def _():
                col_copy(dst, 64, 128, s.sem_col).start()

        return carry

    lax.fori_loop(0, 6, backward, 0)
    down_line = to_far(s.pool, s.down_theirs, s.down_pair, s.down_line, 0, down_ready, down_line)
    lax.fori_loop(6, 8, backward, 0)
    for i in range(n):
        s.send_qkv[i, 0:64] = s.dq[:, i * T : i * T + T].astype(LOW)
    each_column(lambda t: col_copy(t, 0, 64, s.sem_col_dq).start())
    each_peer(lambda dst: dq_copy(dst).start())
    for i in range(4):
        s.col[p, i] = s.send_qkv[i * 4 + p]
    s.dqkv[c] = s.send_qkv[c]

    for slot in (near, (near + 2) % 4):
        one_arrived(slot)
    for at, size, sems in ((64, 128, s.sem_col), (0, 64, s.sem_col_dq)):
        for k in range(1, 4):
            for i in range(4):
                q = (p + k) % 4
                here = s.col.at[q, i, pl.ds(at, size)]
                remote(here, here, sems, 0, q * 4 + i, (home + q, f)).wait_recv()
    col_rows = s.up_full.at[pl.ds(0, 768), pl.ds(2048, 512)]
    in_theirs = s.up_full.at[pl.ds(0, 512), pl.ds(0, 768)]
    in_send = [s.up_full.at[pl.ds(i * T, T), pl.ds(1024, 768)] for i in range(3)]
    for q in range(4):
        for i in range(4):
            for part in range(3):
                col_rows[part * 256 + q * 64 : part * 256 + q * 64 + 64, i * T : i * T + T] = (
                    s.col[q, i, part * 64 : part * 64 + 64]
                )
    head_grad = jnp.concatenate([s.send_qkv[i] for i in range(n)], axis=1)
    bias_sums = dot_nt(jnp.ones((8, 2048), LOW), head_grad)
    s.vec_mine[16:24] = jnp.concatenate([bias_sums[:, 0:64] * scale, bias_sums[:, 128:192]], axis=1)

    for i in range(4):
        right = s.one_all[:, :, i * 256 : i * 256 + 256].reshape(512, 256)
        part = dot(col_rows[...], right)
        part = jnp.concatenate([part[0:256] * scale, part[256:768]], axis=0)
        parts = part.T.reshape(4, 2, 32, 768)
        s.in_mine[i] = jnp.where(first_core, parts[:, 0], parts[:, 1])
        theirs = jnp.where(first_core, parts[:, 1], parts[:, 0])
        in_theirs[i * T : i * T + T] = theirs.reshape(T, 768).astype(LOW)
    in_pair = remote(in_theirs, s.in_pair, s.sem_pair, 8, 8, sibling)
    in_pair.start()
    up_line = to_far(s.up_mine, up_theirs, s.up_pair, s.up_line, 3, up_ready, up_line)
    for i in range(3):
        att_copies[i].wait_recv()
        branch_copies[i].wait_recv()
    part = jnp.zeros((256, 1024), F32)
    for i in range(4):
        part = part + dot(s.att_all[i].reshape(256, T), s.branch_all[i])
    mine, theirs = split_rows(part)
    s.out_mine[...] = mine.reshape(T, 1024)
    s.out_theirs[...] = theirs.reshape(T, 1024)
    out_pair = remote(s.out_theirs, s.out_pair, s.sem_pair, 7, 7, sibling)
    out_pair.start()
    out_pair.wait()
    out_line = to_near(
        s.out_mine, s.out_theirs, s.out_pair, s.out_line, 6, lambda i: None
    )


    def grads_arrived(src):
        remote(
            s.send_qkv.at[src, pl.ds(64, 128)],
            s.dqkv.at[src, pl.ds(64, 128)],
            s.sem_grads,
            src,
            src,
            (src, f),
        ).wait_recv()

    def dq_arrived(src):
        remote(
            s.send_qkv.at[src, pl.ds(0, 64)],
            s.dqkv.at[src, pl.ds(0, 64)],
            s.sem_dq,
            src,
            src,
            (src, f),
        ).wait_recv()

    each_peer(grads_arrived)
    for h in range(n):
        s.gp_t[1024 + h * 64 : 1088 + h * 64] = s.dqkv[h, 64:128]
        s.gp_t[2048 + h * 64 : 2112 + h * 64] = s.dqkv[h, 128:192]
    for i in range(4):
        at = slice(i * 256, i * 256 + 256)
        s.acc_grad[:, at] = dot(s.in_full[at, 1024:3072], s.gp_t[1024:3072]).T
    each_peer(dq_arrived)
    for h in range(n):
        s.gp_t[h * 64 : h * 64 + 64] = s.dqkv[h, 0:64] * jnp.asarray(scale, LOW)
    for i in range(4):
        at = slice(i * 256, i * 256 + 256)
        s.acc_grad[:, at] += dot(s.in_full[at, 0:1024], s.gp_t[0:1024]).T
    unit_one, spread_one = standard(tok_ref[...].astype(F32))
    grad_one = s.acc_grad[...]
    s.late_grad[0:1] = column_sum(grad_one * unit_one)
    s.late_grad[1:2] = column_sum(grad_one)
    late_to = to_owners(s.late_grad, s.late_send, s.late_recv, s.sem_late)
    input_grad[...] = (
        s.grad_middle[...] + standard_back(grad_one, row(4), unit_one, spread_one)
    ).astype(LOW)

    in_pair.wait()

    def in_total(q, at):
        rows = pl.ds(pl.multiple_of(q * T + at * 32, 32), 32)
        return s.in_mine[q, at] + s.in_pair[rows].astype(F32)

    in_copies = []
    for i in range(3):
        for q in range(4):
            at = plane_places[i]
            in_send[i][q * 32 : q * 32 + 32] = in_total(q, at).astype(LOW)
        copy = remote(in_send[i], s.in_plane.at[i], s.sem_in_plane, i, i, planes[i])
        copy.start()
        in_copies.append(copy)
    for q in range(4):
        s.in_own[q] = in_total(q, p)

    out_line = to_far(s.out_mine, s.out_theirs, s.out_pair, s.out_line, 6, lambda i: None, out_line)
    up_line[2].wait_recv()
    up_sum = s.up_mine[lanes(z, T)] + s.up_line[2].astype(F32)
    s.up_piece[...] = up_sum.reshape(4, 32, 1024)
    up_copies = []
    for i in range(3):
        for q in range(4):
            copy = remote(
                s.up_piece.at[plane_places[i], :, pl.ds(q * 256, 256)],
                up_out.at[:, pl.ds(pl.multiple_of(q * 1024 + p * 256, 256), 256)],
                s.sem_up,
                i * 4 + q,
                i * 4 + q,
                planes[i],
            )
            copy.start()
            up_copies.append(copy)
    for q in range(4):
        up_out[:, pl.ds(pl.multiple_of(q * 1024 + p * 256, 256), 256)] = s.up_piece[
            p, :, q * 256 : q * 256 + 256
        ]
    down_line[2].wait_recv()
    down_out[...] = s.pool[lanes(z, T)] + s.down_line[2].astype(F32)
    out_line[2].wait_recv()
    out_out[...] = s.out_mine[lanes(z, 32)] + s.out_line[2].astype(F32)

    for copy in in_copies:
        copy.wait_recv()
    in_line = []
    for k in range(1, 4):
        at = (z + k) % 4
        total = s.in_own[at]
        for i in range(3):
            total = total + s.in_plane[i, pl.ds(pl.multiple_of(at * 32, 32), 32)].astype(F32)
        s.in_line[k - 1] = total.astype(LOW)
        copy = remote(
            s.in_line.at[k - 1], s.in_recv.at[z], s.sem_in, k - 1, z, (at * 4 + p, f)
        )
        copy.start()
        in_line.append(copy)

    def put_in(at, block):
        for part in range(3):
            columns = pl.ds(pl.multiple_of(part * 1024 + at * 256, 256), 256)
            in_out[:, columns] = block[:, part * 256 : part * 256 + 256]

    total = s.in_own[z]
    for i in range(3):
        total = total + s.in_plane[i, pl.ds(pl.multiple_of(z * 32, 32), 32)].astype(F32)
    put_in(z, total)

    s.vec_mine[0:8] = from_owners(s.early_send, s.early_recv, s.sem_early)
    s.vec_mine[8:16] = from_owners(s.late_send, s.late_recv, s.sem_late)
    vec_pair = remote(s.vec_mine, s.vec_pair, s.sem_pair, 9, 9, sibling)
    vec_pair.start()

    for k in range(1, 4):
        at = (z + k) % 4
        here = s.in_recv.at[at]
        remote(here, here, s.sem_in, 0, at, (at * 4 + p, f)).wait_recv()
        put_in(at, s.in_recv[at].astype(F32))
    vec_pair.wait()
    total = s.vec_mine[...] + s.vec_pair[...]
    place = (c * 2 + f) % 4
    picked, up_row = total[0:16, 0:32], total[4:5]
    for i in range(1, 4):
        picked = jnp.where(place == i, total[0:16, 32 * i : 32 * i + 32], picked)
        up_row = jnp.where(place == i, total[4 + i : 5 + i], up_row)
    vec_out[0:16, 0:32] = picked
    vec_out[16:24, 0:32] = jnp.where(first_core, total[16:24, 0:32], total[16:24, 32:64])
    vec_out[24:32, 0:32] = jnp.where(first_core, total[16:24, 64:96], total[16:24, 96:128])
    vec_out[32:40] = jnp.broadcast_to(up_row, (8, T))
    for copy in up_copies:
        copy.wait()
    for g in range(4):
        for part in range(3):
            in_copy_of(g, part).wait_send()
    sent += [copy for line in (down_line, up_line, out_line) for copy in line]
    sent += in_copies + in_line
    each_column(lambda t: col_copy(t, 64, 128, s.sem_col).wait_send())
    each_column(lambda t: col_copy(t, 0, 64, s.sem_col_dq).wait_send())
    for copy in sent:
        copy.wait_send()

    def all_sent(dst):
        back_copy(dst).wait_send()
        grads_copy(dst).wait_send()
        dq_copy(dst).wait_send()
        early_to(dst).wait_send()
        late_to(dst).wait_send()

    each_peer(all_sent)


def finish_kernel(*refs):
    vec = refs[6]
    for src, dst in zip(refs[:6], refs[7:13]):
        dst[...] = src[...]
    for i, dst in zip((16, 24, 0, 1, 8, 9, 2, 3), refs[13:21]):
        dst[...] = vec[i : i + 1, 0:32].reshape(32)
    refs[21][...] = vec[32:33].reshape(T)


def body_fused(
    tokens,
    in_weight,
    query_bias,
    value_bias,
    out_weight,
    out_bias,
    up_weight,
    up_bias,
    down_weight,
    down_bias,
    first_gain,
    first_shift,
    second_gain,
    second_shift,
    lengths,
    slot_places,
    cotangent,
):
    vectors = (
        query_bias,
        value_bias,
        out_bias,
        down_bias,
        first_gain,
        first_shift,
        second_gain,
        second_shift,
        up_bias,
    )
    hbm = pl.BlockSpec(memory_space=pl.ANY)
    vmem = pl.BlockSpec(memory_space=pltpu.VMEM)
    outs = pl.pallas_call(
        layer_kernel,
        out_shape=(
            jax.ShapeDtypeStruct((T, 1024), LOW),
            jax.ShapeDtypeStruct((T, 1024), LOW),
            jax.ShapeDtypeStruct((32, 3072), F32),
            jax.ShapeDtypeStruct((32, 1024), F32),
            jax.ShapeDtypeStruct((32, 4096), F32),
            jax.ShapeDtypeStruct((128, 1024), F32),
            jax.ShapeDtypeStruct((40, 128), F32),
        ),
        in_specs=[vmem] * 3 + [pl.BlockSpec(memory_space=pltpu.SMEM)] + [vmem] * 9 + [hbm] * 4,
        out_specs=(vmem,) * 7,
        scratch_shapes=[scratch()],
        compiler_params=pltpu.CompilerParams(
            collective_id=0, has_side_effects=True, vmem_limit_bytes=59 * 2**20
        ),
        cost_estimate=pl.CostEstimate(
            flops=16 * 10**9, bytes_accessed=40 * 2**20, transcendentals=10**7
        ),
    )(
        tokens[0],
        cotangent[0],
        slot_places,
        lengths,
        *vectors,
        in_weight,
        out_weight,
        up_weight,
        down_weight,
    )
    small = [jax.ShapeDtypeStruct((32,), F32)] * 8 + [jax.ShapeDtypeStruct((T,), F32)]
    outs = pl.pallas_call(
        finish_kernel,
        out_shape=[jax.ShapeDtypeStruct(one.shape, one.dtype) for one in outs[:6]] + small,
        in_specs=[vmem] * 7,
        out_specs=[vmem] * 15,
    )(*outs[:7])
    layer_out, input_grad, in_grad, out_grad, up_grad, down_grad = outs[:6]
    query_sum, value_sum, out_sum, down_sum = outs[6:10]
    gain_one, shift_one, gain_two, shift_two, up_sum = outs[10:]
    return (
        layer_out[None],
        input_grad[None],
        in_grad,
        query_sum,
        value_sum,
        out_grad,
        out_sum,
        up_grad,
        up_sum,
        down_grad,
        down_sum,
        gain_one,
        shift_one,
        gain_two,
        shift_two,
    )


def solution(mesh):
    placed = (
        P("fsdp", "ctx", None),
        P("fsdp", None),
        P("fsdp"),
        P("fsdp"),
        P("fsdp", None),
        P("fsdp"),
        P("fsdp", None),
        P("fsdp"),
        P("fsdp", None),
        P("fsdp"),
        P("fsdp"),
        P("fsdp"),
        P("fsdp"),
        P("fsdp"),
        P("fsdp", None),
        P("fsdp", None),
        P("fsdp", "ctx", None),
    )
    return jax.shard_map(
        body_fused if mesh.shape["ctx"] == H else body_general,
        mesh=mesh,
        in_specs=placed,
        out_specs=(
            P("fsdp", "ctx", None),
            P("fsdp", "ctx", None),
            P(("ctx", "fsdp"), None),
            P(("ctx", "fsdp")),
            P(("ctx", "fsdp")),
            P(("ctx", "fsdp"), None),
            P(("ctx", "fsdp")),
            P(("ctx", "fsdp"), None),
            P(("ctx", "fsdp")),
            P(("ctx", "fsdp"), None),
            P(("ctx", "fsdp")),
            P(("ctx", "fsdp")),
            P(("ctx", "fsdp")),
            P(("ctx", "fsdp")),
            P(("ctx", "fsdp")),
        ),
        check_vma=False,
    )
```
